32 devices in a mesh: shard: 2 (over x), ctx: 4 (over z), tp: 4 (over y, core).
Axes of the slice: x: 2, y: 2, z: 4, core: 2. Of those that a mesh axis runs over, the one named last changes fastest.
Arguments:
- inputs: bfloat16 [2560, 2048], P(('shard', 'ctx')), may hold values from -6 to 6
- parents: int32 [40], replicated, may hold values from -1 to 39, as said below
- attention_routes: int32 [2560, 2], P(('shard', 'ctx')), may hold values from 0 to 3, all different within a row; in each aligned block of 320 rows (0 to 319, 320 to 639, ...) at most 176 rows name the same one
- expert_routes: int32 [2560, 2], P(('shard', 'ctx')), may hold values from 0 to 3, all different within a row; in each aligned block of 320 rows (0 to 319, 320 to 639, ...) at most 176 rows name the same one
- attention_gain: bfloat16 [2048], P(('shard', 'ctx')), may hold values from 0.5 to 1.5
- attention_router: bfloat16 [2048, 4], P(('shard', 'ctx')), may hold values from -0.09375 to 0.09375
- query_weight: bfloat16 [4, 2048, 2048], P(None, ('shard', 'ctx'), 'tp')
- key_weight: bfloat16 [2048, 2048], P(('shard', 'ctx'), 'tp'), may hold values from -0.125 to 0.125
- value_weight: bfloat16 [2048, 2048], P(('shard', 'ctx'), 'tp'), may hold values from -0.125 to 0.125
- output_weight: bfloat16 [4, 2048, 2048], P(None, 'tp', ('shard', 'ctx')), may hold values from -0.5 to 0.5
- expert_gain: bfloat16 [2048], P(('shard', 'ctx')), may hold values from 0.5 to 1.5
- expert_router: bfloat16 [2048, 4], P(('shard', 'ctx')), may hold values from -0.09375 to 0.09375
- gate_weight: bfloat16 [4, 2048, 5632], P(None, ('shard', 'ctx'), 'tp'), may hold values from -0.125 to 0.125
- up_weight: bfloat16 [4, 2048, 5632], P(None, ('shard', 'ctx'), 'tp'), may hold values from -0.125 to 0.125
- down_weight: bfloat16 [4, 5632, 2048], P(None, 'tp', ('shard', 'ctx')), may hold values from -0.15625 to 0.15625
- cotangent: bfloat16 [2560, 2048], P(('shard', 'ctx')), may hold values from -6 to 6
Outputs:
- output: bfloat16 [2560, 2048], P(('shard', 'ctx'))
- input_gradient: bfloat16 [2560, 2048], P(('shard', 'ctx'))
- attention_gain_gradient: float32 [2048], P(('shard', 'ctx'))
- attention_router_gradient: float32 [2048, 4], P(('shard', 'ctx'))
- query_weight_gradient: float32 [4, 2048, 2048], P(None, ('shard', 'ctx'), 'tp')
- key_weight_gradient: float32 [2048, 2048], P(('shard', 'ctx'), 'tp')
- value_weight_gradient: float32 [2048, 2048], P(('shard', 'ctx'), 'tp')
- output_weight_gradient: float32 [4, 2048, 2048], P(None, 'tp', ('shard', 'ctx'))
- expert_gain_gradient: float32 [2048], P(('shard', 'ctx'))
- expert_router_gradient: float32 [2048, 4], P(('shard', 'ctx'))
- gate_weight_gradient: float32 [4, 2048, 5632], P(None, ('shard', 'ctx'), 'tp')
- up_weight_gradient: float32 [4, 2048, 5632], P(None, ('shard', 'ctx'), 'tp')
- down_weight_gradient: float32 [4, 5632, 2048], P(None, 'tp', ('shard', 'ctx'))
- clipped_query: bfloat16 [4, 2048, 2048], P(None, ('shard', 'ctx'), 'tp')
- clipped_key: bfloat16 [2048, 2048], P(('shard', 'ctx'), 'tp')
The draws below stay inside these ranges and needn't reach their ends.
Inputs may be any that keep to these rules, and one draw needn't show every extreme that they name: `parents`: the units of 64 tokens of each index of shard form trees of 20 units: a trunk of 8 units in a chain whose first unit has parent -1, 4 branch units whose parent is the trunk's last unit, and two leaf units under each branch unit. A parent lies among the units of the same index of shard. In each index of shard one tree has units on the first and on the last device of ctx. `attention_routes`: A row names two different experts. In the rows of one device no expert is named more than 176 times, and in some devices one expert is named exactly 176 times. `expert_routes`: A row names two different experts. In the rows of one device no expert is named more than 176 times, and in some devices one expert is named exactly 176 times.
All inputs are finite; a program needn't handle non-finite values.
Results may differ from the reference program's by a relative error of at most 0.024.
Values may be sent and summed in bfloat16 or wider, within the bound.
No kernel may reach another device: no remote copies, remote signals or barrier semaphores. Data moves between devices by JAX's collectives and lax.ppermute only.
A program may use at most 512 MiB of HBM per device.

```python
import math
import jax
import jax.numpy as jnp
import numpy as np
from jax import lax

D = 2048
HEADS = 16
HEAD_DIM = 128
FF = 5632
EXPERTS = 4
TOP = 2
SEG = 64
TREE_UNITS = 20
PATH = 10
UNITS_DEV = 5
TOK_DEV = 320
TOKENS = 2560
UNITS = 40
CAP = 176
N_CTX = 4


def draw_parents(key, part):
    key = jax.random.fold_in(key, 11)
    group_units = UNITS_DEV * N_CTX
    groups = UNITS // group_units
    places = jnp.arange(group_units, dtype=jnp.int32)
    roles = places % TREE_UNITS
    offset = jnp.where(roles >= 8, (roles - 8) % 3, 0)
    parent_role = jnp.where(roles == 0, -1, jnp.where(roles < 8, roles - 1, jnp.where(offset == 0, 7, roles - offset)))
    parent_slot = jnp.where(parent_role < 0, -1, places - roles + parent_role).astype(jnp.int32)

    def one_group(index):
        group_key = jax.random.fold_in(key, index)
        first_key, second_key = jax.random.split(group_key)
        layout = jax.random.permutation(first_key, group_units).astype(jnp.int32)
        priority = jax.random.permutation(second_key, group_units).astype(jnp.int32)
        tree_of = layout // TREE_UNITS
        chosen_tree = tree_of[0]
        candidate = jnp.where((tree_of == chosen_tree) & (places != 0), priority, -1)
        swap_place = jnp.argmax(candidate).astype(jnp.int32)
        last_value = layout[group_units - 1]
        swap_value = layout[swap_place]
        layout = layout.at[swap_place].set(last_value).at[group_units - 1].set(swap_value)
        place_of = jnp.zeros((group_units,), jnp.int32).at[layout].set(places)
        wanted = parent_slot[layout]
        return jnp.where(wanted < 0, -1, place_of[jnp.maximum(wanted, 0)] + index * group_units).astype(jnp.int32)
    return jax.vmap(one_group)(jnp.arange(groups, dtype=jnp.int32)).reshape(UNITS).astype(jnp.int32)


def draw_query_weight(key, part):
    key = jax.random.fold_in(key, 5)
    scale_key, jitter_key, base_key = jax.random.split(key, 3)
    head_scale = jnp.exp(jax.random.uniform(scale_key, (1, 1, HEADS, 1), minval=math.log(0.9), maxval=math.log(3.0)))
    jitter = jax.random.uniform(jitter_key, (EXPERTS, 1, HEADS, 1), minval=0.85, maxval=1.15)
    base = jax.random.normal(base_key, (EXPERTS, D, HEADS, HEAD_DIM))
    values = base * head_scale * jitter / math.sqrt(D)
    return values.reshape(EXPERTS, D, HEADS * HEAD_DIM).astype(jnp.float32).astype(jnp.bfloat16)


def spiked(values, own_key, source, target, blocks, factor):
    owner, partner = [(jnp.arange(values.shape[position]) // (values.shape[position] // blocks)).reshape([-1 if axis == position else 1 for axis in range(values.ndim)]) for position in (source, target)]
    chosen = jax.random.permutation(own_key, blocks)[partner]
    strong = (owner == chosen) | (owner == (partner + blocks // 2) % blocks)
    return jnp.where(strong, factor * values, values)


def level_of(stream_key, dims, shards, least, high):
    loudness = 1.0
    for axis_at, shards_of in shards:
        steps = jax.random.uniform(jax.random.fold_in(jax.random.fold_in(stream_key, 6), axis_at), (shards_of,), jnp.float32, least / len(shards), high / len(shards))
        loudness = loudness * jnp.repeat(jnp.exp(steps), dims[axis_at] // shards_of).reshape((-1,) + (1,) * (len(dims) - 1 - axis_at))
    return loudness


def routed_block(stream_key, own, number, rows, count, top, reach, lean):
    sequence = jax.random.permutation(stream_key, count)
    heavy_load, ordinary = load_shares(count, rows * top, reach, lean, True), load_shares(count, rows * top, reach, lean, False)
    places = jnp.arange(count)

    def named(tallies, rotation):
        used = int((tallies > 0).sum())
        fixed = max(1, used // 4)
        passed = fixed + (places - fixed + rotation * (used - fixed)) % max(1, count - fixed)
        return jnp.zeros((count,), jnp.int32).at[sequence[jnp.where(places < fixed, places, passed)]].set(jnp.asarray(tallies, jnp.int32))

    tallies = jnp.where(number % 4 == 0, named(heavy_load, number // 4), named(ordinary, number - number // 4 - 1))
    mixed = jax.random.permutation(jax.random.fold_in(own, 3), count)
    giver, receiver = mixed[0:count // 2 * 2:2], mixed[1:count // 2 * 2:2]
    margin = jnp.minimum(tallies[giver] - 1, reach - tallies[receiver]) // 2
    margin = jnp.where((giver == sequence[0]) | (receiver == sequence[0]) | (tallies[receiver] == 0), 0, jnp.maximum(margin, 0))
    passed = jax.random.randint(jax.random.fold_in(own, 4), (count // 2,), 0, 1 << 20) % (margin + 1)
    tallies = tallies.at[giver].add(-passed).at[receiver].add(passed)
    members = jnp.searchsorted(jnp.cumsum(tallies), jnp.arange(rows * top), side="right").astype(jnp.int32)
    table = members.reshape(top, rows).T
    table = table[jax.random.permutation(jax.random.fold_in(own, 1), rows)]
    rotation = jax.random.randint(jax.random.fold_in(own, 2), (rows, 1), 0, top)
    return jnp.take_along_axis(table, (jnp.arange(top)[None, :] + rotation) % top, axis=1)


def load_shares(amount, total, reach, skew, full):
    loads = [(1 << 20) // math.isqrt(grade ** skew) + 1 for grade in range(1, amount + 1)]
    largest = reach if full else min(reach, max(-(-total // amount), total * loads[0] // sum(loads)))
    least = 1 if total - largest >= amount - 1 else 0
    holding, surplus = [largest] + [least] * (amount - 1), total - largest - least * (amount - 1)
    while surplus > 0:
        candidates = [i for i in range(1, amount) if holding[i] < largest] or [i for i in range(1, amount) if holding[i] < reach]
        pool, budget = sum([loads[i] for i in candidates]), surplus
        for i in candidates:
            addition = min(reach - holding[i], max(1, budget * loads[i] // pool), surplus)
            holding[i] = holding[i] + addition
            surplus = surplus - addition
    return np.array(holding)


def scatter_about(key, shape, width, limit, cuts=(), held_as=jnp.bfloat16):
    array = width * jax.random.normal(key, shape, jnp.float32)
    if cuts:
        array = array * level_of(key, shape, cuts, -0.22, 0.18)
    return jnp.clip(array, -limit, limit).astype(held_as)


def noise_with(stream_key, shape, spread, bound, cuts, heavy, held_as=jnp.bfloat16):
    entries = spread * jax.random.normal(stream_key, shape, jnp.float32)
    if cuts:
        entries = entries * level_of(stream_key, shape, cuts, -0.22, 0.18)
    return jnp.clip(spiked(entries, jax.random.fold_in(stream_key, 3), *heavy), -bound, bound).astype(held_as)


def setup_inputs(seed: int = 0) -> dict:
    seeds = jax.random.split(jax.random.key(seed), 17)
    inputs = scatter_about(seeds[0], (TOKENS, D), 1.0, 6.0, ((0, 8),))
    parents = draw_parents(jax.random.fold_in(seeds[16], 71), 0)
    attention_routes_keys = jax.random.split(jax.random.fold_in(seeds[2], 1), TOKENS // TOK_DEV)
    attention_routes_turns = jax.random.permutation(jax.random.fold_in(seeds[2], 3), TOKENS // TOK_DEV)
    attention_routes = jax.vmap(lambda own, number: routed_block(jax.random.fold_in(seeds[2], 2), own, number, TOK_DEV, EXPERTS, TOP, CAP, 1))(attention_routes_keys, attention_routes_turns).reshape((TOKENS, TOP))
    expert_routes_keys = jax.random.split(jax.random.fold_in(seeds[3], 1), TOKENS // TOK_DEV)
    expert_routes_turns = jax.random.permutation(jax.random.fold_in(seeds[3], 3), TOKENS // TOK_DEV)
    expert_routes = jax.vmap(lambda own, number: routed_block(jax.random.fold_in(seeds[3], 2), own, number, TOK_DEV, EXPERTS, TOP, CAP, 1))(expert_routes_keys, expert_routes_turns).reshape((TOKENS, TOP))
    attention_gain = jnp.clip(1.0 + 0.1 * jax.random.normal(seeds[4], (D,), jnp.float32), 0.5, 1.5).astype(jnp.bfloat16)
    attention_router = scatter_about(seeds[5], (D, EXPERTS), (2 * D) ** -0.5, 0.09375, ((0, 8),))
    query_weight = draw_query_weight(jax.random.fold_in(seeds[16], 71), 0)
    key_weight = scatter_about(seeds[7], (D, HEADS * HEAD_DIM), D ** -0.5, 0.125, ((0, 8), (1, 4)))
    value_weight = scatter_about(seeds[8], (D, HEADS * HEAD_DIM), D ** -0.5, 0.125, ((0, 8), (1, 4)))
    output_weight = scatter_about(seeds[9], (EXPERTS, HEADS * HEAD_DIM, D), (HEADS * HEAD_DIM // 16) ** -0.5, 0.5, ((1, 4), (2, 8)))
    expert_gain = jnp.clip(1.0 + 0.1 * jax.random.normal(seeds[10], (D,), jnp.float32), 0.5, 1.5).astype(jnp.bfloat16)
    expert_router = scatter_about(seeds[11], (D, EXPERTS), (2 * D) ** -0.5, 0.09375, ((0, 8),))
    gate_weight = scatter_about(seeds[12], (EXPERTS, D, FF), D ** -0.5, 0.125, ((1, 8), (2, 4)))
    up_weight = scatter_about(seeds[13], (EXPERTS, D, FF), D ** -0.5, 0.125, ((1, 8), (2, 4)))
    down_weight = scatter_about(seeds[14], (EXPERTS, FF, D), (FF // 4) ** -0.5, 0.15625, ((1, 4), (2, 8)))
    cotangent = noise_with(seeds[15], (TOKENS, D), 1.0, 6.0, ((0, 8),), (0, 1, 8, 2.0))
    return {"inputs": inputs, "parents": parents, "attention_routes": attention_routes, "expert_routes": expert_routes, "attention_gain": attention_gain, "attention_router": attention_router, "query_weight": query_weight, "key_weight": key_weight, "value_weight": value_weight, "output_weight": output_weight, "expert_gain": expert_gain, "expert_router": expert_router, "gate_weight": gate_weight, "up_weight": up_weight, "down_weight": down_weight, "cotangent": cotangent}


@jax.custom_vjp
def low(v):
    return lax.optimization_barrier(v.astype(jnp.bfloat16)).astype(jnp.float32)

@jax.custom_vjp
def low_back(v):
    return v

def low_keep(v):
    return (low(v), None)

def low_pass(kept, grad):
    return (grad,)

def back_keep(v):
    return (v, None)

def back_low(kept, grad):
    return (low(grad),)
low.defvjp(low_keep, low_pass)
low_back.defvjp(back_keep, back_low)
EPS = 1e-05
ROPE_BASE = 10000.0
CLIP = 2.0
HIGH = lax.Precision.HIGHEST

def normalize(value, gain):
    scale = lax.rsqrt(lax.optimization_barrier(jnp.mean(value * value, axis=-1, keepdims=True)) + EPS)
    return value * scale * gain

def gating(normed, router, routes):
    logits = jnp.dot(normed, router, precision=HIGH)
    chosen = jnp.take_along_axis(logits, routes, axis=1)
    return jax.nn.softmax(chosen, axis=1)

def slot_tables(routes, experts, capacity):
    number = routes.shape[0] * routes.shape[1]
    flat = routes.reshape(number).astype(jnp.int32)
    onehot = (flat[:, None] == jnp.arange(experts, dtype=jnp.int32)[None, :]).astype(jnp.int32)
    before = jnp.cumsum(onehot, axis=0, dtype=jnp.int32) - onehot
    place = lax.optimization_barrier(jnp.sum(before * onehot, axis=1, dtype=jnp.int32))
    slot_index = (flat * capacity + place).astype(jnp.int32)
    pair_index = jnp.zeros((experts * capacity,), jnp.int32).at[slot_index].set(jnp.arange(number, dtype=jnp.int32))
    filled = jnp.zeros((experts * capacity,), jnp.int32).at[slot_index].set(1)
    return (slot_index, pair_index, filled)

def rope_tables(positions, half):
    frequency = ROPE_BASE ** (-jnp.arange(half, dtype=jnp.float32) / half)
    angle = positions.astype(jnp.float32)[:, None] * frequency[None, :]
    return (jnp.cos(angle), jnp.sin(angle))

def rotate(value, cosine, sine):
    half = value.shape[-1] // 2
    first = value[..., :half]
    second = value[..., half:]
    return jnp.concatenate([first * cosine - second * sine, second * cosine + first * sine], axis=-1)

def ancestors(parents, start_units):
    chain = [start_units]
    current = start_units
    for level in range(PATH - 1):
        current = jnp.where(current >= 0, parents[jnp.maximum(current, 0)], -1).astype(jnp.int32)
        chain.append(current)
    return jnp.stack(chain, axis=1)

def unit_mask(valid_row):
    token_row = jnp.arange(SEG * TOP) // TOP
    causal = jnp.arange(SEG)[None, :] <= token_row[:, None]
    others = jnp.broadcast_to(valid_row[None, 1:, None], (SEG * TOP, PATH - 1, SEG))
    return jnp.concatenate([causal[:, None, :], others], axis=1).reshape(SEG * TOP, PATH * SEG)

def reference(inputs, parents, attention_routes, expert_routes, attention_gain, attention_router, query_weight, key_weight, value_weight, output_weight, expert_gain, expert_router, gate_weight, up_weight, down_weight, cotangent):
    blocks = TOKENS // TOK_DEV
    inner = HEADS * HEAD_DIM
    chain = ancestors(parents, jnp.arange(UNITS, dtype=jnp.int32))
    valid = chain >= 0
    depth = lax.optimization_barrier(jnp.sum(valid[:, 1:].astype(jnp.int32), axis=1, dtype=jnp.int32))
    positions = (depth[:, None] * SEG + jnp.arange(SEG, dtype=jnp.int32)[None, :]).reshape(TOKENS)
    cosine, sine = rope_tables(positions, HEAD_DIM // 2)
    safe_chain = jnp.maximum(chain, 0)

    def tables(routes):
        return jax.vmap(lambda block: slot_tables(block, EXPERTS, CAP))(routes.reshape(blocks, TOK_DEV, TOP))
    head_slot, head_pair, head_filled = tables(attention_routes)
    expert_slot, expert_pair, expert_filled = tables(expert_routes)
    cosine_blocks = cosine.reshape(blocks, TOK_DEV, HEAD_DIM // 2)
    sine_blocks = sine.reshape(blocks, TOK_DEV, HEAD_DIM // 2)

    def forward(state, gain_one, router_one, query_matrix, key_matrix, value_matrix, output_matrix, gain_two, router_two, gate_matrix, up_matrix, down_matrix):
        normed = low(normalize(state, gain_one))
        head_gates = gating(normed, router_one, attention_routes)
        key_raw = low_back(jnp.dot(normed, key_matrix, precision=HIGH)).reshape(TOKENS, HEADS, HEAD_DIM)
        keys = low(rotate(key_raw, cosine[:, None, :], sine[:, None, :]))
        values = low(low_back(jnp.dot(normed, value_matrix, precision=HIGH))).reshape(TOKENS, HEADS, HEAD_DIM)

        def query_block(item):
            rows, slot_index, pair_index, filled, cosine_block, sine_block = item
            chosen = jnp.where(filled[:, None] > 0, rows[pair_index // TOP], 0.0).reshape(EXPERTS, CAP, D)
            slots = jnp.einsum('ecd,edf->ecf', chosen, query_matrix, precision=HIGH)
            pairs = low_back(slots.reshape(EXPERTS * CAP, inner)[slot_index]).reshape(TOK_DEV, TOP, HEADS, HEAD_DIM)
            return low(rotate(pairs, cosine_block[:, None, None, :], sine_block[:, None, None, :]))
        queries = lax.map(jax.checkpoint(query_block), (normed.reshape(blocks, TOK_DEV, D), head_slot, head_pair, head_filled, cosine_blocks, sine_blocks))
        key_units = keys.reshape(UNITS, SEG, HEADS, HEAD_DIM)
        value_units = values.reshape(UNITS, SEG, HEADS, HEAD_DIM)

        def attend(item):
            query, unit_chain, unit_valid = item
            near_keys = key_units[unit_chain].reshape(PATH * SEG, HEADS, HEAD_DIM)
            near_values = value_units[unit_chain].reshape(PATH * SEG, HEADS, HEAD_DIM)
            scores = low_back(jnp.einsum('qhd,khd->hqk', query, near_keys, precision=HIGH) * HEAD_DIM ** (-0.5))
            allowed = unit_mask(unit_valid)[None]
            masked = jnp.where(allowed, scores, -1e+30)
            peak = lax.optimization_barrier(jnp.max(masked, axis=-1, keepdims=True))
            weights = jnp.where(allowed, jnp.exp(masked - peak), 0.0)
            shares = low(weights / lax.optimization_barrier(jnp.sum(weights, axis=-1, keepdims=True)))
            mixed = jnp.einsum('hqk,khd->qhd', shares, near_values, precision=HIGH)
            return (low(low_back(mixed)), lax.optimization_barrier(jnp.max(peak[:, :, 0], axis=1)))
        mixed, peaks = lax.map(jax.checkpoint(attend), (queries.reshape(UNITS, SEG * TOP, HEADS, HEAD_DIM), safe_chain, valid))

        def output_block(item):
            mixed_block, gate_block, slot_index, pair_index, filled = item
            chosen = jnp.where(filled[:, None] > 0, mixed_block.reshape(TOK_DEV * TOP, inner)[pair_index], 0.0).reshape(EXPERTS, CAP, inner)
            slots = jnp.einsum('ecf,efd->ecd', chosen, output_matrix, precision=HIGH)
            pairs = low_back(slots.reshape(EXPERTS * CAP, D)[slot_index].reshape(TOK_DEV, TOP, D))
            return lax.optimization_barrier(jnp.sum(gate_block[:, :, None] * pairs, axis=1))
        attention = lax.map(jax.checkpoint(output_block), (mixed.reshape(blocks, TOK_DEV, TOP, inner), head_gates.reshape(blocks, TOK_DEV, TOP), head_slot, head_pair, head_filled)).reshape(TOKENS, D)
        hidden_state = state + attention
        normed_two = low(normalize(hidden_state, gain_two))
        expert_gates = gating(normed_two, router_two, expert_routes)

        def expert_block(item):
            rows, gate_block, slot_index, pair_index, filled = item
            chosen = jnp.where(filled[:, None] > 0, rows[pair_index // TOP], 0.0).reshape(EXPERTS, CAP, D)
            gate_pre = low_back(jnp.einsum('ecd,edf->ecf', chosen, gate_matrix, precision=HIGH))
            up_pre = low_back(jnp.einsum('ecd,edf->ecf', chosen, up_matrix, precision=HIGH))
            activated = low(jax.nn.silu(gate_pre) * up_pre)
            slots = jnp.einsum('ecf,efd->ecd', activated, down_matrix, precision=HIGH)
            pairs = low_back(slots.reshape(EXPERTS * CAP, D)[slot_index].reshape(TOK_DEV, TOP, D))
            return lax.optimization_barrier(jnp.sum(gate_block[:, :, None] * pairs, axis=1))
        feed = lax.map(jax.checkpoint(expert_block), (normed_two.reshape(blocks, TOK_DEV, D), expert_gates.reshape(blocks, TOK_DEV, TOP), expert_slot, expert_pair, expert_filled)).reshape(TOKENS, D)
        return (hidden_state + feed, lax.optimization_barrier(jnp.max(peaks, axis=0)))
    floats = tuple((item.astype(jnp.float32) for item in (inputs, attention_gain, attention_router, query_weight, key_weight, value_weight, output_weight, expert_gain, expert_router, gate_weight, up_weight, down_weight)))
    output, pull, head_peak = jax.vjp(forward, *floats, has_aux=True)
    gradients = pull(cotangent.astype(jnp.float32))
    factor = jnp.sqrt(jnp.minimum(1.0, CLIP / head_peak))
    columns = jnp.repeat(factor, HEAD_DIM)
    clipped_query = (query_weight.astype(jnp.float32) * columns).astype(jnp.bfloat16)
    clipped_key = (key_weight.astype(jnp.float32) * columns).astype(jnp.bfloat16)
    return (output.astype(jnp.bfloat16), gradients[0].astype(jnp.bfloat16), gradients[1], gradients[2], gradients[3], gradients[4], gradients[5], gradients[6], gradients[7], gradients[8], gradients[9], gradients[10], gradients[11], clipped_query, clipped_key)
```

```python
import jax
import jax.numpy as jnp
from jax import lax
from jax.experimental import pallas as pl
from jax.experimental.pallas import tpu as pltpu
from jax.sharding import PartitionSpec as P

HEAD_DIM = 128
TOP = 2
SEG = 64
PATH = 10
CAP = 176


EPS = 1e-05
ROPE_BASE = 10000.0
CLIP = 2.0
HIGH = lax.Precision.HIGHEST


def normalize(value, gain):
    scale = lax.rsqrt(jnp.mean(value * value, axis=-1, keepdims=True) + EPS)
    return value * scale * gain


def normalize_back(change, value, gain):
    scale = lax.rsqrt(jnp.mean(value * value, axis=-1, keepdims=True) + EPS)
    gain_change = jnp.sum(change * value * scale, axis=0)
    scaled = change * gain
    value_change = scale * scaled - value * scale**3 * jnp.mean(
        scaled * value, axis=-1, keepdims=True
    )
    return (value_change, gain_change)


def gating(normed, router, routes):
    logits = jnp.dot(normed, router, preferred_element_type=jnp.float32)
    chosen = jnp.take_along_axis(logits, routes, axis=1)
    return jax.nn.softmax(chosen, axis=1)


def gating_back(change, gates, routes, experts):
    chosen_change = gates * (change - jnp.sum(gates * change, axis=1, keepdims=True))
    onehot = (routes[:, :, None] == jnp.arange(experts, dtype=jnp.int32)[None, None, :]).astype(
        jnp.float32
    )
    return jnp.sum(chosen_change[:, :, None] * onehot, axis=1)


def slot_tables(routes, experts, capacity):
    number = routes.shape[0] * routes.shape[1]
    flat = routes.reshape(number)
    onehot = (flat[:, None] == jnp.arange(experts, dtype=jnp.int32)[None, :]).astype(jnp.int32)
    before = jnp.cumsum(onehot, axis=0, dtype=jnp.int32) - onehot
    place = jnp.sum(before * onehot, axis=1, dtype=jnp.int32)
    slot_index = flat * capacity + place
    pair_index = (
        jnp.zeros((experts * capacity,), jnp.int32)
        .at[slot_index]
        .set(jnp.arange(number, dtype=jnp.int32))
    )
    filled = jnp.zeros((experts * capacity,), jnp.int32).at[slot_index].set(1)
    return (slot_index, pair_index, filled)


def rope_tables(positions, half):
    frequency = ROPE_BASE ** (-jnp.arange(half, dtype=jnp.float32) / half)
    angle = positions.astype(jnp.float32)[:, None] * frequency[None, :]
    return (jnp.cos(angle), jnp.sin(angle))


def rotate(value, cosine, sine):
    half = value.shape[-1] // 2
    first = value[..., :half]
    second = value[..., half:]
    return jnp.concatenate(
        [first * cosine - second * sine, second * cosine + first * sine], axis=-1
    )


def rotate_back(change, cosine, sine):
    half = change.shape[-1] // 2
    first = change[..., :half]
    second = change[..., half:]
    return jnp.concatenate(
        [first * cosine + second * sine, second * cosine - first * sine], axis=-1
    )


def ancestors(parents, start_units):
    chain = [start_units]
    current = start_units
    for level in range(PATH - 1):
        current = jnp.where(current >= 0, parents[jnp.maximum(current, 0)], -1)
        chain.append(current)
    return jnp.stack(chain, axis=1)


def unit_mask(valid_row):
    token_row = jnp.arange(SEG * TOP) // TOP
    causal = jnp.arange(SEG)[None, :] <= token_row[:, None]
    others = jnp.broadcast_to(valid_row[None, 1:, None], (SEG * TOP, PATH - 1, SEG))
    return jnp.concatenate([causal[:, None, :], others], axis=1).reshape(SEG * TOP, PATH * SEG)


def dispatch(rows, pair_index, filled, choose, experts, capacity):
    picked = rows[pair_index // choose]
    return jnp.where(filled[:, None] > 0, picked, jnp.zeros((), rows.dtype)).reshape(
        experts, capacity, rows.shape[1]
    )


def spread(pairs, pair_index, filled, experts, capacity):
    picked = pairs[pair_index]
    return jnp.where(filled[:, None] > 0, picked, jnp.zeros((), pairs.dtype)).reshape(
        experts, capacity, pairs.shape[1]
    )


def on_device_general(
    inputs,
    parents,
    attention_routes,
    expert_routes,
    attention_gain,
    attention_router,
    query_weight,
    key_weight,
    value_weight,
    output_weight,
    expert_gain,
    expert_router,
    gate_weight,
    up_weight,
    down_weight,
    cotangent,
):
    count = inputs.shape[0]
    width = inputs.shape[1]
    experts = query_weight.shape[0]
    local_width = query_weight.shape[2]
    head_dim = HEAD_DIM
    local_heads = local_width // head_dim
    capacity = CAP
    choose = attention_routes.shape[1]
    segment = SEG
    units_here = count // segment
    group_units = lax.axis_size("ctx") * units_here
    scale = head_dim ** (-0.5)
    gain_one, router_one, query_full, key_full, value_full, output_full, gain_two, router_two = (
        lax.all_gather(attention_gain, ("shard", "ctx"), axis=0, tiled=True),
        lax.all_gather(attention_router, ("shard", "ctx"), axis=0, tiled=True),
        lax.all_gather(query_weight, ("shard", "ctx"), axis=1, tiled=True),
        lax.all_gather(key_weight, ("shard", "ctx"), axis=0, tiled=True),
        lax.all_gather(value_weight, ("shard", "ctx"), axis=0, tiled=True),
        lax.all_gather(output_weight, ("shard", "ctx"), axis=2, tiled=True),
        lax.all_gather(expert_gain, ("shard", "ctx"), axis=0, tiled=True),
        lax.all_gather(expert_router, ("shard", "ctx"), axis=0, tiled=True),
    )
    first_unit = (
        lax.axis_index("shard") * lax.axis_size("ctx") + lax.axis_index("ctx")
    ) * units_here
    group_first = lax.axis_index("shard") * group_units
    own_units = first_unit + jnp.arange(units_here, dtype=jnp.int32)
    chain = ancestors(parents, own_units)
    valid = chain >= 0
    depth = jnp.sum(valid[:, 1:].astype(jnp.int32), axis=1, dtype=jnp.int32)
    positions = (depth[:, None] * segment + jnp.arange(segment, dtype=jnp.int32)[None, :]).reshape(
        count
    )
    cosine, sine = rope_tables(positions, head_dim // 2)
    local_chain = jnp.clip(chain - group_first, 0, group_units - 1)
    allowed = jax.vmap(unit_mask)(valid)
    residual = inputs.astype(jnp.float32)
    gain_first = gain_one.astype(jnp.float32)
    normed = normalize(residual, gain_first).astype(jnp.bfloat16)
    head_gates = gating(normed, router_one, attention_routes)
    head_slot, head_pair, head_filled = slot_tables(attention_routes, experts, capacity)
    head_rows = dispatch(normed, head_pair, head_filled, choose, experts, capacity)
    query_slots = jnp.einsum(
        "ecd,edf->ecf", head_rows, query_full, preferred_element_type=jnp.float32
    )
    query_pairs = query_slots.reshape(experts * capacity, local_width)[head_slot].reshape(
        count, choose, local_heads, head_dim
    )
    queries = rotate(query_pairs, cosine[:, None, None, :], sine[:, None, None, :]).astype(
        jnp.bfloat16
    )
    key_raw = jnp.dot(normed, key_full, preferred_element_type=jnp.float32).reshape(
        count, local_heads, head_dim
    )
    keys = (
        rotate(key_raw, cosine[:, None, :], sine[:, None, :])
        .astype(jnp.bfloat16)
        .reshape(count, local_width)
    )
    values = jnp.dot(normed, value_full, preferred_element_type=jnp.float32).astype(jnp.bfloat16)
    all_keys, all_values = (
        lax.all_gather(keys, "ctx", axis=0, tiled=True),
        lax.all_gather(values, "ctx", axis=0, tiled=True),
    )
    path_keys = all_keys.reshape(group_units, segment, local_width)[local_chain].reshape(
        units_here, PATH * segment, local_heads, head_dim
    )
    path_values = all_values.reshape(group_units, segment, local_width)[local_chain].reshape(
        units_here, PATH * segment, local_heads, head_dim
    )
    query_units = queries.reshape(units_here, segment * choose, local_heads, head_dim)
    scores = (
        jnp.einsum("uqhd,ukhd->uhqk", query_units, path_keys, preferred_element_type=jnp.float32)
        * scale
    )
    masked = jnp.where(allowed[:, None], scores, -1e30)
    peak = jnp.max(masked, axis=-1, keepdims=True)
    weights = jnp.where(allowed[:, None], jnp.exp(masked - peak), 0.0)
    total = jnp.sum(weights, axis=-1, keepdims=True)
    log_total = peak + jnp.log(total)
    head_peak = jnp.max(peak[..., 0], axis=(0, 2))
    shares = (weights / total).astype(jnp.bfloat16)
    mixed = (
        jnp.einsum("uhqk,ukhd->uqhd", shares, path_values, preferred_element_type=jnp.float32)
        .astype(jnp.bfloat16)
        .reshape(count * choose, local_width)
    )
    mixed_slots = spread(mixed, head_pair, head_filled, experts, capacity)
    out_slots = jnp.einsum(
        "ecf,efd->ecd", mixed_slots, output_full, preferred_element_type=jnp.float32
    )
    out_pairs = out_slots.reshape(experts * capacity, width)[head_slot].reshape(
        count, choose, width
    )
    attention = lax.psum(jnp.sum(head_gates[:, :, None] * out_pairs, axis=1), "tp")
    hidden_state = residual + attention
    peak_all = lax.pmax(head_peak, ("shard", "ctx"))
    gain_second = gain_two.astype(jnp.float32)
    normed_two = normalize(hidden_state, gain_second).astype(jnp.bfloat16)
    expert_gates = gating(normed_two, router_two, expert_routes)
    expert_slot, expert_pair, expert_filled = slot_tables(expert_routes, experts, capacity)
    expert_rows = dispatch(normed_two, expert_pair, expert_filled, choose, experts, capacity)
    gate_full, up_full, down_full = (
        lax.all_gather(gate_weight, ("shard", "ctx"), axis=1, tiled=True),
        lax.all_gather(up_weight, ("shard", "ctx"), axis=1, tiled=True),
        lax.all_gather(down_weight, ("shard", "ctx"), axis=2, tiled=True),
    )
    gate_pre = jnp.einsum(
        "ecd,edf->ecf", expert_rows, gate_full, preferred_element_type=jnp.float32
    )
    up_pre = jnp.einsum("ecd,edf->ecf", expert_rows, up_full, preferred_element_type=jnp.float32)
    activated = (jax.nn.silu(gate_pre) * up_pre).astype(jnp.bfloat16)
    down_slots = jnp.einsum(
        "ecf,efd->ecd", activated, down_full, preferred_element_type=jnp.float32
    )
    down_pairs = down_slots.reshape(experts * capacity, width)[expert_slot].reshape(
        count, choose, width
    )
    feed = lax.psum(
        jnp.sum(expert_gates[:, :, None] * down_pairs, axis=1).astype(jnp.bfloat16), "tp"
    ).astype(jnp.float32)
    output = (hidden_state + feed).astype(jnp.bfloat16)
    upstream = cotangent.astype(jnp.float32)
    down_back = (
        (expert_gates[:, :, None] * upstream[:, None, :])
        .astype(jnp.bfloat16)
        .reshape(count * choose, width)
    )
    expert_gate_part = jnp.sum(down_pairs * upstream[:, None, :], axis=2)
    down_back_slots = spread(down_back, expert_pair, expert_filled, experts, capacity)
    act_back = jnp.einsum(
        "ecd,efd->ecf", down_back_slots, down_full, preferred_element_type=jnp.float32
    )
    sigmoid = jax.nn.sigmoid(gate_pre)
    gate_back = (act_back * up_pre * sigmoid * (1.0 + gate_pre * (1.0 - sigmoid))).astype(
        jnp.bfloat16
    )
    up_back = (act_back * gate_pre * sigmoid).astype(jnp.bfloat16)
    rows_back = jnp.einsum(
        "ecf,edf->ecd", gate_back, gate_full, preferred_element_type=jnp.float32
    ) + jnp.einsum("ecf,edf->ecd", up_back, up_full, preferred_element_type=jnp.float32)
    normed_two_part = jnp.sum(
        rows_back.reshape(experts * capacity, width)[expert_slot].reshape(count, choose, width),
        axis=1,
    )
    collected = []
    for expert in range(experts):
        gate_term = jnp.einsum(
            "cd,cf->df", expert_rows[expert], gate_back[expert], preferred_element_type=jnp.float32
        )
        up_term = jnp.einsum(
            "cd,cf->df", expert_rows[expert], up_back[expert], preferred_element_type=jnp.float32
        )
        down_term = jnp.einsum(
            "cf,cd->fd",
            activated[expert],
            down_back_slots[expert],
            preferred_element_type=jnp.float32,
        )
        collected.append(
            (
                lax.psum_scatter(
                    gate_term.astype(jnp.bfloat16),
                    ("shard", "ctx"),
                    scatter_dimension=0,
                    tiled=True,
                ).astype(jnp.float32),
                lax.psum_scatter(
                    up_term.astype(jnp.bfloat16), ("shard", "ctx"), scatter_dimension=0, tiled=True
                ).astype(jnp.float32),
                lax.psum_scatter(
                    down_term.astype(jnp.bfloat16),
                    ("shard", "ctx"),
                    scatter_dimension=1,
                    tiled=True,
                ).astype(jnp.float32),
            )
        )
    gate_gradient = jnp.stack([item[0] for item in collected])
    up_gradient = jnp.stack([item[1] for item in collected])
    down_gradient = jnp.stack([item[2] for item in collected])
    normed_two_back, expert_gate_back = lax.psum((normed_two_part, expert_gate_part), "tp")
    expert_logit_back = gating_back(expert_gate_back, expert_gates, expert_routes, experts)
    router_two_term = jnp.einsum(
        "td,te->de", normed_two.astype(jnp.float32), expert_logit_back, precision=HIGH
    )
    normed_two_back = normed_two_back + jnp.einsum(
        "te,de->td", expert_logit_back, router_two.astype(jnp.float32), precision=HIGH
    )
    hidden_back, gain_two_term = normalize_back(normed_two_back, hidden_state, gain_second)
    hidden_back = hidden_back + upstream
    head_back = (
        (head_gates[:, :, None] * hidden_back[:, None, :])
        .astype(jnp.bfloat16)
        .reshape(count * choose, width)
    )
    head_gate_part = jnp.sum(out_pairs * hidden_back[:, None, :], axis=2)
    head_back_slots = spread(head_back, head_pair, head_filled, experts, capacity)
    output_term = jnp.einsum(
        "ecf,ecd->efd", mixed_slots, head_back_slots, preferred_element_type=jnp.float32
    )
    mixed_back_slots = jnp.einsum(
        "ecd,efd->ecf", head_back_slots, output_full, preferred_element_type=jnp.float32
    )
    mixed_back = (
        mixed_back_slots.reshape(experts * capacity, local_width)[head_slot]
        .astype(jnp.bfloat16)
        .reshape(units_here, segment * choose, local_heads, head_dim)
    )
    again = (
        jnp.einsum("uqhd,ukhd->uhqk", query_units, path_keys, preferred_element_type=jnp.float32)
        * scale
    )
    chances = jnp.where(allowed[:, None], jnp.exp(again - log_total), 0.0)
    value_path_back = jnp.einsum(
        "uhqk,uqhd->ukhd",
        chances.astype(jnp.bfloat16),
        mixed_back,
        preferred_element_type=jnp.float32,
    )
    share_back = jnp.einsum(
        "uqhd,ukhd->uhqk", mixed_back, path_values, preferred_element_type=jnp.float32
    )
    score_back = (
        chances * (share_back - jnp.sum(chances * share_back, axis=-1, keepdims=True))
    ).astype(jnp.bfloat16)
    query_back_raw = (
        jnp.einsum("uhqk,ukhd->uqhd", score_back, path_keys, preferred_element_type=jnp.float32)
        * scale
    )
    key_path_back = (
        jnp.einsum("uhqk,uqhd->ukhd", score_back, query_units, preferred_element_type=jnp.float32)
        * scale
    )
    owner = (
        (local_chain[:, :, None] == jnp.arange(group_units, dtype=jnp.int32)[None, None, :])
        & valid[:, :, None]
    ).astype(jnp.float32)
    key_group = jnp.einsum(
        "upg,upsc->gsc",
        owner,
        key_path_back.reshape(units_here, PATH, segment, local_width),
        precision=HIGH,
    )
    value_group = jnp.einsum(
        "upg,upsc->gsc",
        owner,
        value_path_back.reshape(units_here, PATH, segment, local_width),
        precision=HIGH,
    )
    key_mine, value_mine = (
        lax.psum_scatter(
            key_group.reshape(group_units * segment, local_width).astype(jnp.bfloat16),
            "ctx",
            scatter_dimension=0,
            tiled=True,
        ).astype(jnp.float32),
        lax.psum_scatter(
            value_group.reshape(group_units * segment, local_width).astype(jnp.bfloat16),
            "ctx",
            scatter_dimension=0,
            tiled=True,
        ).astype(jnp.float32),
    )
    key_back = (
        rotate_back(
            key_mine.reshape(count, local_heads, head_dim), cosine[:, None, :], sine[:, None, :]
        )
        .astype(jnp.bfloat16)
        .reshape(count, local_width)
    )
    value_back = value_mine.astype(jnp.bfloat16)
    query_back = (
        rotate_back(
            query_back_raw.reshape(count, choose, local_heads, head_dim),
            cosine[:, None, None, :],
            sine[:, None, None, :],
        )
        .astype(jnp.bfloat16)
        .reshape(count * choose, local_width)
    )
    query_back_slots = spread(query_back, head_pair, head_filled, experts, capacity)
    query_term = jnp.einsum(
        "ecd,ecf->edf", head_rows, query_back_slots, preferred_element_type=jnp.float32
    )
    key_term = jnp.einsum("td,tf->df", normed, key_back, preferred_element_type=jnp.float32)
    value_term = jnp.einsum("td,tf->df", normed, value_back, preferred_element_type=jnp.float32)
    query_rows_back = jnp.einsum(
        "ecf,edf->ecd", query_back_slots, query_full, preferred_element_type=jnp.float32
    )
    normed_part = jnp.sum(
        query_rows_back.reshape(experts * capacity, width)[head_slot].reshape(count, choose, width),
        axis=1,
    )
    normed_part = (
        normed_part
        + jnp.einsum("tf,df->td", key_back, key_full, preferred_element_type=jnp.float32)
        + jnp.einsum("tf,df->td", value_back, value_full, preferred_element_type=jnp.float32)
    )
    normed_back, head_gate_back = (
        lax.psum(normed_part.astype(jnp.bfloat16), "tp").astype(jnp.float32),
        lax.psum(head_gate_part.astype(jnp.bfloat16), "tp").astype(jnp.float32),
    )
    head_logit_back = gating_back(head_gate_back, head_gates, attention_routes, experts)
    router_one_term = jnp.einsum(
        "td,te->de", normed.astype(jnp.float32), head_logit_back, precision=HIGH
    )
    normed_back = normed_back + jnp.einsum(
        "te,de->td", head_logit_back, router_one.astype(jnp.float32), precision=HIGH
    )
    input_back, gain_one_term = normalize_back(normed_back, residual, gain_first)
    input_gradient = (input_back + hidden_back).astype(jnp.bfloat16)
    (
        gain_one_gradient,
        router_one_gradient,
        query_gradient,
        key_gradient,
        value_gradient,
        output_gradient,
        gain_two_gradient,
        router_two_gradient,
    ) = (
        lax.psum_scatter(
            gain_one_term.astype(jnp.bfloat16), ("shard", "ctx"), scatter_dimension=0, tiled=True
        ).astype(jnp.float32),
        lax.psum_scatter(
            router_one_term.astype(jnp.bfloat16), ("shard", "ctx"), scatter_dimension=0, tiled=True
        ).astype(jnp.float32),
        lax.psum_scatter(
            query_term.astype(jnp.bfloat16), ("shard", "ctx"), scatter_dimension=1, tiled=True
        ).astype(jnp.float32),
        lax.psum_scatter(
            key_term.astype(jnp.bfloat16), ("shard", "ctx"), scatter_dimension=0, tiled=True
        ).astype(jnp.float32),
        lax.psum_scatter(
            value_term.astype(jnp.bfloat16), ("shard", "ctx"), scatter_dimension=0, tiled=True
        ).astype(jnp.float32),
        lax.psum_scatter(
            output_term.astype(jnp.bfloat16), ("shard", "ctx"), scatter_dimension=2, tiled=True
        ).astype(jnp.float32),
        lax.psum_scatter(
            gain_two_term.astype(jnp.bfloat16), ("shard", "ctx"), scatter_dimension=0, tiled=True
        ).astype(jnp.float32),
        lax.psum_scatter(
            router_two_term.astype(jnp.bfloat16), ("shard", "ctx"), scatter_dimension=0, tiled=True
        ).astype(jnp.float32),
    )
    factor = jnp.sqrt(jnp.minimum(1.0, CLIP / peak_all))
    columns = jnp.repeat(factor, head_dim)
    clipped_query = (query_weight.astype(jnp.float32) * columns).astype(jnp.bfloat16)
    clipped_key = (key_weight.astype(jnp.float32) * columns).astype(jnp.bfloat16)
    return (
        output,
        input_gradient,
        gain_one_gradient,
        router_one_gradient,
        query_gradient,
        key_gradient,
        value_gradient,
        output_gradient,
        gain_two_gradient,
        router_two_gradient,
        gate_gradient,
        up_gradient,
        down_gradient,
        clipped_query,
        clipped_key,
    )


def along(value, axis, step):
    count = lax.axis_size(axis)
    if step % count == 0:
        return value
    return lax.ppermute(value, axis, [(place, (place + step) % count) for place in range(count)])


def across(value, bits):
    count = lax.axis_size("tp")
    return lax.ppermute(value, "tp", [(place, place ^ bits) for place in range(count)])


def f32(value):
    return value.astype(jnp.float32)


def bf16(value):
    return value.astype(jnp.bfloat16)


def dot(left, right, contract):
    return lax.dot_general(
        left, right, ((contract[:1], contract[1:]), ((), ())), preferred_element_type=jnp.float32
    )


def gather_tokens(own):
    blocks = []
    for step in range(lax.axis_size("ctx")):
        first = along(own, "ctx", step)
        second = across(first, 2)
        blocks += [first, across(first, 1), second, across(second, 1)]
    return jnp.concatenate(blocks, axis=0)


def scatter_tokens(part):
    steps = lax.axis_size("ctx")
    pieces = part.reshape((steps, 2, 2, part.shape[0] // (4 * steps)) + part.shape[1:])
    total = None
    for step in range(steps - 1, -1, -1):
        piece = pieces[step]
        upper = across(bf16(piece[1, 1]), 1)
        lower = across(bf16(piece[0, 1]), 1)
        high = f32(piece[1, 0]) + f32(upper)
        low = f32(piece[0, 0]) + f32(lower)
        done = low + f32(across(bf16(high), 2))
        if step:
            done = f32(along(bf16(done), "ctx", -step))
        total = done if total is None else total + done
    return total


def scatter_small(part):
    steps = lax.axis_size("ctx")
    half = part[:, :, 0::2] + across(part[:, :, 1::2], 1)
    done = half[:, :, 0] + across(half[:, :, 1], 2)
    return [along(done[:, step], "ctx", -step) for step in range(steps)]


def share_out(own):
    rows = own.shape[0]
    second = across(own, 2)
    blocks = [own, across(own, 1), second, across(second, 1)]
    place = lax.axis_index("tp")
    whole = jnp.zeros((rows * 4, own.shape[1]), own.dtype)
    for bits in range(4):
        whole = lax.dynamic_update_slice(whole, blocks[bits], ((place ^ bits) * rows, 0))
    return whole


def spread_weight(parts, whole, column):
    steps, rows = parts.shape[0], parts.shape[1]
    shards = lax.axis_size("shard")
    here, side = lax.axis_index("ctx"), lax.axis_index("shard")
    for step in range(steps):
        mine = lax.dynamic_index_in_dim(parts, (here + step) % steps, 0, keepdims=False)
        mine = along(mine, "ctx", step)
        source = (here - step) % steps
        for turn in range(shards):
            block = along(mine, "shard", turn)
            row = (((side - turn) % shards) * steps + source) * rows
            whole = lax.dynamic_update_slice(whole, block, (row, column))
    return whole


def return_gradient(term):
    steps, shards = lax.axis_size("ctx"), lax.axis_size("shard")
    rows = term.shape[0] // (steps * shards)
    here, side = lax.axis_index("ctx"), lax.axis_index("shard")
    result = []
    for step in range(steps):
        target = (here + step) % steps
        total = None
        for turn in range(shards):
            row = (((side + turn) % shards) * steps + target) * rows
            piece = lax.dynamic_slice(term, (row, 0), (rows, term.shape[1]))
            piece = f32(along(piece, "shard", turn))
            total = piece if total is None else total + piece
        result.append(along(bf16(total), "ctx", step))
    return result


def in_order(blocks):
    steps = len(blocks)
    here = lax.axis_index("ctx")
    whole = jnp.zeros((steps,) + blocks[0].shape, jnp.float32)
    for step in range(steps):
        whole = lax.dynamic_update_slice(
            whole, f32(blocks[step])[None], ((here - step) % steps,) + (0,) * blocks[0].ndim
        )
    return whole


def attend_kernel(q_ref, k_ref, v_ref, bias_ref, mixed_ref, norm_ref, peak_ref):
    scale = HEAD_DIM ** (-0.5)
    scores = dot(q_ref[...], k_ref[...], (1, 1)) * scale + f32(bias_ref[...])
    peak = jnp.max(scores, axis=-1, keepdims=True)
    weights = jnp.exp(scores - peak)
    total = jnp.sum(weights, axis=-1, keepdims=True)
    mixed_ref[...] = bf16(dot(bf16(weights / total), v_ref[...], (1, 0)))
    norm_ref[...] = jnp.broadcast_to(peak + jnp.log(total), norm_ref.shape)
    peak_ref[...] = jnp.broadcast_to(jnp.max(peak, axis=0, keepdims=True), peak_ref.shape)


def attend_back_kernel(
    q_ref, k_ref, v_ref, bias_ref, norm_ref, back_ref, dq_ref, dk_ref, dv_ref
):
    scale = HEAD_DIM ** (-0.5)

    @pl.when(pl.program_id(0) == 0)
    def _():
        dk_ref[...] = jnp.zeros_like(dk_ref)
        dv_ref[...] = jnp.zeros_like(dv_ref)

    scores = dot(q_ref[...], k_ref[...], (1, 1)) * scale + f32(bias_ref[...])
    chances = jnp.exp(scores - norm_ref[:, :1])
    dv_ref[...] += dot(bf16(chances), back_ref[...], (0, 0))
    share_back = dot(back_ref[...], v_ref[...], (1, 1))
    score_back = bf16(
        chances * (share_back - jnp.sum(chances * share_back, axis=-1, keepdims=True))
    )
    dq_ref[...] = dot(score_back, k_ref[...], (1, 0)) * scale
    dk_ref[...] += dot(score_back, q_ref[...], (0, 0)) * scale


ROWS = 256


def attend(queries, keys, values, bias):
    rows, size = queries.shape
    count = keys.shape[0]
    turns = count // ROWS
    row = pl.BlockSpec((ROWS, size), lambda i: (i, 0))
    whole = pl.BlockSpec((count, size), lambda i: (0, 0))
    return pl.pallas_call(
        attend_kernel,
        grid=(rows // ROWS,),
        in_specs=[row, whole, whole, pl.BlockSpec((ROWS, count), lambda i: (i % turns, 0))],
        out_specs=[row, row, pl.BlockSpec((8, size), lambda i: (i, 0))],
        out_shape=[
            jax.ShapeDtypeStruct((rows, size), jnp.bfloat16),
            jax.ShapeDtypeStruct((rows, size), jnp.float32),
            jax.ShapeDtypeStruct((rows // ROWS * 8, size), jnp.float32),
        ],
        compiler_params=pltpu.CompilerParams(vmem_limit_bytes=48 * 1024 * 1024),
        cost_estimate=pl.CostEstimate(
            flops=4 * rows * count * size,
            bytes_accessed=4 * rows * size * 2 + 2 * count * count * 2,
            transcendentals=rows * count,
        ),
    )(queries, keys, values, bias)


def attend_back(queries, keys, values, bias, norm, back):
    rows, size = queries.shape
    count = keys.shape[0]
    turns = count // ROWS
    row = pl.BlockSpec((ROWS, size), lambda i: (i, 0))
    whole = pl.BlockSpec((count, size), lambda i: (0, 0))
    return pl.pallas_call(
        attend_back_kernel,
        grid=(rows // ROWS,),
        in_specs=[
            row, whole, whole, pl.BlockSpec((ROWS, count), lambda i: (i % turns, 0)), row, row
        ],
        out_specs=[row, whole, whole],
        out_shape=[
            jax.ShapeDtypeStruct((rows, size), jnp.float32),
            jax.ShapeDtypeStruct((count, size), jnp.float32),
            jax.ShapeDtypeStruct((count, size), jnp.float32),
        ],
        compiler_params=pltpu.CompilerParams(vmem_limit_bytes=48 * 1024 * 1024),
        cost_estimate=pl.CostEstimate(
            flops=10 * rows * count * size,
            bytes_accessed=6 * rows * size * 2 + 2 * count * count * 2,
            transcendentals=rows * count,
        ),
    )(queries, keys, values, bias, norm, back)


def pair_gates(logits, routes):
    chosen = []
    for choice in range(TOP):
        chosen.append(
            sum(
                jnp.where(routes[choice] == expert, logits[expert], 0.0)
                for expert in range(logits.shape[0])
            )
        )
    top = jnp.maximum(chosen[0], chosen[1])
    powers = [jnp.exp(item - top) for item in chosen]
    return [power / (powers[0] + powers[1]) for power in powers]


def pair_gates_back(changes, gates, routes, experts):
    mean = gates[0] * changes[0] + gates[1] * changes[1]
    chosen = [gates[choice] * (changes[choice] - mean) for choice in range(TOP)]
    return jnp.stack(
        [
            sum(jnp.where(routes[choice] == expert, chosen[choice], 0.0) for choice in range(TOP))
            for expert in range(experts)
        ]
    )


def swap_halves(value):
    half = value.shape[-1] // 2
    return jnp.concatenate([value[..., half:], value[..., :half]], axis=-1)


def small_gradient(part):
    steps, shards = lax.axis_size("ctx"), lax.axis_size("shard")
    here, side = lax.axis_index("ctx"), lax.axis_index("shard")
    part = part + across(part, 1) + across(part, 2) + across(part, 3)
    pieces = part.reshape(part.shape[0], shards, steps, part.shape[1] // (shards * steps))
    total = None
    for turn in range(shards):
        for step in range(steps):
            piece = lax.dynamic_slice(
                pieces,
                (0, (side + turn) % shards, (here + step) % steps, 0),
                (pieces.shape[0], 1, 1, pieces.shape[3]),
            )[:, 0, 0]
            piece = along(along(piece, "shard", turn), "ctx", step)
            total = piece if total is None else total + piece
    return total


def on_device_fast(
    inputs,
    parents,
    attention_routes,
    expert_routes,
    attention_gain,
    attention_router,
    query_weight,
    key_weight,
    value_weight,
    output_weight,
    expert_gain,
    expert_router,
    gate_weight,
    up_weight,
    down_weight,
    cotangent,
):
    count, width = inputs.shape
    experts, depth_here, local_width = query_weight.shape
    hidden = gate_weight.shape[2]
    steps, shards, tps = lax.axis_size("ctx"), lax.axis_size("shard"), lax.axis_size("tp")
    here, side, place = lax.axis_index("ctx"), lax.axis_index("shard"), lax.axis_index("tp")
    heads = local_width // HEAD_DIM
    rows = count // tps
    tokens = count * steps
    capacity = CAP

    own_inputs = lax.dynamic_slice(inputs, (place * rows, 0), (rows, width))
    all_inputs = gather_tokens(own_inputs)
    small = jnp.concatenate(
        [attention_gain[None], expert_gain[None], attention_router.T, expert_router.T], axis=0
    )
    relative = [along(small, "ctx", step) for step in range(steps)]
    relative = jnp.stack(
        [jnp.stack([along(item, "shard", turn) for item in relative]) for turn in range(shards)]
    )
    side_order = (side - jnp.arange(shards)) % shards
    here_order = (here - jnp.arange(steps)) % steps
    small_all = relative[side_order][:, here_order]
    small_all = small_all.transpose(2, 0, 1, 3).reshape(small.shape[0], width)
    gain_first, gain_second = f32(small_all[0]), f32(small_all[1])
    router_first, router_second = small_all[2 : 2 + experts], small_all[2 + experts :]

    routes = jnp.concatenate([attention_routes.T, expert_routes.T], axis=0)
    bits_order = place ^ jnp.arange(tps)
    routes_here = routes.reshape(2 * TOP, tps, rows)[:, bits_order]
    routes_all = jnp.concatenate(
        [along(routes_here, "ctx", step).reshape(2 * TOP, count) for step in range(steps)], axis=1
    )
    head_routes, expert_routes_all = routes_all[:TOP], routes_all[TOP:]
    own_head_routes = routes_here[:TOP, 0]
    own_expert_routes = routes_here[TOP:, 0]

    query_parts = query_weight.reshape(experts, depth_here, heads, HEAD_DIM)
    query_parts = query_parts.transpose(2, 1, 0, 3).reshape(heads, depth_here, experts * HEAD_DIM)
    key_parts = key_weight.reshape(depth_here, heads, HEAD_DIM).transpose(1, 0, 2)
    value_parts = value_weight.reshape(depth_here, heads, HEAD_DIM).transpose(1, 0, 2)
    project_parts = jnp.concatenate([query_parts, key_parts, value_parts], axis=2)
    output_parts = output_weight.reshape(experts, heads, HEAD_DIM, depth_here)
    output_parts = output_parts.transpose(1, 3, 0, 2).reshape(
        heads, depth_here, experts * HEAD_DIM
    )
    down_parts = down_weight.transpose(0, 2, 1)
    project = spread_weight(
        project_parts, jnp.zeros((width, project_parts.shape[2]), jnp.bfloat16), 0
    )
    outward = spread_weight(
        output_parts, jnp.zeros((width, output_parts.shape[2]), jnp.bfloat16), 0
    )
    gate_up = spread_weight(gate_weight, jnp.zeros((width, 2 * hidden), jnp.bfloat16), 0)
    gate_up = spread_weight(up_weight, gate_up, hidden)
    down = spread_weight(down_parts, jnp.zeros((width, hidden), jnp.bfloat16), 0)
    own_cotangent = lax.dynamic_slice(cotangent, (place * rows, 0), (rows, width))
    all_cotangent = gather_tokens(own_cotangent)

    number = jnp.arange(tokens, dtype=jnp.int32)
    block = number // count
    bits = (number % count) // rows
    token = ((here - block) % steps) * count + (place ^ bits) * rows + number % rows
    unit = token // SEG
    group_units = tokens // SEG
    group_first = side * group_units
    chain = ancestors(parents, group_first + jnp.arange(group_units, dtype=jnp.int32))
    valid = chain >= 0
    depth = jnp.sum(valid[:, 1:].astype(jnp.int32), axis=1, dtype=jnp.int32)
    reached = jnp.any(
        (chain[:, :, None] - group_first == jnp.arange(group_units, dtype=jnp.int32))
        & valid[:, :, None],
        axis=1,
    )
    unit_onehot = (unit[:, None] == jnp.arange(group_units, dtype=jnp.int32)[None, :]).astype(
        jnp.bfloat16
    )
    row_reach = bf16(dot(unit_onehot, reached.astype(jnp.bfloat16), (1, 0)))
    reach = dot(row_reach, unit_onehot, (1, 1))
    allowed = (reach > 0.5) & (
        (unit[:, None] != unit[None, :]) | (token[None, :] <= token[:, None])
    )
    bias = jnp.where(allowed, 0.0, -1e30).astype(jnp.bfloat16)
    token_depth = jnp.sum(
        jnp.where(unit[:, None] == jnp.arange(group_units)[None, :], depth[None, :], 0), axis=1
    )
    cosine, sine = rope_tables(token_depth * SEG + token % SEG, HEAD_DIM // 2)
    cosine = jnp.concatenate([cosine, cosine], axis=1)
    sine = jnp.concatenate([-sine, sine], axis=1)

    normed = bf16(normalize(f32(all_inputs), gain_first))
    head_gates = pair_gates(dot(router_first, normed, (1, 1)), head_routes)
    raw = dot(normed, project, (1, 0))
    chosen_heads = [
        [head_routes[choice][:, None] == expert for expert in range(experts)]
        for choice in range(TOP)
    ]

    def pick(value, choice):
        return sum(
            jnp.where(
                chosen_heads[choice][expert],
                value[:, expert * HEAD_DIM : (expert + 1) * HEAD_DIM],
                0.0,
            )
            for expert in range(experts)
        )

    def place_pair(pair):
        return jnp.concatenate(
            [
                sum(jnp.where(chosen_heads[choice][expert], pair[choice], 0.0) for choice in range(TOP))
                for expert in range(experts)
            ],
            axis=1,
        )

    def turn(value):
        return value * cosine + swap_halves(value) * sine

    def turn_back(value):
        return value * cosine - swap_halves(value) * sine

    inner = experts * HEAD_DIM
    queries = bf16(jnp.concatenate([turn(pick(raw, choice)) for choice in range(TOP)], axis=0))
    keys = bf16(turn(raw[:, inner : inner + HEAD_DIM]))
    values = bf16(raw[:, inner + HEAD_DIM :])
    mixed, norm, peaks = attend(queries, keys, values, bias)
    mixed_pair = [f32(mixed[:tokens]), f32(mixed[tokens:])]
    gated_mixed = bf16(
        place_pair([head_gates[choice][:, None] * mixed_pair[choice] for choice in range(TOP)])
    )
    attention = scatter_tokens(bf16(dot(gated_mixed, outward, (1, 1))))
    hidden_state = f32(own_inputs) + attention
    own_normed_two = bf16(normalize(hidden_state, gain_second))
    normed_two = gather_tokens(own_normed_two)

    expert_gates = pair_gates(dot(router_second, normed_two, (1, 1)), expert_routes_all)
    named = [expert_routes_all[choice] == here for choice in range(TOP)]
    gate_of = sum(jnp.where(named[choice], expert_gates[choice], 0.0) for choice in range(TOP))
    member = (named[0] | named[1]).reshape(steps, count)
    slot = jnp.cumsum(member.astype(jnp.int32), axis=1) - 1
    onehot = (
        (slot[:, None, :] == jnp.arange(capacity, dtype=jnp.int32)[None, :, None])
        & member[:, None, :]
    )
    gate_slot = jnp.sum(
        jnp.where(onehot, gate_of.reshape(steps, 1, count), 0.0), axis=2
    ).reshape(steps * capacity, 1)
    onehot = onehot.astype(jnp.bfloat16)

    def to_slots(value):
        return bf16(
            jnp.einsum(
                "bst,btd->bsd",
                onehot,
                value.reshape(steps, count, width),
                preferred_element_type=jnp.float32,
            )
        ).reshape(steps * capacity, width)

    def from_slots(value):
        return bf16(
            jnp.einsum(
                "bst,bsd->btd",
                onehot,
                value.reshape(steps, capacity, width),
                preferred_element_type=jnp.float32,
            )
        ).reshape(tokens, width)

    slot_rows = to_slots(normed_two)
    slot_upstream = to_slots(all_cotangent)
    both = dot(slot_rows, gate_up, (1, 0))
    gate_pre, up_pre = both[:, :hidden], both[:, hidden:]
    act_raw = dot(slot_upstream, down, (1, 0))
    sigmoid = jax.nn.sigmoid(gate_pre)
    activated = gate_pre * sigmoid * up_pre
    gated_act = bf16(activated * gate_slot)
    gate_back_slot = jnp.sum(activated * act_raw, axis=1)
    act_back = act_raw * gate_slot
    both_back = bf16(
        jnp.concatenate(
            [
                act_back * up_pre * sigmoid * (1.0 + gate_pre * (1.0 - sigmoid)),
                act_back * gate_pre * sigmoid,
            ],
            axis=1,
        )
    )
    rows_back = from_slots(bf16(dot(both_back, gate_up, (1, 1))))
    gate_change = jnp.sum(
        jnp.where(onehot > 0, gate_back_slot.reshape(steps, capacity, 1), 0.0), axis=1
    ).reshape(1, steps, tps, rows)
    normed_two_back = scatter_tokens(rows_back)
    gate_changes = scatter_small(gate_change)
    down_blocks = return_gradient(bf16(dot(slot_upstream, gated_act, (0, 0))))
    gate_up_term = bf16(dot(slot_rows, both_back, (0, 0)))
    gate_blocks = return_gradient(gate_up_term[:, :hidden])
    up_blocks = return_gradient(gate_up_term[:, hidden:])
    feed = scatter_tokens(from_slots(bf16(dot(gated_act, down, (1, 1)))))
    output = share_out(bf16(hidden_state + feed))

    own_expert_gates = pair_gates(dot(router_second, own_normed_two, (1, 1)), own_expert_routes)
    expert_gate_back = [
        sum(
            jnp.where(own_expert_routes[choice] == (here + step) % steps, gate_changes[step][0], 0.0)
            for step in range(steps)
        )
        for choice in range(TOP)
    ]
    expert_logit_back = pair_gates_back(
        expert_gate_back, own_expert_gates, own_expert_routes, experts
    )
    router_second_term = jnp.einsum(
        "et,td->ed", expert_logit_back, f32(own_normed_two), precision=HIGH
    )
    normed_two_back = normed_two_back + jnp.einsum(
        "et,ed->td", expert_logit_back, f32(router_second), precision=HIGH
    )
    hidden_back, gain_second_term = normalize_back(normed_two_back, hidden_state, gain_second)
    hidden_back = hidden_back + f32(own_cotangent)
    second_small = small_gradient(
        jnp.concatenate([gain_second_term[None], router_second_term], axis=0)
    )

    all_back = gather_tokens(bf16(hidden_back))
    raw_back = dot(all_back, outward, (1, 0))
    pair_back = [pick(raw_back, choice) for choice in range(TOP)]
    head_change = jnp.stack(
        [jnp.sum(mixed_pair[choice] * pair_back[choice], axis=1) for choice in range(TOP)]
    )
    mixed_back = bf16(
        jnp.concatenate(
            [head_gates[choice][:, None] * pair_back[choice] for choice in range(TOP)], axis=0
        )
    )
    query_change, key_change, value_change = attend_back(
        queries, keys, values, bias, norm, mixed_back
    )
    change = bf16(
        jnp.concatenate(
            [
                place_pair(
                    [turn_back(query_change[:tokens]), turn_back(query_change[tokens:])]
                ),
                turn_back(f32(bf16(key_change))),
                value_change,
            ],
            axis=1,
        )
    )
    normed_back = scatter_tokens(bf16(dot(change, project, (1, 1))))
    head_changes = scatter_small(head_change.reshape(TOP, steps, tps, rows))
    output_blocks = return_gradient(bf16(dot(all_back, gated_mixed, (0, 0))))
    project_blocks = return_gradient(bf16(dot(normed, change, (0, 0))))
    own_normed = bf16(normalize(f32(own_inputs), gain_first))
    own_head_gates = pair_gates(dot(router_first, own_normed, (1, 1)), own_head_routes)
    head_gate_back = sum(head_changes)
    head_logit_back = pair_gates_back(
        [head_gate_back[choice] for choice in range(TOP)],
        own_head_gates,
        own_head_routes,
        experts,
    )
    router_first_term = jnp.einsum(
        "et,td->ed", head_logit_back, f32(own_normed), precision=HIGH
    )
    normed_back = normed_back + jnp.einsum(
        "et,ed->td", head_logit_back, f32(router_first), precision=HIGH
    )
    input_back, gain_first_term = normalize_back(normed_back, f32(own_inputs), gain_first)
    input_gradient = share_out(bf16(input_back + hidden_back))
    first_small = small_gradient(
        jnp.concatenate([gain_first_term[None], router_first_term], axis=0)
    )

    gate_gradient = in_order(gate_blocks)
    up_gradient = in_order(up_blocks)
    down_gradient = in_order([item.T for item in down_blocks])
    project_all = in_order(project_blocks)
    query_gradient = (
        project_all[:, :, :inner]
        .reshape(heads, depth_here, experts, HEAD_DIM)
        .transpose(2, 1, 0, 3)
        .reshape(experts, depth_here, local_width)
    )
    key_gradient = (
        project_all[:, :, inner : inner + HEAD_DIM].transpose(1, 0, 2).reshape(depth_here, local_width)
    )
    value_gradient = (
        project_all[:, :, inner + HEAD_DIM :].transpose(1, 0, 2).reshape(depth_here, local_width)
    )
    output_gradient = (
        in_order(output_blocks)
        .reshape(heads, depth_here, experts, HEAD_DIM)
        .transpose(2, 0, 3, 1)
        .reshape(experts, local_width, depth_here)
    )

    peak = jnp.max(peaks, axis=0, keepdims=True)
    for turn_by in range(1, shards):
        peak = jnp.maximum(peak, along(peak, "shard", turn_by))
    head_peaks = in_order([along(peak, "ctx", step) for step in range(steps)])
    factor = jnp.sqrt(jnp.minimum(1.0, CLIP / head_peaks)).reshape(local_width)
    clipped_query = bf16(f32(query_weight) * factor)
    clipped_key = bf16(f32(key_weight) * factor)
    return (
        output,
        input_gradient,
        first_small[0],
        first_small[1:].T,
        query_gradient,
        key_gradient,
        value_gradient,
        output_gradient,
        second_small[0],
        second_small[1:].T,
        gate_gradient,
        up_gradient,
        down_gradient,
        clipped_query,
        clipped_key,
    )


def on_device(*arrays):
    experts, _, local_width = arrays[6].shape
    steps = lax.axis_size("ctx")
    tokens = arrays[0].shape[0] * steps
    fits = (
        experts == steps
        and local_width == steps * HEAD_DIM
        and lax.axis_size("tp") == 4
        and tokens % ROWS == 0
    )
    return on_device_fast(*arrays) if fits else on_device_general(*arrays)


def solution(mesh):
    placed = (
        P(("shard", "ctx"), None),
        P(),
        P(("shard", "ctx"), None),
        P(("shard", "ctx"), None),
        P(("shard", "ctx")),
        P(("shard", "ctx"), None),
        P(None, ("shard", "ctx"), "tp"),
        P(("shard", "ctx"), "tp"),
        P(("shard", "ctx"), "tp"),
        P(None, "tp", ("shard", "ctx")),
        P(("shard", "ctx")),
        P(("shard", "ctx"), None),
        P(None, ("shard", "ctx"), "tp"),
        P(None, ("shard", "ctx"), "tp"),
        P(None, "tp", ("shard", "ctx")),
        P(("shard", "ctx"), None),
    )
    return jax.shard_map(
        on_device,
        mesh=mesh,
        in_specs=placed,
        out_specs=(
            P(("shard", "ctx"), None),
            P(("shard", "ctx"), None),
            P(("shard", "ctx")),
            P(("shard", "ctx"), None),
            P(None, ("shard", "ctx"), "tp"),
            P(("shard", "ctx"), "tp"),
            P(("shard", "ctx"), "tp"),
            P(None, "tp", ("shard", "ctx")),
            P(("shard", "ctx")),
            P(("shard", "ctx"), None),
            P(None, ("shard", "ctx"), "tp"),
            P(None, ("shard", "ctx"), "tp"),
            P(None, "tp", ("shard", "ctx")),
            P(None, ("shard", "ctx"), "tp"),
            P(("shard", "ctx"), "tp"),
        ),
        check_vma=False,
    )
```

```python
import jax
import jax.numpy as jnp
from jax import lax
from jax.experimental import pallas as pl
from jax.experimental.pallas import tpu as pltpu
from jax.sharding import PartitionSpec as P

SHARD, CTX, TP = "shard", "ctx", "tp"
BOTH = (SHARD, CTX)
HEAD_DIM = 128
TOP = 2
SEG = 64
PATH = 10
CAP = 176


EPS = 1e-05
ROPE_BASE = 10000.0
CLIP = 2.0
HIGH = lax.Precision.HIGHEST


def normalize(value, gain):
    scale = lax.rsqrt(jnp.mean(value * value, axis=-1, keepdims=True) + EPS)
    return value * scale * gain


def normalize_back(change, value, gain):
    scale = lax.rsqrt(jnp.mean(value * value, axis=-1, keepdims=True) + EPS)
    gain_change = jnp.sum(change * value * scale, axis=0)
    scaled = change * gain
    value_change = scale * scaled - value * scale**3 * jnp.mean(
        scaled * value, axis=-1, keepdims=True
    )
    return (value_change, gain_change)


def gating(normed, router, routes):
    logits = jnp.dot(normed, router, preferred_element_type=jnp.float32)
    chosen = jnp.take_along_axis(logits, routes, axis=1)
    return jax.nn.softmax(chosen, axis=1)


def gating_back(change, gates, routes, experts):
    chosen_change = gates * (change - jnp.sum(gates * change, axis=1, keepdims=True))
    onehot = (routes[:, :, None] == jnp.arange(experts, dtype=jnp.int32)[None, None, :]).astype(
        jnp.float32
    )
    return jnp.sum(chosen_change[:, :, None] * onehot, axis=1)


def slot_tables(routes, experts, capacity):
    number = routes.shape[0] * routes.shape[1]
    flat = routes.reshape(number)
    onehot = (flat[:, None] == jnp.arange(experts, dtype=jnp.int32)[None, :]).astype(jnp.int32)
    before = jnp.cumsum(onehot, axis=0, dtype=jnp.int32) - onehot
    place = jnp.sum(before * onehot, axis=1, dtype=jnp.int32)
    slot_index = flat * capacity + place
    pair_index = (
        jnp.zeros((experts * capacity,), jnp.int32)
        .at[slot_index]
        .set(jnp.arange(number, dtype=jnp.int32))
    )
    filled = jnp.zeros((experts * capacity,), jnp.int32).at[slot_index].set(1)
    return (slot_index, pair_index, filled)


def rope_tables(positions, half):
    frequency = ROPE_BASE ** (-jnp.arange(half, dtype=jnp.float32) / half)
    angle = positions.astype(jnp.float32)[:, None] * frequency[None, :]
    return (jnp.cos(angle), jnp.sin(angle))


def rotate(value, cosine, sine):
    half = value.shape[-1] // 2
    first = value[..., :half]
    second = value[..., half:]
    return jnp.concatenate(
        [first * cosine - second * sine, second * cosine + first * sine], axis=-1
    )


def rotate_back(change, cosine, sine):
    half = change.shape[-1] // 2
    first = change[..., :half]
    second = change[..., half:]
    return jnp.concatenate(
        [first * cosine + second * sine, second * cosine - first * sine], axis=-1
    )


def ancestors(parents, start_units):
    chain = [start_units]
    current = start_units
    for level in range(PATH - 1):
        current = jnp.where(current >= 0, parents[jnp.maximum(current, 0)], -1)
        chain.append(current)
    return jnp.stack(chain, axis=1)


def unit_mask(valid_row):
    token_row = jnp.arange(SEG * TOP) // TOP
    causal = jnp.arange(SEG)[None, :] <= token_row[:, None]
    others = jnp.broadcast_to(valid_row[None, 1:, None], (SEG * TOP, PATH - 1, SEG))
    return jnp.concatenate([causal[:, None, :], others], axis=1).reshape(SEG * TOP, PATH * SEG)


def dispatch(rows, pair_index, filled, choose, experts, capacity):
    picked = rows[pair_index // choose]
    return jnp.where(filled[:, None] > 0, picked, jnp.zeros((), rows.dtype)).reshape(
        experts, capacity, rows.shape[1]
    )


def spread(pairs, pair_index, filled, experts, capacity):
    picked = pairs[pair_index]
    return jnp.where(filled[:, None] > 0, picked, jnp.zeros((), pairs.dtype)).reshape(
        experts, capacity, pairs.shape[1]
    )


def on_device_general(
    inputs,
    parents,
    attention_routes,
    expert_routes,
    attention_gain,
    attention_router,
    query_weight,
    key_weight,
    value_weight,
    output_weight,
    expert_gain,
    expert_router,
    gate_weight,
    up_weight,
    down_weight,
    cotangent,
):
    count = inputs.shape[0]
    width = inputs.shape[1]
    experts = query_weight.shape[0]
    local_width = query_weight.shape[2]
    head_dim = HEAD_DIM
    local_heads = local_width // head_dim
    capacity = CAP
    choose = attention_routes.shape[1]
    segment = SEG
    units_here = count // segment
    group_units = lax.axis_size(CTX) * units_here
    scale = head_dim ** (-0.5)
    gain_one, router_one, query_full, key_full, value_full, output_full, gain_two, router_two = (
        lax.all_gather(attention_gain, BOTH, axis=0, tiled=True),
        lax.all_gather(attention_router, BOTH, axis=0, tiled=True),
        lax.all_gather(query_weight, BOTH, axis=1, tiled=True),
        lax.all_gather(key_weight, BOTH, axis=0, tiled=True),
        lax.all_gather(value_weight, BOTH, axis=0, tiled=True),
        lax.all_gather(output_weight, BOTH, axis=2, tiled=True),
        lax.all_gather(expert_gain, BOTH, axis=0, tiled=True),
        lax.all_gather(expert_router, BOTH, axis=0, tiled=True),
    )
    first_unit = (
        lax.axis_index(SHARD) * lax.axis_size(CTX) + lax.axis_index(CTX)
    ) * units_here
    group_first = lax.axis_index(SHARD) * group_units
    own_units = first_unit + jnp.arange(units_here, dtype=jnp.int32)
    chain = ancestors(parents, own_units)
    valid = chain >= 0
    depth = jnp.sum(valid[:, 1:].astype(jnp.int32), axis=1, dtype=jnp.int32)
    positions = (depth[:, None] * segment + jnp.arange(segment, dtype=jnp.int32)[None, :]).reshape(
        count
    )
    cosine, sine = rope_tables(positions, head_dim // 2)
    local_chain = jnp.clip(chain - group_first, 0, group_units - 1)
    allowed = jax.vmap(unit_mask)(valid)
    residual = inputs.astype(jnp.float32)
    gain_first = gain_one.astype(jnp.float32)
    normed = normalize(residual, gain_first).astype(jnp.bfloat16)
    head_gates = gating(normed, router_one, attention_routes)
    head_slot, head_pair, head_filled = slot_tables(attention_routes, experts, capacity)
    head_rows = dispatch(normed, head_pair, head_filled, choose, experts, capacity)
    query_slots = jnp.einsum(
        "ecd,edf->ecf", head_rows, query_full, preferred_element_type=jnp.float32
    )
    query_pairs = query_slots.reshape(experts * capacity, local_width)[head_slot].reshape(
        count, choose, local_heads, head_dim
    )
    queries = rotate(query_pairs, cosine[:, None, None, :], sine[:, None, None, :]).astype(
        jnp.bfloat16
    )
    key_raw = jnp.dot(normed, key_full, preferred_element_type=jnp.float32).reshape(
        count, local_heads, head_dim
    )
    keys = (
        rotate(key_raw, cosine[:, None, :], sine[:, None, :])
        .astype(jnp.bfloat16)
        .reshape(count, local_width)
    )
    values = jnp.dot(normed, value_full, preferred_element_type=jnp.float32).astype(jnp.bfloat16)
    all_keys, all_values = (
        lax.all_gather(keys, CTX, axis=0, tiled=True),
        lax.all_gather(values, CTX, axis=0, tiled=True),
    )
    path_keys = all_keys.reshape(group_units, segment, local_width)[local_chain].reshape(
        units_here, PATH * segment, local_heads, head_dim
    )
    path_values = all_values.reshape(group_units, segment, local_width)[local_chain].reshape(
        units_here, PATH * segment, local_heads, head_dim
    )
    query_units = queries.reshape(units_here, segment * choose, local_heads, head_dim)
    scores = (
        jnp.einsum("uqhd,ukhd->uhqk", query_units, path_keys, preferred_element_type=jnp.float32)
        * scale
    )
    masked = jnp.where(allowed[:, None], scores, -1e30)
    peak = jnp.max(masked, axis=-1, keepdims=True)
    weights = jnp.where(allowed[:, None], jnp.exp(masked - peak), 0.0)
    total = jnp.sum(weights, axis=-1, keepdims=True)
    log_total = peak + jnp.log(total)
    head_peak = jnp.max(peak[..., 0], axis=(0, 2))
    shares = (weights / total).astype(jnp.bfloat16)
    mixed = (
        jnp.einsum("uhqk,ukhd->uqhd", shares, path_values, preferred_element_type=jnp.float32)
        .astype(jnp.bfloat16)
        .reshape(count * choose, local_width)
    )
    mixed_slots = spread(mixed, head_pair, head_filled, experts, capacity)
    out_slots = jnp.einsum(
        "ecf,efd->ecd", mixed_slots, output_full, preferred_element_type=jnp.float32
    )
    out_pairs = out_slots.reshape(experts * capacity, width)[head_slot].reshape(
        count, choose, width
    )
    attention = lax.psum(jnp.sum(head_gates[:, :, None] * out_pairs, axis=1), TP)
    hidden_state = residual + attention
    peak_all = lax.pmax(head_peak, BOTH)
    gain_second = gain_two.astype(jnp.float32)
    normed_two = normalize(hidden_state, gain_second).astype(jnp.bfloat16)
    expert_gates = gating(normed_two, router_two, expert_routes)
    expert_slot, expert_pair, expert_filled = slot_tables(expert_routes, experts, capacity)
    expert_rows = dispatch(normed_two, expert_pair, expert_filled, choose, experts, capacity)
    gate_full, up_full, down_full = (
        lax.all_gather(gate_weight, BOTH, axis=1, tiled=True),
        lax.all_gather(up_weight, BOTH, axis=1, tiled=True),
        lax.all_gather(down_weight, BOTH, axis=2, tiled=True),
    )
    gate_pre = jnp.einsum(
        "ecd,edf->ecf", expert_rows, gate_full, preferred_element_type=jnp.float32
    )
    up_pre = jnp.einsum("ecd,edf->ecf", expert_rows, up_full, preferred_element_type=jnp.float32)
    activated = (jax.nn.silu(gate_pre) * up_pre).astype(jnp.bfloat16)
    down_slots = jnp.einsum(
        "ecf,efd->ecd", activated, down_full, preferred_element_type=jnp.float32
    )
    down_pairs = down_slots.reshape(experts * capacity, width)[expert_slot].reshape(
        count, choose, width
    )
    feed = lax.psum(
        jnp.sum(expert_gates[:, :, None] * down_pairs, axis=1).astype(jnp.bfloat16), TP
    ).astype(jnp.float32)
    output = (hidden_state + feed).astype(jnp.bfloat16)
    upstream = cotangent.astype(jnp.float32)
    down_back = (
        (expert_gates[:, :, None] * upstream[:, None, :])
        .astype(jnp.bfloat16)
        .reshape(count * choose, width)
    )
    expert_gate_part = jnp.sum(down_pairs * upstream[:, None, :], axis=2)
    down_back_slots = spread(down_back, expert_pair, expert_filled, experts, capacity)
    act_back = jnp.einsum(
        "ecd,efd->ecf", down_back_slots, down_full, preferred_element_type=jnp.float32
    )
    sigmoid = jax.nn.sigmoid(gate_pre)
    gate_back = (act_back * up_pre * sigmoid * (1.0 + gate_pre * (1.0 - sigmoid))).astype(
        jnp.bfloat16
    )
    up_back = (act_back * gate_pre * sigmoid).astype(jnp.bfloat16)
    rows_back = jnp.einsum(
        "ecf,edf->ecd", gate_back, gate_full, preferred_element_type=jnp.float32
    ) + jnp.einsum("ecf,edf->ecd", up_back, up_full, preferred_element_type=jnp.float32)
    normed_two_part = jnp.sum(
        rows_back.reshape(experts * capacity, width)[expert_slot].reshape(count, choose, width),
        axis=1,
    )
    collected = []
    for expert in range(experts):
        gate_term = jnp.einsum(
            "cd,cf->df", expert_rows[expert], gate_back[expert], preferred_element_type=jnp.float32
        )
        up_term = jnp.einsum(
            "cd,cf->df", expert_rows[expert], up_back[expert], preferred_element_type=jnp.float32
        )
        down_term = jnp.einsum(
            "cf,cd->fd",
            activated[expert],
            down_back_slots[expert],
            preferred_element_type=jnp.float32,
        )
        collected.append(
            (
                lax.psum_scatter(
                    gate_term.astype(jnp.bfloat16),
                    BOTH,
                    scatter_dimension=0,
                    tiled=True,
                ).astype(jnp.float32),
                lax.psum_scatter(
                    up_term.astype(jnp.bfloat16), BOTH, scatter_dimension=0, tiled=True
                ).astype(jnp.float32),
                lax.psum_scatter(
                    down_term.astype(jnp.bfloat16),
                    BOTH,
                    scatter_dimension=1,
                    tiled=True,
                ).astype(jnp.float32),
            )
        )
    gate_gradient = jnp.stack([item[0] for item in collected])
    up_gradient = jnp.stack([item[1] for item in collected])
    down_gradient = jnp.stack([item[2] for item in collected])
    normed_two_back, expert_gate_back = lax.psum((normed_two_part, expert_gate_part), TP)
    expert_logit_back = gating_back(expert_gate_back, expert_gates, expert_routes, experts)
    router_two_term = jnp.einsum(
        "td,te->de", normed_two.astype(jnp.float32), expert_logit_back, precision=HIGH
    )
    normed_two_back = normed_two_back + jnp.einsum(
        "te,de->td", expert_logit_back, router_two.astype(jnp.float32), precision=HIGH
    )
    hidden_back, gain_two_term = normalize_back(normed_two_back, hidden_state, gain_second)
    hidden_back = hidden_back + upstream
    head_back = (
        (head_gates[:, :, None] * hidden_back[:, None, :])
        .astype(jnp.bfloat16)
        .reshape(count * choose, width)
    )
    head_gate_part = jnp.sum(out_pairs * hidden_back[:, None, :], axis=2)
    head_back_slots = spread(head_back, head_pair, head_filled, experts, capacity)
    output_term = jnp.einsum(
        "ecf,ecd->efd", mixed_slots, head_back_slots, preferred_element_type=jnp.float32
    )
    mixed_back_slots = jnp.einsum(
        "ecd,efd->ecf", head_back_slots, output_full, preferred_element_type=jnp.float32
    )
    mixed_back = (
        mixed_back_slots.reshape(experts * capacity, local_width)[head_slot]
        .astype(jnp.bfloat16)
        .reshape(units_here, segment * choose, local_heads, head_dim)
    )
    again = (
        jnp.einsum("uqhd,ukhd->uhqk", query_units, path_keys, preferred_element_type=jnp.float32)
        * scale
    )
    chances = jnp.where(allowed[:, None], jnp.exp(again - log_total), 0.0)
    value_path_back = jnp.einsum(
        "uhqk,uqhd->ukhd",
        chances.astype(jnp.bfloat16),
        mixed_back,
        preferred_element_type=jnp.float32,
    )
    share_back = jnp.einsum(
        "uqhd,ukhd->uhqk", mixed_back, path_values, preferred_element_type=jnp.float32
    )
    score_back = (
        chances * (share_back - jnp.sum(chances * share_back, axis=-1, keepdims=True))
    ).astype(jnp.bfloat16)
    query_back_raw = (
        jnp.einsum("uhqk,ukhd->uqhd", score_back, path_keys, preferred_element_type=jnp.float32)
        * scale
    )
    key_path_back = (
        jnp.einsum("uhqk,uqhd->ukhd", score_back, query_units, preferred_element_type=jnp.float32)
        * scale
    )
    owner = (
        (local_chain[:, :, None] == jnp.arange(group_units, dtype=jnp.int32)[None, None, :])
        & valid[:, :, None]
    ).astype(jnp.float32)
    key_group = jnp.einsum(
        "upg,upsc->gsc",
        owner,
        key_path_back.reshape(units_here, PATH, segment, local_width),
        precision=HIGH,
    )
    value_group = jnp.einsum(
        "upg,upsc->gsc",
        owner,
        value_path_back.reshape(units_here, PATH, segment, local_width),
        precision=HIGH,
    )
    key_mine, value_mine = (
        lax.psum_scatter(
            key_group.reshape(group_units * segment, local_width).astype(jnp.bfloat16),
            CTX,
            scatter_dimension=0,
            tiled=True,
        ).astype(jnp.float32),
        lax.psum_scatter(
            value_group.reshape(group_units * segment, local_width).astype(jnp.bfloat16),
            CTX,
            scatter_dimension=0,
            tiled=True,
        ).astype(jnp.float32),
    )
    key_back = (
        rotate_back(
            key_mine.reshape(count, local_heads, head_dim), cosine[:, None, :], sine[:, None, :]
        )
        .astype(jnp.bfloat16)
        .reshape(count, local_width)
    )
    value_back = value_mine.astype(jnp.bfloat16)
    query_back = (
        rotate_back(
            query_back_raw.reshape(count, choose, local_heads, head_dim),
            cosine[:, None, None, :],
            sine[:, None, None, :],
        )
        .astype(jnp.bfloat16)
        .reshape(count * choose, local_width)
    )
    query_back_slots = spread(query_back, head_pair, head_filled, experts, capacity)
    query_term = jnp.einsum(
        "ecd,ecf->edf", head_rows, query_back_slots, preferred_element_type=jnp.float32
    )
    key_term = jnp.einsum("td,tf->df", normed, key_back, preferred_element_type=jnp.float32)
    value_term = jnp.einsum("td,tf->df", normed, value_back, preferred_element_type=jnp.float32)
    query_rows_back = jnp.einsum(
        "ecf,edf->ecd", query_back_slots, query_full, preferred_element_type=jnp.float32
    )
    normed_part = jnp.sum(
        query_rows_back.reshape(experts * capacity, width)[head_slot].reshape(count, choose, width),
        axis=1,
    )
    normed_part = (
        normed_part
        + jnp.einsum("tf,df->td", key_back, key_full, preferred_element_type=jnp.float32)
        + jnp.einsum("tf,df->td", value_back, value_full, preferred_element_type=jnp.float32)
    )
    normed_back, head_gate_back = (
        lax.psum(normed_part.astype(jnp.bfloat16), TP).astype(jnp.float32),
        lax.psum(head_gate_part.astype(jnp.bfloat16), TP).astype(jnp.float32),
    )
    head_logit_back = gating_back(head_gate_back, head_gates, attention_routes, experts)
    router_one_term = jnp.einsum(
        "td,te->de", normed.astype(jnp.float32), head_logit_back, precision=HIGH
    )
    normed_back = normed_back + jnp.einsum(
        "te,de->td", head_logit_back, router_one.astype(jnp.float32), precision=HIGH
    )
    input_back, gain_one_term = normalize_back(normed_back, residual, gain_first)
    input_gradient = (input_back + hidden_back).astype(jnp.bfloat16)
    (
        gain_one_gradient,
        router_one_gradient,
        query_gradient,
        key_gradient,
        value_gradient,
        output_gradient,
        gain_two_gradient,
        router_two_gradient,
    ) = (
        lax.psum_scatter(
            gain_one_term.astype(jnp.bfloat16), BOTH, scatter_dimension=0, tiled=True
        ).astype(jnp.float32),
        lax.psum_scatter(
            router_one_term.astype(jnp.bfloat16), BOTH, scatter_dimension=0, tiled=True
        ).astype(jnp.float32),
        lax.psum_scatter(
            query_term.astype(jnp.bfloat16), BOTH, scatter_dimension=1, tiled=True
        ).astype(jnp.float32),
        lax.psum_scatter(
            key_term.astype(jnp.bfloat16), BOTH, scatter_dimension=0, tiled=True
        ).astype(jnp.float32),
        lax.psum_scatter(
            value_term.astype(jnp.bfloat16), BOTH, scatter_dimension=0, tiled=True
        ).astype(jnp.float32),
        lax.psum_scatter(
            output_term.astype(jnp.bfloat16), BOTH, scatter_dimension=2, tiled=True
        ).astype(jnp.float32),
        lax.psum_scatter(
            gain_two_term.astype(jnp.bfloat16), BOTH, scatter_dimension=0, tiled=True
        ).astype(jnp.float32),
        lax.psum_scatter(
            router_two_term.astype(jnp.bfloat16), BOTH, scatter_dimension=0, tiled=True
        ).astype(jnp.float32),
    )
    factor = jnp.sqrt(jnp.minimum(1.0, CLIP / peak_all))
    columns = jnp.repeat(factor, head_dim)
    clipped_query = (query_weight.astype(jnp.float32) * columns).astype(jnp.bfloat16)
    clipped_key = (key_weight.astype(jnp.float32) * columns).astype(jnp.bfloat16)
    return (
        output,
        input_gradient,
        gain_one_gradient,
        router_one_gradient,
        query_gradient,
        key_gradient,
        value_gradient,
        output_gradient,
        gain_two_gradient,
        router_two_gradient,
        gate_gradient,
        up_gradient,
        down_gradient,
        clipped_query,
        clipped_key,
    )


def along(value, axis, step):
    count = lax.axis_size(axis)
    if step % count == 0:
        return value
    return lax.ppermute(value, axis, [(place, (place + step) % count) for place in range(count)])


def across(value, bits):
    count = lax.axis_size(TP)
    return lax.ppermute(value, TP, [(place, place ^ bits) for place in range(count)])


def f32(value):
    return value.astype(jnp.float32)


def bf16(value):
    return value.astype(jnp.bfloat16)


def dot(left, right, contract):
    return lax.dot_general(
        left, right, ((contract[:1], contract[1:]), ((), ())), preferred_element_type=jnp.float32
    )


def either(bit, zero, one):
    return jnp.where(bit == 0, zero, one)


def tp_bits():
    place = lax.axis_index(TP)
    return place % 2, place // 2


def in_columns(own, other, far, both):
    low, high = tp_bits()
    first, second = either(low, own, other), either(low, other, own)
    third, fourth = either(low, far, both), either(low, both, far)
    return jnp.concatenate(
        [
            either(high, first, third),
            either(high, second, fourth),
            either(high, third, first),
            either(high, fourth, second),
        ],
        axis=1,
    )


def from_ctx(blocks):
    return [along(block, CTX, step) for step, block in enumerate(blocks)]


def gather_pairs(near):
    far = [across(block, 2) for block in near]

    def stacked(items):
        steps, rows = len(items), items[0].shape[0]
        whole = jnp.zeros((steps * rows, items[0].shape[1]), items[0].dtype)
        for step, item in enumerate(items):
            row = ((lax.axis_index(CTX) - step) % steps) * rows
            whole = lax.dynamic_update_slice(whole, item, (row, 0))
        return whole

    return stacked(near), stacked(far)


def gather_columns(near):
    own, far = gather_pairs(near)
    return in_columns(own, across(own, 1), far, across(far, 1))


def gather_dense(own):
    whole = lax.all_gather(own, (TP, CTX), axis=0, tiled=True)
    tps = lax.axis_size(TP)
    whole = whole.reshape(tps, whole.shape[0] // tps, own.shape[1])
    return jnp.concatenate([whole[index] for index in range(tps)], axis=1)


def outward_kernel(left_ref, right_ref, out_ref):
    out_ref[0] = bf16(dot(left_ref[...], right_ref[...], (1, 1)))


def by_quarter(left, right):
    tps = lax.axis_size(TP)
    count, depth = left.shape
    size = right.shape[0] // tps
    return pl.pallas_call(
        outward_kernel,
        grid=(tps, count // ROWS),
        in_specs=[
            pl.BlockSpec((ROWS, depth), lambda q, i: (i, 0)),
            pl.BlockSpec((size, depth), lambda q, i: (q, 0)),
        ],
        out_specs=pl.BlockSpec((1, ROWS, size), lambda q, i: (q, i, 0)),
        out_shape=jax.ShapeDtypeStruct((tps, count, size), jnp.bfloat16),
        compiler_params=pltpu.CompilerParams(vmem_limit_bytes=32 * 1024 * 1024),
        cost_estimate=pl.CostEstimate(
            flops=2 * count * depth * right.shape[0],
            bytes_accessed=2 * (tps * count * depth + right.size + count * right.shape[0]),
            transcendentals=0,
        ),
    )(left, right)


def scatter_dense(left, right):
    part = by_quarter(left, right)
    part = part.reshape(-1, part.shape[2])
    return f32(lax.psum_scatter(part, (TP, CTX), scatter_dimension=0, tiled=True))


def scatter_columns(part):
    steps = lax.axis_size(CTX)
    low, high = tp_bits()
    size = part.shape[1] // 4
    quarter = [part[:, index * size : (index + 1) * size] for index in range(4)]
    sent = jnp.concatenate(
        [either(low, quarter[1], quarter[0]), either(low, quarter[3], quarter[2])], axis=1
    )
    came = across(sent, 1)
    first = f32(either(low, quarter[0], quarter[1])) + f32(came[:, :size])
    second = f32(either(low, quarter[2], quarter[3])) + f32(came[:, size:])
    kept = bf16(either(high, first, second))
    sent = bf16(either(high, second, first))
    rows = part.shape[0] // steps
    result = [None] * steps
    for step in list(range(1, steps)) + [0]:
        row = ((lax.axis_index(CTX) - step) % steps) * rows
        own, other = [lax.dynamic_slice_in_dim(item, row, rows, axis=0) for item in (kept, sent)]
        done = bf16(f32(own) + f32(across(other, 2)))
        result[step] = along(done, CTX, -step)
    return result


def tp_sum(part):
    return part + across(part, 1) + across(part, 2) + across(part, 3)


def share_out(own):
    return in_columns(own, across(own, 1), across(own, 2), across(own, 3))


def tie(*values):
    return lax.optimization_barrier(values)


def after(value, *others):
    return lax.optimization_barrier((value, *others))[0]


def by_place(blocks):
    order = (lax.axis_index(CTX) - jnp.arange(len(blocks))) % len(blocks)
    return jnp.stack(blocks)[order]


def exchange(parts):
    return lax.all_to_all(parts, CTX, 0, 0)


def swap(value):
    return lax.ppermute(value, SHARD, [(0, 1), (1, 0)])


def joined(near, far):
    first = lax.axis_index(SHARD) == 0
    return jnp.concatenate([jnp.where(first, near, far), jnp.where(first, far, near)], axis=0)


def halves(value):
    half = value.shape[1] // 2
    side = lax.axis_index(SHARD)
    return (
        lax.dynamic_slice_in_dim(value, side * half, half, axis=1),
        lax.dynamic_slice_in_dim(value, (1 - side) * half, half, axis=1),
    )


def far_gradient(rows, change):
    return bf16(dot(halves(rows)[1], change, (0, 0)))


def near_gradient(rows, change, arrived):
    total = bf16(dot(halves(rows)[0], change, (0, 0)) + f32(arrived))
    steps = lax.axis_size(CTX)
    return total.reshape(steps, total.shape[0] // steps, total.shape[1])


def attend_kernel(q_ref, k_ref, v_ref, bias_ref, mixed_ref, norm_ref, peak_ref):
    scale = HEAD_DIM ** (-0.5)
    scores = dot(q_ref[...], k_ref[...], (1, 1)) * scale + f32(bias_ref[...])
    peak = jnp.max(scores, axis=-1, keepdims=True)
    weights = jnp.exp(scores - peak)
    total = jnp.sum(weights, axis=-1, keepdims=True)
    mixed_ref[...] = bf16(dot(bf16(weights / total), v_ref[...], (1, 0)))
    norm_ref[...] = jnp.broadcast_to(peak + jnp.log(total), norm_ref.shape)
    peak_ref[...] = jnp.broadcast_to(jnp.max(peak, axis=0, keepdims=True), peak_ref.shape)


def attend_back_kernel(
    q_ref, k_ref, v_ref, bias_ref, norm_ref, back_ref, dq_ref, dk_ref, dv_ref
):
    scale = HEAD_DIM ** (-0.5)

    @pl.when(pl.program_id(0) == 0)
    def _():
        dk_ref[...] = jnp.zeros_like(dk_ref)
        dv_ref[...] = jnp.zeros_like(dv_ref)

    scores = dot(q_ref[...], k_ref[...], (1, 1)) * scale + f32(bias_ref[...])
    chances = jnp.exp(scores - norm_ref[:, :1])
    dv_ref[...] += dot(bf16(chances), back_ref[...], (0, 0))
    share_back = dot(back_ref[...], v_ref[...], (1, 1))
    score_back = bf16(
        chances * (share_back - jnp.sum(chances * share_back, axis=-1, keepdims=True))
    )
    dq_ref[...] = dot(score_back, k_ref[...], (1, 0)) * scale
    dk_ref[...] += dot(score_back, q_ref[...], (0, 0)) * scale


ROWS = 256


def attend(queries, keys, values, bias):
    rows, size = queries.shape
    count = keys.shape[0]
    turns = count // ROWS
    row = pl.BlockSpec((ROWS, size), lambda i: (i, 0))
    whole = pl.BlockSpec((count, size), lambda i: (0, 0))
    return pl.pallas_call(
        attend_kernel,
        grid=(rows // ROWS,),
        in_specs=[row, whole, whole, pl.BlockSpec((ROWS, count), lambda i: (i % turns, 0))],
        out_specs=[row, row, pl.BlockSpec((8, size), lambda i: (i, 0))],
        out_shape=[
            jax.ShapeDtypeStruct((rows, size), jnp.bfloat16),
            jax.ShapeDtypeStruct((rows, size), jnp.float32),
            jax.ShapeDtypeStruct((rows // ROWS * 8, size), jnp.float32),
        ],
        compiler_params=pltpu.CompilerParams(vmem_limit_bytes=48 * 1024 * 1024),
        cost_estimate=pl.CostEstimate(
            flops=4 * rows * count * size,
            bytes_accessed=4 * rows * size * 2 + 2 * count * count * 2,
            transcendentals=rows * count,
        ),
    )(queries, keys, values, bias)


def attend_back(queries, keys, values, bias, norm, back):
    rows, size = queries.shape
    count = keys.shape[0]
    turns = count // ROWS
    row = pl.BlockSpec((ROWS, size), lambda i: (i, 0))
    whole = pl.BlockSpec((count, size), lambda i: (0, 0))
    return pl.pallas_call(
        attend_back_kernel,
        grid=(rows // ROWS,),
        in_specs=[
            row, whole, whole, pl.BlockSpec((ROWS, count), lambda i: (i % turns, 0)), row, row
        ],
        out_specs=[row, whole, whole],
        out_shape=[
            jax.ShapeDtypeStruct((rows, size), jnp.float32),
            jax.ShapeDtypeStruct((count, size), jnp.float32),
            jax.ShapeDtypeStruct((count, size), jnp.float32),
        ],
        compiler_params=pltpu.CompilerParams(vmem_limit_bytes=48 * 1024 * 1024),
        cost_estimate=pl.CostEstimate(
            flops=10 * rows * count * size,
            bytes_accessed=6 * rows * size * 2 + 2 * count * count * 2,
            transcendentals=rows * count,
        ),
    )(queries, keys, values, bias, norm, back)


def pair_gates(logits, routes):
    chosen = []
    for choice in range(TOP):
        chosen.append(
            sum(
                jnp.where(routes[choice] == expert, logits[expert], 0.0)
                for expert in range(logits.shape[0])
            )
        )
    top = jnp.maximum(chosen[0], chosen[1])
    powers = [jnp.exp(item - top) for item in chosen]
    return [power / (powers[0] + powers[1]) for power in powers]


def pair_gates_back(changes, gates, routes, experts):
    mean = gates[0] * changes[0] + gates[1] * changes[1]
    chosen = [gates[choice] * (changes[choice] - mean) for choice in range(TOP)]
    return jnp.stack(
        [
            sum(jnp.where(routes[choice] == expert, chosen[choice], 0.0) for choice in range(TOP))
            for expert in range(experts)
        ]
    )


def swap_halves(value):
    half = value.shape[-1] // 2
    return jnp.concatenate([value[..., half:], value[..., :half]], axis=-1)


def small_gradient(part, extra):
    steps = lax.axis_size(CTX)
    here, side = lax.axis_index(CTX), lax.axis_index(SHARD)
    whole = jnp.concatenate([share_out(part), extra], axis=0)
    half = whole.shape[1] // 2
    whole = either(side, whole[:, :half], whole[:, half:]) + swap(
        either(side, whole[:, half:], whole[:, :half])
    )
    pieces = whole.reshape(whole.shape[0], steps, half // steps).transpose(1, 0, 2)
    return sum(
        along(
            lax.dynamic_index_in_dim(pieces, (here + step) % steps, 0, keepdims=False), CTX, step
        )
        for step in range(steps)
    )


def on_device_fast(
    inputs,
    parents,
    attention_routes,
    expert_routes,
    attention_gain,
    attention_router,
    query_weight,
    key_weight,
    value_weight,
    output_weight,
    expert_gain,
    expert_router,
    gate_weight,
    up_weight,
    down_weight,
    cotangent,
):
    count, width = inputs.shape
    experts, depth_here, local_width = query_weight.shape
    hidden = gate_weight.shape[2]
    steps, shards, tps = lax.axis_size(CTX), lax.axis_size(SHARD), lax.axis_size(TP)
    here, side, place = lax.axis_index(CTX), lax.axis_index(SHARD), lax.axis_index(TP)
    heads = local_width // HEAD_DIM
    rows, quarter = count // tps, width // tps
    tokens = count * steps
    slots = -(-CAP // 64) * 64

    def own_columns(value):
        return lax.dynamic_slice_in_dim(value, place * quarter, quarter, axis=value.ndim - 1)

    own_inputs = own_columns(inputs)
    def gather_rows(value):
        value = lax.dynamic_slice_in_dim(value, place * rows, rows, axis=0)
        return lax.all_gather(value, (CTX, TP), axis=0, tiled=True)

    all_inputs = gather_rows(inputs)
    small = jnp.concatenate(
        [attention_gain[None], expert_gain[None], attention_router.T, expert_router.T], axis=0
    )
    routes = jnp.concatenate([attention_routes.T, expert_routes.T], axis=0)
    packed = jnp.zeros((small.shape[0] + 2 * TOP, max(count, depth_here)), jnp.bfloat16)
    packed = lax.dynamic_update_slice(packed, small, (0, 0))
    packed = lax.dynamic_update_slice(packed, bf16(routes), (small.shape[0], 0))
    packed_near = [along(packed, CTX, step) for step in range(steps)]
    packed_all = by_place(packed_near)
    routes_all = packed_all[:, small.shape[0] :, :count].transpose(1, 0, 2).astype(jnp.int32)
    head_routes = routes_all[:TOP].reshape(TOP, tokens)
    own_head_routes, own_expert_routes = routes[:TOP], routes[TOP:]
    small_near = packed_all[:, : small.shape[0], :depth_here].transpose(1, 0, 2)
    small_near = small_near.reshape(small.shape[0], steps * depth_here).T
    small_all = joined(small_near, swap(small_near)).T
    gain_first, gain_second = f32(small_all[0]), f32(small_all[1])
    router_first, router_second = small_all[2 : 2 + experts], small_all[2 + experts :]
    own_small = f32(own_columns(small_all))
    own_gain_first, own_gain_second = own_small[0], own_small[1]
    own_router_first, own_router_second = own_small[2 : 2 + experts], own_small[2 + experts :]

    def rows_of(value):
        return value.reshape(-1, value.shape[2])

    def project_parts(query, key, value):
        query = query.reshape(experts, depth_here, heads, HEAD_DIM).transpose(2, 1, 0, 3)
        key, value = [
            item.reshape(depth_here, heads, HEAD_DIM).transpose(1, 0, 2) for item in (key, value)
        ]
        query = query.reshape(heads, depth_here, experts * HEAD_DIM)
        return jnp.concatenate([query, key, value], axis=2)

    def output_parts(weight):
        weight = weight.reshape(experts, heads, HEAD_DIM, depth_here).transpose(1, 3, 0, 2)
        return weight.reshape(heads, depth_here, experts * HEAD_DIM)

    nears = [exchange(project_parts(query_weight, key_weight, value_weight))]
    weight, nears[0] = tie(output_weight, nears[0])
    fars = [swap(nears[0])]
    nears.append(exchange(output_parts(weight)))
    weight, nears[1] = tie(gate_weight, nears[1])
    nears.append(exchange(weight))
    project = joined(rows_of(nears[0]), rows_of(fars[0]))
    own_upstream = own_columns(cotangent)

    target = (here + jnp.arange(steps, dtype=jnp.int32)) % steps
    named = own_expert_routes[None] == target[:, None, None]
    member = named[:, 0] | named[:, 1]
    slot = jnp.cumsum(member.astype(jnp.int32), axis=1) - 1
    onehot = (slot[:, None, :] == jnp.arange(slots, dtype=jnp.int32)[None, :, None]) & member[
        :, None, :
    ]
    onehot_all = onehot.astype(jnp.bfloat16).reshape(steps * slots, count)

    def picked_slots(value):
        picked = bf16(dot(onehot_all, value, (1, 0)))
        return from_ctx([picked[step * slots : (step + 1) * slots] for step in range(steps)])

    def from_slots(value):
        return dot(onehot_all, jnp.concatenate(scatter_columns(value), axis=0), (0, 0))

    chosen = (routes_all[TOP] == here) | (routes_all[TOP + 1] == here)
    chosen_slot = jnp.cumsum(chosen.astype(jnp.int32), axis=1) - 1
    chosen_onehot = (
        chosen_slot[:, None, :] == jnp.arange(slots, dtype=jnp.int32)[None, :, None]
    ) & chosen[:, None, :]

    token = jnp.arange(tokens, dtype=jnp.int32)
    unit = token // SEG
    group_units = tokens // SEG
    group_first = side * group_units
    parents, all_inputs = tie(parents, all_inputs)
    chain = ancestors(parents, group_first + jnp.arange(group_units, dtype=jnp.int32))
    valid = chain >= 0
    depth = jnp.sum(valid[:, 1:].astype(jnp.int32), axis=1, dtype=jnp.int32)
    reached = jnp.any(
        (chain[:, :, None] - group_first == jnp.arange(group_units, dtype=jnp.int32))
        & valid[:, :, None],
        axis=1,
    )
    unit_onehot = (unit[:, None] == jnp.arange(group_units, dtype=jnp.int32)[None, :]).astype(
        jnp.bfloat16
    )
    row_reach = bf16(dot(unit_onehot, reached.astype(jnp.bfloat16), (1, 0)))
    reach = dot(row_reach, unit_onehot, (1, 1))
    allowed = (reach > 0.5) & (
        (unit[:, None] != unit[None, :]) | (token[None, :] <= token[:, None])
    )
    bias = jnp.where(allowed, 0.0, -1e30).astype(jnp.bfloat16)
    token_depth = jnp.sum(
        jnp.where(unit[:, None] == jnp.arange(group_units)[None, :], depth[None, :], 0), axis=1
    )
    cosine, sine = rope_tables(token_depth * SEG + token % SEG, HEAD_DIM // 2)
    cosine = jnp.concatenate([cosine, cosine], axis=1)
    sine = jnp.concatenate([-sine, sine], axis=1)

    normed = bf16(normalize(f32(all_inputs), gain_first))
    head_gates = pair_gates(dot(router_first, normed, (1, 1)), head_routes)
    raw = dot(normed, project, (1, 0))
    nears[1], raw = tie(nears[1], raw)
    fars.append(swap(nears[1]))
    outward = joined(rows_of(nears[1]), rows_of(fars[1]))
    chosen_heads = [
        [head_routes[choice][:, None] == expert for expert in range(experts)]
        for choice in range(TOP)
    ]

    def pick(value, choice):
        return sum(
            jnp.where(
                chosen_heads[choice][expert],
                value[:, expert * HEAD_DIM : (expert + 1) * HEAD_DIM],
                0.0,
            )
            for expert in range(experts)
        )

    def place_pair(pair):
        return jnp.concatenate(
            [
                sum(jnp.where(chosen_heads[choice][expert], pair[choice], 0.0) for choice in range(TOP))
                for expert in range(experts)
            ],
            axis=1,
        )

    def turn(value):
        return value * cosine + swap_halves(value) * sine

    def turn_back(value):
        return value * cosine - swap_halves(value) * sine

    inner = experts * HEAD_DIM
    queries = bf16(jnp.concatenate([turn(pick(raw, choice)) for choice in range(TOP)], axis=0))
    keys = bf16(turn(raw[:, inner : inner + HEAD_DIM]))
    values = bf16(raw[:, inner + HEAD_DIM :])
    mixed, norm, peaks = attend(queries, keys, values, bias)
    mixed_pair = [f32(mixed[:tokens]), f32(mixed[tokens:])]
    gated_mixed = bf16(
        place_pair([head_gates[choice][:, None] * mixed_pair[choice] for choice in range(TOP)])
    )
    weight, nears[2] = tie(up_weight, nears[2])
    fars.append(swap(nears[2]))
    nears.append(exchange(weight))
    attention, nears[3], fars[2] = tie(scatter_dense(gated_mixed, outward), nears[3], fars[2])
    fars.append(swap(nears[3]))
    down_parts = after(down_weight, nears[3]).transpose(0, 2, 1)
    half = depth_here // 2
    down_near = [exchange(down_parts[:, :half])]
    down_far = [swap(down_near[0])]
    hidden_state = f32(own_inputs) + attention
    statistics = tp_sum(
        jnp.concatenate(
            [
                jnp.sum(hidden_state * hidden_state, axis=1)[None],
                jnp.einsum(
                    "td,ed->et", hidden_state * own_gain_second, own_router_second, precision=HIGH
                ),
            ],
            axis=0,
        )
    )
    norm_two = lax.rsqrt(statistics[0] / width + EPS)
    expert_gates = pair_gates(statistics[1:] * norm_two, own_expert_routes)
    own_normed_two = bf16(hidden_state * norm_two[:, None] * own_gain_second)
    gate_of = jnp.where(named[:, 0], expert_gates[0], 0.0) + jnp.where(
        named[:, 1], expert_gates[1], 0.0
    )
    gate_sent = jnp.sum(jnp.where(onehot, gate_of[:, None, :], 0.0), axis=2)
    gate_slot = by_place(from_ctx([gate_sent[step : step + 1] for step in range(steps)]))
    gate_slot = gate_slot.reshape(steps * slots, 1)
    row_blocks = picked_slots(own_normed_two)
    down_near.append(exchange(after(down_parts, *row_blocks)[:, half:]))
    down_far.append(swap(down_near[1]))
    slot_rows, down_near[0] = tie(gather_columns(row_blocks), down_near[0])
    down_near[1], gate_slot = tie(down_near[1], gate_slot)
    all_cotangent = gather_rows(after(cotangent, *row_blocks))
    slot_upstream = bf16(
        jnp.einsum(
            "bst,btd->bsd",
            chosen_onehot.astype(jnp.bfloat16),
            all_cotangent.reshape(steps, count, width),
            preferred_element_type=jnp.float32,
        )
    ).reshape(steps * slots, width)

    def whole(index):
        return joined(rows_of(nears[index]), rows_of(fars[index]))

    gate, up = whole(2), whole(3)
    down = joined(
        rows_of(jnp.concatenate(down_near, axis=1)), rows_of(jnp.concatenate(down_far, axis=1))
    )
    gate_pre = dot(slot_rows, gate, (1, 0))
    up_pre = dot(slot_rows, up, (1, 0))
    act_raw = dot(slot_upstream, down, (1, 0))
    sigmoid = jax.nn.sigmoid(gate_pre)
    activated = gate_pre * sigmoid * up_pre
    gated_act = bf16(activated * gate_slot)
    gate_back_slot = jnp.sum(activated * act_raw, axis=1, keepdims=True)
    act_back = act_raw * gate_slot
    gate_back = bf16(act_back * up_pre * sigmoid * (1.0 + gate_pre * (1.0 - sigmoid)))
    up_back = bf16(act_back * gate_pre * sigmoid)
    pairs = [(slot_upstream, gated_act), (slot_rows, gate_back), (slot_rows, up_back)]
    far_terms = [far_gradient(*pair) for pair in pairs]
    arrived = [swap(term) for term in far_terms]
    rows_back = bf16(
        dot(after(gate_back, *far_terms), gate, (1, 1)) + dot(up_back, up, (1, 1))
    )
    fed = bf16(dot(gated_act, down, (1, 1)))
    gate_sums = tp_sum(after(gate_back_slot, rows_back).reshape(steps, slots))
    gate_sums = jnp.concatenate(
        [
            along(lax.dynamic_slice_in_dim(gate_sums, (here - step) % steps, 1), CTX, -step)
            for step in range(steps)
        ]
    )
    gate_changes = jnp.sum(jnp.where(onehot, gate_sums[:, :, None], 0.0), axis=1)
    normed_two_back, ready = tie(
        from_slots(rows_back), near_gradient(*pairs[0], arrived[0])
    )

    expert_gate_back = [
        sum(
            jnp.where(named[step, choice], gate_changes[step], 0.0) for step in range(steps)
        )
        for choice in range(TOP)
    ]
    expert_logit_back = pair_gates_back(
        expert_gate_back, expert_gates, own_expert_routes, experts
    )
    router_second_term = jnp.einsum(
        "et,td->ed", expert_logit_back, f32(own_normed_two), precision=HIGH
    )
    normed_two_back = normed_two_back + jnp.einsum(
        "et,ed->td", expert_logit_back, own_router_second, precision=HIGH
    )
    scaled = normed_two_back * own_gain_second
    mean = tp_sum(jnp.sum(scaled * hidden_state, axis=1)[None])[0] / width
    gain_second_term = jnp.sum(normed_two_back * hidden_state * norm_two[:, None], axis=0)
    hidden_back = (
        f32(own_upstream)
        + norm_two[:, None] * scaled
        - hidden_state * (norm_two**3 * mean)[:, None]
    )

    down_back = exchange(ready)
    all_back, gate_ready = tie(
        gather_dense(bf16(hidden_back)),
        near_gradient(slot_rows, after(gate_back, hidden_back), arrived[1]),
    )
    raw_back = dot(all_back, outward, (1, 0))
    pair_back = [pick(raw_back, choice) for choice in range(TOP)]
    head_change = jnp.stack(
        [jnp.sum(mixed_pair[choice] * pair_back[choice], axis=1) for choice in range(TOP)]
    )
    head_sums = tp_sum(head_change).reshape(TOP, steps, count).transpose(1, 0, 2)
    head_gate_back = sum(
        along(
            lax.dynamic_index_in_dim(head_sums, (here - step) % steps, 0, keepdims=False),
            CTX,
            -step,
        )
        for step in range(steps)
    )
    mixed_back = bf16(
        jnp.concatenate(
            [head_gates[choice][:, None] * pair_back[choice] for choice in range(TOP)], axis=0
        )
    )
    mixed_back, down_back = tie(mixed_back, down_back)
    gate_returned = [exchange(after(gate_ready, down_back)[:, :half])]
    query_change, key_change, value_change = attend_back(
        queries, keys, values, bias, norm, mixed_back
    )
    change = bf16(
        jnp.concatenate(
            [
                place_pair(
                    [turn_back(query_change[:tokens]), turn_back(query_change[tokens:])]
                ),
                turn_back(f32(bf16(key_change))),
                value_change,
            ],
            axis=1,
        )
    )
    change, head_gate_back, arrived[2], gate_returned[0] = tie(
        change, head_gate_back, arrived[2], gate_returned[0]
    )
    feed = from_slots(after(fed, change))
    gate_returned.append(exchange(after(gate_ready, gate_returned[0])[:, half:]))
    up_ready = near_gradient(slot_rows, after(up_back, change), arrived[2])
    pairs += [(all_back, gated_mixed), (normed, change)]
    arrived += [swap(far_gradient(*pair)) for pair in pairs[3:]]
    up_returned = exchange(after(up_ready, gate_returned[1]))
    normed_back, feed, output_ready, project_ready, gate_returned[1], up_returned = tie(
        scatter_dense(change, project),
        feed,
        near_gradient(*pairs[3], arrived[3]),
        near_gradient(*pairs[4], arrived[4]),
        gate_returned[1],
        up_returned,
    )
    output = share_out(bf16(hidden_state + feed))
    output_all = exchange(output_ready)
    project_all = exchange(after(project_ready, output_all))
    output_all, project_all = f32(output_all), f32(project_all)
    down_gradient = f32(down_back.transpose(0, 2, 1))
    gate_gradient = f32(jnp.concatenate(gate_returned, axis=1))
    up_gradient = f32(up_returned)
    own_rows = f32(inputs)
    norm_one = lax.rsqrt(jnp.mean(own_rows * own_rows, axis=1) + EPS)
    own_values = f32(own_inputs)
    own_normed = bf16(own_values * norm_one[:, None] * own_gain_first)
    own_head_gates = [
        lax.dynamic_slice_in_dim(gate_item, here * count, count, axis=0)
        for gate_item in head_gates
    ]
    head_logit_back = pair_gates_back(
        [head_gate_back[choice] for choice in range(TOP)],
        own_head_gates,
        own_head_routes,
        experts,
    )
    router_first_term = jnp.einsum(
        "et,td->ed", head_logit_back, f32(own_normed), precision=HIGH
    )
    normed_back = normed_back + jnp.einsum(
        "et,ed->td", head_logit_back, own_router_first, precision=HIGH
    )
    scaled = normed_back * own_gain_first
    mean = tp_sum(jnp.sum(scaled * own_values, axis=1)[None])[0] / width
    gain_first_term = jnp.sum(normed_back * own_values * norm_one[:, None], axis=0)
    input_gradient = share_out(
        bf16(
            hidden_back
            + norm_one[:, None] * scaled
            - own_values * (norm_one**3 * mean)[:, None]
        )
    )
    small_sums = small_gradient(
        jnp.concatenate(
            [
                gain_first_term[None],
                gain_second_term[None],
                router_first_term,
                router_second_term,
            ],
            axis=0,
        ),
        jnp.where(
            jnp.arange(width)[None] % depth_here == side * steps + here, jnp.max(peaks), 0.0
        ),
    )

    query_gradient = (
        project_all[:, :, :inner]
        .reshape(heads, depth_here, experts, HEAD_DIM)
        .transpose(2, 1, 0, 3)
        .reshape(experts, depth_here, local_width)
    )
    key_gradient = (
        project_all[:, :, inner : inner + HEAD_DIM].transpose(1, 0, 2).reshape(depth_here, local_width)
    )
    value_gradient = (
        project_all[:, :, inner + HEAD_DIM :].transpose(1, 0, 2).reshape(depth_here, local_width)
    )
    output_gradient = (
        f32(output_all)
        .reshape(heads, depth_here, experts, HEAD_DIM)
        .transpose(2, 0, 3, 1)
        .reshape(experts, local_width, depth_here)
    )

    head_peaks = jnp.max(
        small_sums[-1, : shards * steps].reshape(shards, steps), axis=0
    )
    factor = jnp.repeat(jnp.sqrt(jnp.minimum(1.0, CLIP / head_peaks)), HEAD_DIM)
    clipped_query = bf16(f32(query_weight) * factor)
    clipped_key = bf16(f32(key_weight) * factor)
    return (
        output,
        input_gradient,
        small_sums[0],
        small_sums[2 : 2 + experts].T,
        query_gradient,
        key_gradient,
        value_gradient,
        output_gradient,
        small_sums[1],
        small_sums[2 + experts : 2 + 2 * experts].T,
        gate_gradient,
        up_gradient,
        down_gradient,
        clipped_query,
        clipped_key,
    )


def on_device(*arrays):
    experts, _, local_width = arrays[6].shape
    steps = lax.axis_size(CTX)
    tokens = arrays[0].shape[0] * steps
    fits = (
        experts == steps
        and local_width == steps * HEAD_DIM
        and lax.axis_size(TP) == 4
        and lax.axis_size(SHARD) == 2
        and tokens % ROWS == 0
    )
    return on_device_fast(*arrays) if fits else on_device_general(*arrays)


def solution(mesh):
    placed = (
        P(BOTH, None),
        P(),
        P(BOTH, None),
        P(BOTH, None),
        P(BOTH),
        P(BOTH, None),
        P(None, BOTH, TP),
        P(BOTH, TP),
        P(BOTH, TP),
        P(None, TP, BOTH),
        P(BOTH),
        P(BOTH, None),
        P(None, BOTH, TP),
        P(None, BOTH, TP),
        P(None, TP, BOTH),
        P(BOTH, None),
    )
    return jax.shard_map(
        on_device,
        mesh=mesh,
        in_specs=placed,
        out_specs=(
            P(BOTH, None),
            P(BOTH, None),
            P(BOTH),
            P(BOTH, None),
            P(None, BOTH, TP),
            P(BOTH, TP),
            P(BOTH, TP),
            P(None, TP, BOTH),
            P(BOTH),
            P(BOTH, None),
            P(None, BOTH, TP),
            P(None, BOTH, TP),
            P(None, TP, BOTH),
            P(None, BOTH, TP),
            P(BOTH, TP),
        ),
        check_vma=False,
    )
```

```python
import jax
import jax.numpy as jnp
from jax import lax
from jax.experimental import pallas as pl
from jax.experimental.pallas import tpu as pltpu
from jax.sharding import PartitionSpec as P

SHARD, CTX, TP = "shard", "ctx", "tp"
BOTH = (SHARD, CTX)
HEAD_DIM = 128
TOP = 2
SEG = 64
PATH = 10
CAP = 176


EPS = 1e-05
ROPE_BASE = 10000.0
CLIP = 2.0
HIGH = lax.Precision.HIGHEST


def normalize(value, gain):
    scale = lax.rsqrt(jnp.mean(value * value, axis=-1, keepdims=True) + EPS)
    return value * scale * gain


def normalize_back(change, value, gain):
    scale = lax.rsqrt(jnp.mean(value * value, axis=-1, keepdims=True) + EPS)
    gain_change = jnp.sum(change * value * scale, axis=0)
    scaled = change * gain
    value_change = scale * scaled - value * scale**3 * jnp.mean(
        scaled * value, axis=-1, keepdims=True
    )
    return (value_change, gain_change)


def gating(normed, router, routes):
    logits = jnp.dot(normed, router, preferred_element_type=jnp.float32)
    chosen = jnp.take_along_axis(logits, routes, axis=1)
    return jax.nn.softmax(chosen, axis=1)


def gating_back(change, gates, routes, experts):
    chosen_change = gates * (change - jnp.sum(gates * change, axis=1, keepdims=True))
    onehot = (routes[:, :, None] == jnp.arange(experts, dtype=jnp.int32)[None, None, :]).astype(
        jnp.float32
    )
    return jnp.sum(chosen_change[:, :, None] * onehot, axis=1)


def slot_tables(routes, experts, capacity):
    number = routes.shape[0] * routes.shape[1]
    flat = routes.reshape(number)
    onehot = (flat[:, None] == jnp.arange(experts, dtype=jnp.int32)[None, :]).astype(jnp.int32)
    before = jnp.cumsum(onehot, axis=0, dtype=jnp.int32) - onehot
    place = jnp.sum(before * onehot, axis=1, dtype=jnp.int32)
    slot_index = flat * capacity + place
    pair_index = (
        jnp.zeros((experts * capacity,), jnp.int32)
        .at[slot_index]
        .set(jnp.arange(number, dtype=jnp.int32))
    )
    filled = jnp.zeros((experts * capacity,), jnp.int32).at[slot_index].set(1)
    return (slot_index, pair_index, filled)


def rope_tables(positions, half):
    frequency = ROPE_BASE ** (-jnp.arange(half, dtype=jnp.float32) / half)
    angle = positions.astype(jnp.float32)[:, None] * frequency[None, :]
    return (jnp.cos(angle), jnp.sin(angle))


def rotate(value, cosine, sine):
    half = value.shape[-1] // 2
    first = value[..., :half]
    second = value[..., half:]
    return jnp.concatenate(
        [first * cosine - second * sine, second * cosine + first * sine], axis=-1
    )


def rotate_back(change, cosine, sine):
    half = change.shape[-1] // 2
    first = change[..., :half]
    second = change[..., half:]
    return jnp.concatenate(
        [first * cosine + second * sine, second * cosine - first * sine], axis=-1
    )


def ancestors(parents, start_units):
    chain = [start_units]
    current = start_units
    for level in range(PATH - 1):
        current = jnp.where(current >= 0, parents[jnp.maximum(current, 0)], -1)
        chain.append(current)
    return jnp.stack(chain, axis=1)


def unit_mask(valid_row):
    token_row = jnp.arange(SEG * TOP) // TOP
    causal = jnp.arange(SEG)[None, :] <= token_row[:, None]
    others = jnp.broadcast_to(valid_row[None, 1:, None], (SEG * TOP, PATH - 1, SEG))
    return jnp.concatenate([causal[:, None, :], others], axis=1).reshape(SEG * TOP, PATH * SEG)


def dispatch(rows, pair_index, filled, choose, experts, capacity):
    picked = rows[pair_index // choose]
    return jnp.where(filled[:, None] > 0, picked, jnp.zeros((), rows.dtype)).reshape(
        experts, capacity, rows.shape[1]
    )


def spread(pairs, pair_index, filled, experts, capacity):
    picked = pairs[pair_index]
    return jnp.where(filled[:, None] > 0, picked, jnp.zeros((), pairs.dtype)).reshape(
        experts, capacity, pairs.shape[1]
    )


def on_device_general(
    inputs,
    parents,
    attention_routes,
    expert_routes,
    attention_gain,
    attention_router,
    query_weight,
    key_weight,
    value_weight,
    output_weight,
    expert_gain,
    expert_router,
    gate_weight,
    up_weight,
    down_weight,
    cotangent,
):
    count = inputs.shape[0]
    width = inputs.shape[1]
    experts = query_weight.shape[0]
    local_width = query_weight.shape[2]
    head_dim = HEAD_DIM
    local_heads = local_width // head_dim
    capacity = CAP
    choose = attention_routes.shape[1]
    segment = SEG
    units_here = count // segment
    group_units = lax.axis_size(CTX) * units_here
    scale = head_dim ** (-0.5)
    gain_one, router_one, query_full, key_full, value_full, output_full, gain_two, router_two = (
        lax.all_gather(attention_gain, BOTH, axis=0, tiled=True),
        lax.all_gather(attention_router, BOTH, axis=0, tiled=True),
        lax.all_gather(query_weight, BOTH, axis=1, tiled=True),
        lax.all_gather(key_weight, BOTH, axis=0, tiled=True),
        lax.all_gather(value_weight, BOTH, axis=0, tiled=True),
        lax.all_gather(output_weight, BOTH, axis=2, tiled=True),
        lax.all_gather(expert_gain, BOTH, axis=0, tiled=True),
        lax.all_gather(expert_router, BOTH, axis=0, tiled=True),
    )
    first_unit = (
        lax.axis_index(SHARD) * lax.axis_size(CTX) + lax.axis_index(CTX)
    ) * units_here
    group_first = lax.axis_index(SHARD) * group_units
    own_units = first_unit + jnp.arange(units_here, dtype=jnp.int32)
    chain = ancestors(parents, own_units)
    valid = chain >= 0
    depth = jnp.sum(valid[:, 1:].astype(jnp.int32), axis=1, dtype=jnp.int32)
    positions = (depth[:, None] * segment + jnp.arange(segment, dtype=jnp.int32)[None, :]).reshape(
        count
    )
    cosine, sine = rope_tables(positions, head_dim // 2)
    local_chain = jnp.clip(chain - group_first, 0, group_units - 1)
    allowed = jax.vmap(unit_mask)(valid)
    residual = inputs.astype(jnp.float32)
    gain_first = gain_one.astype(jnp.float32)
    normed = normalize(residual, gain_first).astype(jnp.bfloat16)
    head_gates = gating(normed, router_one, attention_routes)
    head_slot, head_pair, head_filled = slot_tables(attention_routes, experts, capacity)
    head_rows = dispatch(normed, head_pair, head_filled, choose, experts, capacity)
    query_slots = jnp.einsum(
        "ecd,edf->ecf", head_rows, query_full, preferred_element_type=jnp.float32
    )
    query_pairs = query_slots.reshape(experts * capacity, local_width)[head_slot].reshape(
        count, choose, local_heads, head_dim
    )
    queries = rotate(query_pairs, cosine[:, None, None, :], sine[:, None, None, :]).astype(
        jnp.bfloat16
    )
    key_raw = jnp.dot(normed, key_full, preferred_element_type=jnp.float32).reshape(
        count, local_heads, head_dim
    )
    keys = (
        rotate(key_raw, cosine[:, None, :], sine[:, None, :])
        .astype(jnp.bfloat16)
        .reshape(count, local_width)
    )
    values = jnp.dot(normed, value_full, preferred_element_type=jnp.float32).astype(jnp.bfloat16)
    all_keys, all_values = (
        lax.all_gather(keys, CTX, axis=0, tiled=True),
        lax.all_gather(values, CTX, axis=0, tiled=True),
    )
    path_keys = all_keys.reshape(group_units, segment, local_width)[local_chain].reshape(
        units_here, PATH * segment, local_heads, head_dim
    )
    path_values = all_values.reshape(group_units, segment, local_width)[local_chain].reshape(
        units_here, PATH * segment, local_heads, head_dim
    )
    query_units = queries.reshape(units_here, segment * choose, local_heads, head_dim)
    scores = (
        jnp.einsum("uqhd,ukhd->uhqk", query_units, path_keys, preferred_element_type=jnp.float32)
        * scale
    )
    masked = jnp.where(allowed[:, None], scores, -1e30)
    peak = jnp.max(masked, axis=-1, keepdims=True)
    weights = jnp.where(allowed[:, None], jnp.exp(masked - peak), 0.0)
    total = jnp.sum(weights, axis=-1, keepdims=True)
    log_total = peak + jnp.log(total)
    head_peak = jnp.max(peak[..., 0], axis=(0, 2))
    shares = (weights / total).astype(jnp.bfloat16)
    mixed = (
        jnp.einsum("uhqk,ukhd->uqhd", shares, path_values, preferred_element_type=jnp.float32)
        .astype(jnp.bfloat16)
        .reshape(count * choose, local_width)
    )
    mixed_slots = spread(mixed, head_pair, head_filled, experts, capacity)
    out_slots = jnp.einsum(
        "ecf,efd->ecd", mixed_slots, output_full, preferred_element_type=jnp.float32
    )
    out_pairs = out_slots.reshape(experts * capacity, width)[head_slot].reshape(
        count, choose, width
    )
    attention = lax.psum(jnp.sum(head_gates[:, :, None] * out_pairs, axis=1), TP)
    hidden_state = residual + attention
    peak_all = lax.pmax(head_peak, BOTH)
    gain_second = gain_two.astype(jnp.float32)
    normed_two = normalize(hidden_state, gain_second).astype(jnp.bfloat16)
    expert_gates = gating(normed_two, router_two, expert_routes)
    expert_slot, expert_pair, expert_filled = slot_tables(expert_routes, experts, capacity)
    expert_rows = dispatch(normed_two, expert_pair, expert_filled, choose, experts, capacity)
    gate_full, up_full, down_full = (
        lax.all_gather(gate_weight, BOTH, axis=1, tiled=True),
        lax.all_gather(up_weight, BOTH, axis=1, tiled=True),
        lax.all_gather(down_weight, BOTH, axis=2, tiled=True),
    )
    gate_pre = jnp.einsum(
        "ecd,edf->ecf", expert_rows, gate_full, preferred_element_type=jnp.float32
    )
    up_pre = jnp.einsum("ecd,edf->ecf", expert_rows, up_full, preferred_element_type=jnp.float32)
    activated = (jax.nn.silu(gate_pre) * up_pre).astype(jnp.bfloat16)
    down_slots = jnp.einsum(
        "ecf,efd->ecd", activated, down_full, preferred_element_type=jnp.float32
    )
    down_pairs = down_slots.reshape(experts * capacity, width)[expert_slot].reshape(
        count, choose, width
    )
    feed = lax.psum(
        jnp.sum(expert_gates[:, :, None] * down_pairs, axis=1).astype(jnp.bfloat16), TP
    ).astype(jnp.float32)
    output = (hidden_state + feed).astype(jnp.bfloat16)
    upstream = cotangent.astype(jnp.float32)
    down_back = (
        (expert_gates[:, :, None] * upstream[:, None, :])
        .astype(jnp.bfloat16)
        .reshape(count * choose, width)
    )
    expert_gate_part = jnp.sum(down_pairs * upstream[:, None, :], axis=2)
    down_back_slots = spread(down_back, expert_pair, expert_filled, experts, capacity)
    act_back = jnp.einsum(
        "ecd,efd->ecf", down_back_slots, down_full, preferred_element_type=jnp.float32
    )
    sigmoid = jax.nn.sigmoid(gate_pre)
    gate_back = (act_back * up_pre * sigmoid * (1.0 + gate_pre * (1.0 - sigmoid))).astype(
        jnp.bfloat16
    )
    up_back = (act_back * gate_pre * sigmoid).astype(jnp.bfloat16)
    rows_back = jnp.einsum(
        "ecf,edf->ecd", gate_back, gate_full, preferred_element_type=jnp.float32
    ) + jnp.einsum("ecf,edf->ecd", up_back, up_full, preferred_element_type=jnp.float32)
    normed_two_part = jnp.sum(
        rows_back.reshape(experts * capacity, width)[expert_slot].reshape(count, choose, width),
        axis=1,
    )
    collected = []
    for expert in range(experts):
        gate_term = jnp.einsum(
            "cd,cf->df", expert_rows[expert], gate_back[expert], preferred_element_type=jnp.float32
        )
        up_term = jnp.einsum(
            "cd,cf->df", expert_rows[expert], up_back[expert], preferred_element_type=jnp.float32
        )
        down_term = jnp.einsum(
            "cf,cd->fd",
            activated[expert],
            down_back_slots[expert],
            preferred_element_type=jnp.float32,
        )
        collected.append(
            (
                lax.psum_scatter(
                    gate_term.astype(jnp.bfloat16),
                    BOTH,
                    scatter_dimension=0,
                    tiled=True,
                ).astype(jnp.float32),
                lax.psum_scatter(
                    up_term.astype(jnp.bfloat16), BOTH, scatter_dimension=0, tiled=True
                ).astype(jnp.float32),
                lax.psum_scatter(
                    down_term.astype(jnp.bfloat16),
                    BOTH,
                    scatter_dimension=1,
                    tiled=True,
                ).astype(jnp.float32),
            )
        )
    gate_gradient = jnp.stack([item[0] for item in collected])
    up_gradient = jnp.stack([item[1] for item in collected])
    down_gradient = jnp.stack([item[2] for item in collected])
    normed_two_back, expert_gate_back = lax.psum((normed_two_part, expert_gate_part), TP)
    expert_logit_back = gating_back(expert_gate_back, expert_gates, expert_routes, experts)
    router_two_term = jnp.einsum(
        "td,te->de", normed_two.astype(jnp.float32), expert_logit_back, precision=HIGH
    )
    normed_two_back = normed_two_back + jnp.einsum(
        "te,de->td", expert_logit_back, router_two.astype(jnp.float32), precision=HIGH
    )
    hidden_back, gain_two_term = normalize_back(normed_two_back, hidden_state, gain_second)
    hidden_back = hidden_back + upstream
    head_back = (
        (head_gates[:, :, None] * hidden_back[:, None, :])
        .astype(jnp.bfloat16)
        .reshape(count * choose, width)
    )
    head_gate_part = jnp.sum(out_pairs * hidden_back[:, None, :], axis=2)
    head_back_slots = spread(head_back, head_pair, head_filled, experts, capacity)
    output_term = jnp.einsum(
        "ecf,ecd->efd", mixed_slots, head_back_slots, preferred_element_type=jnp.float32
    )
    mixed_back_slots = jnp.einsum(
        "ecd,efd->ecf", head_back_slots, output_full, preferred_element_type=jnp.float32
    )
    mixed_back = (
        mixed_back_slots.reshape(experts * capacity, local_width)[head_slot]
        .astype(jnp.bfloat16)
        .reshape(units_here, segment * choose, local_heads, head_dim)
    )
    again = (
        jnp.einsum("uqhd,ukhd->uhqk", query_units, path_keys, preferred_element_type=jnp.float32)
        * scale
    )
    chances = jnp.where(allowed[:, None], jnp.exp(again - log_total), 0.0)
    value_path_back = jnp.einsum(
        "uhqk,uqhd->ukhd",
        chances.astype(jnp.bfloat16),
        mixed_back,
        preferred_element_type=jnp.float32,
    )
    share_back = jnp.einsum(
        "uqhd,ukhd->uhqk", mixed_back, path_values, preferred_element_type=jnp.float32
    )
    score_back = (
        chances * (share_back - jnp.sum(chances * share_back, axis=-1, keepdims=True))
    ).astype(jnp.bfloat16)
    query_back_raw = (
        jnp.einsum("uhqk,ukhd->uqhd", score_back, path_keys, preferred_element_type=jnp.float32)
        * scale
    )
    key_path_back = (
        jnp.einsum("uhqk,uqhd->ukhd", score_back, query_units, preferred_element_type=jnp.float32)
        * scale
    )
    owner = (
        (local_chain[:, :, None] == jnp.arange(group_units, dtype=jnp.int32)[None, None, :])
        & valid[:, :, None]
    ).astype(jnp.float32)
    key_group = jnp.einsum(
        "upg,upsc->gsc",
        owner,
        key_path_back.reshape(units_here, PATH, segment, local_width),
        precision=HIGH,
    )
    value_group = jnp.einsum(
        "upg,upsc->gsc",
        owner,
        value_path_back.reshape(units_here, PATH, segment, local_width),
        precision=HIGH,
    )
    key_mine, value_mine = (
        lax.psum_scatter(
            key_group.reshape(group_units * segment, local_width).astype(jnp.bfloat16),
            CTX,
            scatter_dimension=0,
            tiled=True,
        ).astype(jnp.float32),
        lax.psum_scatter(
            value_group.reshape(group_units * segment, local_width).astype(jnp.bfloat16),
            CTX,
            scatter_dimension=0,
            tiled=True,
        ).astype(jnp.float32),
    )
    key_back = (
        rotate_back(
            key_mine.reshape(count, local_heads, head_dim), cosine[:, None, :], sine[:, None, :]
        )
        .astype(jnp.bfloat16)
        .reshape(count, local_width)
    )
    value_back = value_mine.astype(jnp.bfloat16)
    query_back = (
        rotate_back(
            query_back_raw.reshape(count, choose, local_heads, head_dim),
            cosine[:, None, None, :],
            sine[:, None, None, :],
        )
        .astype(jnp.bfloat16)
        .reshape(count * choose, local_width)
    )
    query_back_slots = spread(query_back, head_pair, head_filled, experts, capacity)
    query_term = jnp.einsum(
        "ecd,ecf->edf", head_rows, query_back_slots, preferred_element_type=jnp.float32
    )
    key_term = jnp.einsum("td,tf->df", normed, key_back, preferred_element_type=jnp.float32)
    value_term = jnp.einsum("td,tf->df", normed, value_back, preferred_element_type=jnp.float32)
    query_rows_back = jnp.einsum(
        "ecf,edf->ecd", query_back_slots, query_full, preferred_element_type=jnp.float32
    )
    normed_part = jnp.sum(
        query_rows_back.reshape(experts * capacity, width)[head_slot].reshape(count, choose, width),
        axis=1,
    )
    normed_part = (
        normed_part
        + jnp.einsum("tf,df->td", key_back, key_full, preferred_element_type=jnp.float32)
        + jnp.einsum("tf,df->td", value_back, value_full, preferred_element_type=jnp.float32)
    )
    normed_back, head_gate_back = (
        lax.psum(normed_part.astype(jnp.bfloat16), TP).astype(jnp.float32),
        lax.psum(head_gate_part.astype(jnp.bfloat16), TP).astype(jnp.float32),
    )
    head_logit_back = gating_back(head_gate_back, head_gates, attention_routes, experts)
    router_one_term = jnp.einsum(
        "td,te->de", normed.astype(jnp.float32), head_logit_back, precision=HIGH
    )
    normed_back = normed_back + jnp.einsum(
        "te,de->td", head_logit_back, router_one.astype(jnp.float32), precision=HIGH
    )
    input_back, gain_one_term = normalize_back(normed_back, residual, gain_first)
    input_gradient = (input_back + hidden_back).astype(jnp.bfloat16)
    (
        gain_one_gradient,
        router_one_gradient,
        query_gradient,
        key_gradient,
        value_gradient,
        output_gradient,
        gain_two_gradient,
        router_two_gradient,
    ) = (
        lax.psum_scatter(
            gain_one_term.astype(jnp.bfloat16), BOTH, scatter_dimension=0, tiled=True
        ).astype(jnp.float32),
        lax.psum_scatter(
            router_one_term.astype(jnp.bfloat16), BOTH, scatter_dimension=0, tiled=True
        ).astype(jnp.float32),
        lax.psum_scatter(
            query_term.astype(jnp.bfloat16), BOTH, scatter_dimension=1, tiled=True
        ).astype(jnp.float32),
        lax.psum_scatter(
            key_term.astype(jnp.bfloat16), BOTH, scatter_dimension=0, tiled=True
        ).astype(jnp.float32),
        lax.psum_scatter(
            value_term.astype(jnp.bfloat16), BOTH, scatter_dimension=0, tiled=True
        ).astype(jnp.float32),
        lax.psum_scatter(
            output_term.astype(jnp.bfloat16), BOTH, scatter_dimension=2, tiled=True
        ).astype(jnp.float32),
        lax.psum_scatter(
            gain_two_term.astype(jnp.bfloat16), BOTH, scatter_dimension=0, tiled=True
        ).astype(jnp.float32),
        lax.psum_scatter(
            router_two_term.astype(jnp.bfloat16), BOTH, scatter_dimension=0, tiled=True
        ).astype(jnp.float32),
    )
    factor = jnp.sqrt(jnp.minimum(1.0, CLIP / peak_all))
    columns = jnp.repeat(factor, head_dim)
    clipped_query = (query_weight.astype(jnp.float32) * columns).astype(jnp.bfloat16)
    clipped_key = (key_weight.astype(jnp.float32) * columns).astype(jnp.bfloat16)
    return (
        output,
        input_gradient,
        gain_one_gradient,
        router_one_gradient,
        query_gradient,
        key_gradient,
        value_gradient,
        output_gradient,
        gain_two_gradient,
        router_two_gradient,
        gate_gradient,
        up_gradient,
        down_gradient,
        clipped_query,
        clipped_key,
    )


def along(value, axis, step):
    count = lax.axis_size(axis)
    if step % count == 0:
        return value
    return lax.ppermute(value, axis, [(place, (place + step) % count) for place in range(count)])


def across(value, bits):
    count = lax.axis_size(TP)
    return lax.ppermute(value, TP, [(place, place ^ bits) for place in range(count)])


def f32(value):
    return value.astype(jnp.float32)


def bf16(value):
    return value.astype(jnp.bfloat16)


def dot(left, right, contract):
    return lax.dot_general(
        left, right, ((contract[:1], contract[1:]), ((), ())), preferred_element_type=jnp.float32
    )


def either(bit, zero, one):
    return jnp.where(bit == 0, zero, one)


def tp_bits():
    place = lax.axis_index(TP)
    return place % 2, place // 2


def in_columns(own, other, far, both):
    low, high = tp_bits()
    first, second = either(low, own, other), either(low, other, own)
    third, fourth = either(low, far, both), either(low, both, far)
    return jnp.concatenate(
        [
            either(high, first, third),
            either(high, second, fourth),
            either(high, third, first),
            either(high, fourth, second),
        ],
        axis=1,
    )


def from_ctx(blocks):
    return [along(block, CTX, step) for step, block in enumerate(blocks)]


def gather_pairs(near):
    far = [across(block, 2) for block in near]

    def stacked(items):
        steps, rows = len(items), items[0].shape[0]
        whole = jnp.zeros((steps * rows, items[0].shape[1]), items[0].dtype)
        for step, item in enumerate(items):
            row = ((lax.axis_index(CTX) - step) % steps) * rows
            whole = lax.dynamic_update_slice(whole, item, (row, 0))
        return whole

    return stacked(near), stacked(far)


def gather_columns(near):
    own, far = gather_pairs(near)
    return in_columns(own, across(own, 1), far, across(far, 1))


def gather_dense(own):
    whole = lax.all_gather(own, (TP, CTX), axis=0, tiled=True)
    tps = lax.axis_size(TP)
    whole = whole.reshape(tps, whole.shape[0] // tps, own.shape[1])
    return jnp.concatenate([whole[index] for index in range(tps)], axis=1)


def outward_kernel(left_ref, right_ref, out_ref):
    out_ref[0] = bf16(dot(left_ref[...], right_ref[...], (1, 1)))


def by_quarter(left, right):
    tps = lax.axis_size(TP)
    count, depth = left.shape
    size = right.shape[0] // tps
    return pl.pallas_call(
        outward_kernel,
        grid=(tps,),
        in_specs=[
            pl.BlockSpec((count, depth), lambda q: (0, 0)),
            pl.BlockSpec((size, depth), lambda q: (q, 0)),
        ],
        out_specs=pl.BlockSpec((1, count, size), lambda q: (q, 0, 0)),
        out_shape=jax.ShapeDtypeStruct((tps, count, size), jnp.bfloat16),
        compiler_params=pltpu.CompilerParams(vmem_limit_bytes=32 * 1024 * 1024),
        cost_estimate=pl.CostEstimate(
            flops=2 * count * depth * right.shape[0],
            bytes_accessed=2 * (tps * count * depth + right.size + count * right.shape[0]),
            transcendentals=0,
        ),
    )(left, right)


def scatter_dense(left, right):
    part = by_quarter(left, right)
    part = part.reshape(-1, part.shape[2])
    return f32(lax.psum_scatter(part, (TP, CTX), scatter_dimension=0, tiled=True))


def scatter_columns(part):
    steps = lax.axis_size(CTX)
    low, high = tp_bits()
    size = part.shape[1] // 4
    quarter = [part[:, index * size : (index + 1) * size] for index in range(4)]
    sent = jnp.concatenate(
        [either(low, quarter[1], quarter[0]), either(low, quarter[3], quarter[2])], axis=1
    )
    came = across(sent, 1)
    first = f32(either(low, quarter[0], quarter[1])) + f32(came[:, :size])
    second = f32(either(low, quarter[2], quarter[3])) + f32(came[:, size:])
    kept = bf16(either(high, first, second))
    sent = bf16(either(high, second, first))
    rows = part.shape[0] // steps
    result = [None] * steps
    for step in list(range(1, steps)) + [0]:
        row = ((lax.axis_index(CTX) - step) % steps) * rows
        own, other = [lax.dynamic_slice_in_dim(item, row, rows, axis=0) for item in (kept, sent)]
        done = bf16(f32(own) + f32(across(other, 2)))
        result[step] = along(done, CTX, -step)
    return result


def tp_sum(part):
    return part + across(part, 1) + across(part, 2) + across(part, 3)


def share_out(own):
    return in_columns(own, across(own, 1), across(own, 2), across(own, 3))


def tie(*values):
    return lax.optimization_barrier(values)


def after(value, *others):
    return lax.optimization_barrier((value, *others))[0]


def by_place(blocks):
    order = (lax.axis_index(CTX) - jnp.arange(len(blocks))) % len(blocks)
    return jnp.stack(blocks)[order]


def exchange(parts):
    return lax.all_to_all(parts, CTX, 0, 0)


def swap(value):
    return lax.ppermute(value, SHARD, [(0, 1), (1, 0)])


def joined(near, far):
    first = lax.axis_index(SHARD) == 0
    return jnp.concatenate([jnp.where(first, near, far), jnp.where(first, far, near)], axis=0)


def halves(value):
    half = value.shape[1] // 2
    side = lax.axis_index(SHARD)
    return (
        lax.dynamic_slice_in_dim(value, side * half, half, axis=1),
        lax.dynamic_slice_in_dim(value, (1 - side) * half, half, axis=1),
    )


def far_gradient(rows, change):
    return bf16(dot(halves(rows)[1], change, (0, 0)))


def near_gradient(rows, change, arrived):
    total = bf16(dot(halves(rows)[0], change, (0, 0)) + f32(arrived))
    steps = lax.axis_size(CTX)
    return total.reshape(steps, total.shape[0] // steps, total.shape[1])


def attend_kernel(q_ref, k_ref, v_ref, bias_ref, mixed_ref, norm_ref, peak_ref):
    scale = HEAD_DIM ** (-0.5)
    scores = dot(q_ref[...], k_ref[...], (1, 1)) * scale + f32(bias_ref[...])
    peak = jnp.max(scores, axis=-1, keepdims=True)
    weights = jnp.exp(scores - peak)
    total = jnp.sum(weights, axis=-1, keepdims=True)
    mixed_ref[...] = bf16(dot(bf16(weights / total), v_ref[...], (1, 0)))
    norm_ref[...] = jnp.broadcast_to(peak + jnp.log(total), norm_ref.shape)
    peak_ref[...] = jnp.broadcast_to(jnp.max(peak, axis=0, keepdims=True), peak_ref.shape)


def attend_back_kernel(
    q_ref, k_ref, v_ref, bias_ref, norm_ref, back_ref, dq_ref, dk_ref, dv_ref
):
    scale = HEAD_DIM ** (-0.5)

    @pl.when(pl.program_id(0) == 0)
    def _():
        dk_ref[...] = jnp.zeros_like(dk_ref)
        dv_ref[...] = jnp.zeros_like(dv_ref)

    scores = dot(q_ref[...], k_ref[...], (1, 1)) * scale + f32(bias_ref[...])
    chances = jnp.exp(scores - norm_ref[:, :1])
    dv_ref[...] += dot(bf16(chances), back_ref[...], (0, 0))
    share_back = dot(back_ref[...], v_ref[...], (1, 1))
    score_back = bf16(
        chances * (share_back - jnp.sum(chances * share_back, axis=-1, keepdims=True))
    )
    dq_ref[...] = dot(score_back, k_ref[...], (1, 0)) * scale
    dk_ref[...] += dot(score_back, q_ref[...], (0, 0)) * scale


ROWS = 640


def attend(queries, keys, values, bias):
    rows, size = queries.shape
    count = keys.shape[0]
    turns = count // ROWS
    row = pl.BlockSpec((ROWS, size), lambda i: (i, 0))
    whole = pl.BlockSpec((count, size), lambda i: (0, 0))
    return pl.pallas_call(
        attend_kernel,
        grid=(rows // ROWS,),
        in_specs=[row, whole, whole, pl.BlockSpec((ROWS, count), lambda i: (i % turns, 0))],
        out_specs=[row, row, pl.BlockSpec((8, size), lambda i: (i, 0))],
        out_shape=[
            jax.ShapeDtypeStruct((rows, size), jnp.bfloat16),
            jax.ShapeDtypeStruct((rows, size), jnp.float32),
            jax.ShapeDtypeStruct((rows // ROWS * 8, size), jnp.float32),
        ],
        compiler_params=pltpu.CompilerParams(vmem_limit_bytes=48 * 1024 * 1024),
        cost_estimate=pl.CostEstimate(
            flops=4 * rows * count * size,
            bytes_accessed=4 * rows * size * 2 + 2 * count * count * 2,
            transcendentals=rows * count,
        ),
    )(queries, keys, values, bias)


def attend_back(queries, keys, values, bias, norm, back):
    rows, size = queries.shape
    count = keys.shape[0]
    turns = count // ROWS
    row = pl.BlockSpec((ROWS, size), lambda i: (i, 0))
    whole = pl.BlockSpec((count, size), lambda i: (0, 0))
    return pl.pallas_call(
        attend_back_kernel,
        grid=(rows // ROWS,),
        in_specs=[
            row, whole, whole, pl.BlockSpec((ROWS, count), lambda i: (i % turns, 0)), row, row
        ],
        out_specs=[row, whole, whole],
        out_shape=[
            jax.ShapeDtypeStruct((rows, size), jnp.float32),
            jax.ShapeDtypeStruct((count, size), jnp.float32),
            jax.ShapeDtypeStruct((count, size), jnp.float32),
        ],
        compiler_params=pltpu.CompilerParams(vmem_limit_bytes=48 * 1024 * 1024),
        cost_estimate=pl.CostEstimate(
            flops=10 * rows * count * size,
            bytes_accessed=6 * rows * size * 2 + 2 * count * count * 2,
            transcendentals=rows * count,
        ),
    )(queries, keys, values, bias, norm, back)


def pair_gates(logits, routes):
    chosen = []
    for choice in range(TOP):
        chosen.append(
            sum(
                jnp.where(routes[choice] == expert, logits[expert], 0.0)
                for expert in range(logits.shape[0])
            )
        )
    top = jnp.maximum(chosen[0], chosen[1])
    powers = [jnp.exp(item - top) for item in chosen]
    return [power / (powers[0] + powers[1]) for power in powers]


def pair_gates_back(changes, gates, routes, experts):
    mean = gates[0] * changes[0] + gates[1] * changes[1]
    chosen = [gates[choice] * (changes[choice] - mean) for choice in range(TOP)]
    return jnp.stack(
        [
            sum(jnp.where(routes[choice] == expert, chosen[choice], 0.0) for choice in range(TOP))
            for expert in range(experts)
        ]
    )


def swap_halves(value):
    half = value.shape[-1] // 2
    return jnp.concatenate([value[..., half:], value[..., :half]], axis=-1)


def small_gradient(part, extra):
    steps = lax.axis_size(CTX)
    here, side = lax.axis_index(CTX), lax.axis_index(SHARD)
    whole = jnp.concatenate([share_out(part), extra], axis=0)
    half = whole.shape[1] // 2
    whole = either(side, whole[:, :half], whole[:, half:]) + swap(
        either(side, whole[:, half:], whole[:, :half])
    )
    pieces = whole.reshape(whole.shape[0], steps, half // steps).transpose(1, 0, 2)
    return sum(
        along(
            lax.dynamic_index_in_dim(pieces, (here + step) % steps, 0, keepdims=False), CTX, step
        )
        for step in range(steps)
    )


def on_device_fast(
    inputs,
    parents,
    attention_routes,
    expert_routes,
    attention_gain,
    attention_router,
    query_weight,
    key_weight,
    value_weight,
    output_weight,
    expert_gain,
    expert_router,
    gate_weight,
    up_weight,
    down_weight,
    cotangent,
):
    count, width = inputs.shape
    experts, depth_here, local_width = query_weight.shape
    hidden = gate_weight.shape[2]
    steps, shards, tps = lax.axis_size(CTX), lax.axis_size(SHARD), lax.axis_size(TP)
    here, side, place = lax.axis_index(CTX), lax.axis_index(SHARD), lax.axis_index(TP)
    heads = local_width // HEAD_DIM
    rows, quarter = count // tps, width // tps
    tokens = count * steps
    slots = -(-CAP // 64) * 64

    def own_columns(value):
        return lax.dynamic_slice_in_dim(value, place * quarter, quarter, axis=value.ndim - 1)

    own_inputs = own_columns(inputs)
    def gather_rows(value):
        value = lax.dynamic_slice_in_dim(value, place * rows, rows, axis=0)
        return lax.all_gather(value, (CTX, TP), axis=0, tiled=True)

    all_inputs = gather_rows(inputs)
    small = jnp.concatenate(
        [attention_gain[None], expert_gain[None], attention_router.T, expert_router.T], axis=0
    )
    routes = jnp.concatenate([attention_routes.T, expert_routes.T], axis=0)
    packed = jnp.zeros((small.shape[0] + 2 * TOP, max(count, depth_here)), jnp.bfloat16)
    packed = lax.dynamic_update_slice(packed, small, (0, 0))
    packed = lax.dynamic_update_slice(packed, bf16(routes), (small.shape[0], 0))
    packed_near = [along(packed, CTX, step) for step in range(steps)]
    packed_all = by_place(packed_near)
    routes_all = packed_all[:, small.shape[0] :, :count].transpose(1, 0, 2).astype(jnp.int32)
    head_routes = routes_all[:TOP].reshape(TOP, tokens)
    own_head_routes, own_expert_routes = routes[:TOP], routes[TOP:]
    small_near = packed_all[:, : small.shape[0], :depth_here].transpose(1, 0, 2)
    small_near = small_near.reshape(small.shape[0], steps * depth_here).T
    small_all = joined(small_near, swap(small_near)).T
    gain_first, gain_second = f32(small_all[0]), f32(small_all[1])
    router_first, router_second = small_all[2 : 2 + experts], small_all[2 + experts :]
    own_small = f32(own_columns(small_all))
    own_gain_first, own_gain_second = own_small[0], own_small[1]
    own_router_first, own_router_second = own_small[2 : 2 + experts], own_small[2 + experts :]

    def rows_of(value):
        return value.reshape(-1, value.shape[2])

    def project_parts(query, key, value):
        query = query.reshape(experts, depth_here, heads, HEAD_DIM).transpose(2, 1, 0, 3)
        key, value = [
            item.reshape(depth_here, heads, HEAD_DIM).transpose(1, 0, 2) for item in (key, value)
        ]
        query = query.reshape(heads, depth_here, experts * HEAD_DIM)
        return jnp.concatenate([query, key, value], axis=2)

    def output_parts(weight):
        weight = weight.reshape(experts, heads, HEAD_DIM, depth_here).transpose(1, 3, 0, 2)
        return weight.reshape(heads, depth_here, experts * HEAD_DIM)

    nears = [exchange(project_parts(query_weight, key_weight, value_weight))]
    weight, nears[0] = tie(output_weight, nears[0])
    fars = [swap(nears[0])]
    nears.append(exchange(output_parts(weight)))
    weight, nears[1] = tie(gate_weight, nears[1])
    nears.append(exchange(weight))
    project = joined(rows_of(nears[0]), rows_of(fars[0]))
    own_upstream = own_columns(cotangent)

    target = (here + jnp.arange(steps, dtype=jnp.int32)) % steps
    named = own_expert_routes[None] == target[:, None, None]
    member = named[:, 0] | named[:, 1]
    slot = jnp.cumsum(member.astype(jnp.int32), axis=1) - 1
    onehot = (slot[:, None, :] == jnp.arange(slots, dtype=jnp.int32)[None, :, None]) & member[
        :, None, :
    ]
    onehot_all = onehot.astype(jnp.bfloat16).reshape(steps * slots, count)

    def picked_slots(value):
        picked = bf16(dot(onehot_all, value, (1, 0)))
        return from_ctx([picked[step * slots : (step + 1) * slots] for step in range(steps)])

    def from_slots(value):
        return dot(onehot_all, jnp.concatenate(scatter_columns(value), axis=0), (0, 0))

    chosen = (routes_all[TOP] == here) | (routes_all[TOP + 1] == here)
    chosen_slot = jnp.cumsum(chosen.astype(jnp.int32), axis=1) - 1
    chosen_onehot = (
        chosen_slot[:, None, :] == jnp.arange(slots, dtype=jnp.int32)[None, :, None]
    ) & chosen[:, None, :]

    token = jnp.arange(tokens, dtype=jnp.int32)
    unit = token // SEG
    group_units = tokens // SEG
    group_first = side * group_units
    parents, all_inputs = tie(parents, all_inputs)
    chain = ancestors(parents, group_first + jnp.arange(group_units, dtype=jnp.int32))
    valid = chain >= 0
    depth = jnp.sum(valid[:, 1:].astype(jnp.int32), axis=1, dtype=jnp.int32)
    reached = jnp.any(
        (chain[:, :, None] - group_first == jnp.arange(group_units, dtype=jnp.int32))
        & valid[:, :, None],
        axis=1,
    )
    unit_onehot = (unit[:, None] == jnp.arange(group_units, dtype=jnp.int32)[None, :]).astype(
        jnp.bfloat16
    )
    row_reach = bf16(dot(unit_onehot, reached.astype(jnp.bfloat16), (1, 0)))
    reach = dot(row_reach, unit_onehot, (1, 1))
    allowed = (reach > 0.5) & (
        (unit[:, None] != unit[None, :]) | (token[None, :] <= token[:, None])
    )
    bias = jnp.where(allowed, 0.0, -1e30).astype(jnp.bfloat16)
    token_depth = jnp.sum(
        jnp.where(unit[:, None] == jnp.arange(group_units)[None, :], depth[None, :], 0), axis=1
    )
    cosine, sine = rope_tables(token_depth * SEG + token % SEG, HEAD_DIM // 2)
    cosine = jnp.concatenate([cosine, cosine], axis=1)
    sine = jnp.concatenate([-sine, sine], axis=1)

    normed = bf16(normalize(f32(all_inputs), gain_first))
    head_gates = pair_gates(dot(router_first, normed, (1, 1)), head_routes)
    raw = dot(normed, project, (1, 0))
    nears[1], raw = tie(nears[1], raw)
    fars.append(swap(nears[1]))
    outward = joined(rows_of(nears[1]), rows_of(fars[1]))
    chosen_heads = [
        [head_routes[choice][:, None] == expert for expert in range(experts)]
        for choice in range(TOP)
    ]

    def pick(value, choice):
        return sum(
            jnp.where(
                chosen_heads[choice][expert],
                value[:, expert * HEAD_DIM : (expert + 1) * HEAD_DIM],
                0.0,
            )
            for expert in range(experts)
        )

    def place_pair(pair):
        return jnp.concatenate(
            [
                sum(jnp.where(chosen_heads[choice][expert], pair[choice], 0.0) for choice in range(TOP))
                for expert in range(experts)
            ],
            axis=1,
        )

    def turn(value):
        return value * cosine + swap_halves(value) * sine

    def turn_back(value):
        return value * cosine - swap_halves(value) * sine

    inner = experts * HEAD_DIM
    queries = bf16(jnp.concatenate([turn(pick(raw, choice)) for choice in range(TOP)], axis=0))
    keys = bf16(turn(raw[:, inner : inner + HEAD_DIM]))
    values = bf16(raw[:, inner + HEAD_DIM :])
    mixed, norm, peaks = attend(queries, keys, values, bias)
    mixed_pair = [f32(mixed[:tokens]), f32(mixed[tokens:])]
    gated_mixed = bf16(
        place_pair([head_gates[choice][:, None] * mixed_pair[choice] for choice in range(TOP)])
    )
    weight, nears[2] = tie(up_weight, nears[2])
    fars.append(swap(nears[2]))
    nears.append(exchange(weight))
    attention, nears[3], fars[2] = tie(scatter_dense(gated_mixed, outward), nears[3], fars[2])
    fars.append(swap(nears[3]))
    down_parts = after(down_weight, nears[3]).transpose(0, 2, 1)
    half = depth_here // 2
    down_near = [exchange(down_parts[:, :half])]
    down_far = [swap(down_near[0])]
    hidden_state = f32(own_inputs) + attention
    statistics = tp_sum(
        jnp.concatenate(
            [
                jnp.sum(hidden_state * hidden_state, axis=1)[None],
                jnp.einsum(
                    "td,ed->et", hidden_state * own_gain_second, own_router_second, precision=HIGH
                ),
            ],
            axis=0,
        )
    )
    norm_two = lax.rsqrt(statistics[0] / width + EPS)
    expert_gates = pair_gates(statistics[1:] * norm_two, own_expert_routes)
    own_normed_two = bf16(hidden_state * norm_two[:, None] * own_gain_second)
    gate_of = jnp.where(named[:, 0], expert_gates[0], 0.0) + jnp.where(
        named[:, 1], expert_gates[1], 0.0
    )
    gate_sent = jnp.sum(jnp.where(onehot, gate_of[:, None, :], 0.0), axis=2)
    gate_slot = by_place(from_ctx([gate_sent[step : step + 1] for step in range(steps)]))
    gate_slot = gate_slot.reshape(steps * slots, 1)
    row_blocks = picked_slots(own_normed_two)
    down_near.append(exchange(after(down_parts, *row_blocks)[:, half:]))
    down_far.append(swap(down_near[1]))
    slot_rows, down_near[0] = tie(gather_columns(row_blocks), down_near[0])
    down_near[1], gate_slot = tie(down_near[1], gate_slot)
    all_cotangent = gather_rows(after(cotangent, *row_blocks))
    slot_upstream = bf16(
        jnp.einsum(
            "bst,btd->bsd",
            chosen_onehot.astype(jnp.bfloat16),
            all_cotangent.reshape(steps, count, width),
            preferred_element_type=jnp.float32,
        )
    ).reshape(steps * slots, width)

    def whole(index):
        return joined(rows_of(nears[index]), rows_of(fars[index]))

    gate, up = whole(2), whole(3)
    down = joined(
        rows_of(jnp.concatenate(down_near, axis=1)), rows_of(jnp.concatenate(down_far, axis=1))
    )
    gate_pre = dot(slot_rows, gate, (1, 0))
    up_pre = dot(slot_rows, up, (1, 0))
    act_raw = dot(slot_upstream, down, (1, 0))
    sigmoid = jax.nn.sigmoid(gate_pre)
    activated = gate_pre * sigmoid * up_pre
    gated_act = bf16(activated * gate_slot)
    gate_back_slot = jnp.sum(activated * act_raw, axis=1, keepdims=True)
    act_back = act_raw * gate_slot
    gate_back = bf16(act_back * up_pre * sigmoid * (1.0 + gate_pre * (1.0 - sigmoid)))
    up_back = bf16(act_back * gate_pre * sigmoid)
    pairs = [(slot_upstream, gated_act), (slot_rows, gate_back), (slot_rows, up_back)]
    far_terms = [far_gradient(*pair) for pair in pairs]
    arrived = [swap(term) for term in far_terms]
    rows_back = bf16(
        dot(after(gate_back, *far_terms), gate, (1, 1)) + dot(up_back, up, (1, 1))
    )
    fed = bf16(dot(gated_act, down, (1, 1)))
    gate_sums = tp_sum(after(gate_back_slot, rows_back).reshape(steps, slots))
    gate_sums = jnp.concatenate(
        [
            along(lax.dynamic_slice_in_dim(gate_sums, (here - step) % steps, 1), CTX, -step)
            for step in range(steps)
        ]
    )
    gate_changes = jnp.sum(jnp.where(onehot, gate_sums[:, :, None], 0.0), axis=1)
    normed_two_back, ready = tie(
        from_slots(rows_back), near_gradient(*pairs[0], arrived[0])
    )

    expert_gate_back = [
        sum(
            jnp.where(named[step, choice], gate_changes[step], 0.0) for step in range(steps)
        )
        for choice in range(TOP)
    ]
    expert_logit_back = pair_gates_back(
        expert_gate_back, expert_gates, own_expert_routes, experts
    )
    router_second_term = jnp.einsum(
        "et,td->ed", expert_logit_back, f32(own_normed_two), precision=HIGH
    )
    normed_two_back = normed_two_back + jnp.einsum(
        "et,ed->td", expert_logit_back, own_router_second, precision=HIGH
    )
    scaled = normed_two_back * own_gain_second
    mean = tp_sum(jnp.sum(scaled * hidden_state, axis=1)[None])[0] / width
    gain_second_term = jnp.sum(normed_two_back * hidden_state * norm_two[:, None], axis=0)
    hidden_back = (
        f32(own_upstream)
        + norm_two[:, None] * scaled
        - hidden_state * (norm_two**3 * mean)[:, None]
    )

    down_back = exchange(ready)
    all_back, gate_ready = tie(
        gather_dense(bf16(hidden_back)),
        near_gradient(slot_rows, after(gate_back, hidden_back), arrived[1]),
    )
    raw_back = dot(all_back, outward, (1, 0))
    pair_back = [pick(raw_back, choice) for choice in range(TOP)]
    head_change = jnp.stack(
        [jnp.sum(mixed_pair[choice] * pair_back[choice], axis=1) for choice in range(TOP)]
    )
    head_sums = tp_sum(head_change).reshape(TOP, steps, count).transpose(1, 0, 2)
    head_gate_back = sum(
        along(
            lax.dynamic_index_in_dim(head_sums, (here - step) % steps, 0, keepdims=False),
            CTX,
            -step,
        )
        for step in range(steps)
    )
    mixed_back = bf16(
        jnp.concatenate(
            [head_gates[choice][:, None] * pair_back[choice] for choice in range(TOP)], axis=0
        )
    )
    mixed_back, down_back, head_gate_back = tie(mixed_back, down_back, head_gate_back)
    gate_returned = [exchange(after(gate_ready, down_back)[:, :half])]
    query_change, key_change, value_change = attend_back(
        queries, keys, values, bias, norm, mixed_back
    )
    change = bf16(
        jnp.concatenate(
            [
                place_pair(
                    [turn_back(query_change[:tokens]), turn_back(query_change[tokens:])]
                ),
                turn_back(f32(bf16(key_change))),
                value_change,
            ],
            axis=1,
        )
    )
    change, arrived[2], gate_returned[0] = tie(change, arrived[2], gate_returned[0])
    feed = from_slots(after(fed, change))
    gate_returned.append(exchange(after(gate_ready, gate_returned[0])[:, half:]))
    up_ready = near_gradient(slot_rows, after(up_back, change), arrived[2])
    pairs += [(all_back, gated_mixed), (normed, change)]
    arrived += [swap(far_gradient(*pair)) for pair in pairs[3:]]
    up_returned = exchange(after(up_ready, gate_returned[1]))
    normed_back, feed, output_ready, project_ready, gate_returned[1], up_returned = tie(
        scatter_dense(change, project),
        feed,
        near_gradient(*pairs[3], arrived[3]),
        near_gradient(*pairs[4], arrived[4]),
        gate_returned[1],
        up_returned,
    )
    output = share_out(bf16(hidden_state + feed))
    output_all = exchange(output_ready)
    project_all = exchange(after(project_ready, output_all))
    down_gradient = f32(down_back.transpose(0, 2, 1))
    gate_gradient = f32(jnp.concatenate(gate_returned, axis=1))
    up_gradient = f32(up_returned)
    own_rows = f32(inputs)
    norm_one = lax.rsqrt(jnp.mean(own_rows * own_rows, axis=1) + EPS)
    own_values = f32(own_inputs)
    own_normed = bf16(own_values * norm_one[:, None] * own_gain_first)
    own_head_gates = [
        lax.dynamic_slice_in_dim(gate_item, here * count, count, axis=0)
        for gate_item in head_gates
    ]
    head_logit_back = pair_gates_back(
        [head_gate_back[choice] for choice in range(TOP)],
        own_head_gates,
        own_head_routes,
        experts,
    )
    router_first_term = jnp.einsum(
        "et,td->ed", head_logit_back, f32(own_normed), precision=HIGH
    )
    normed_back = normed_back + jnp.einsum(
        "et,ed->td", head_logit_back, own_router_first, precision=HIGH
    )
    scaled = normed_back * own_gain_first
    mean = tp_sum(jnp.sum(scaled * own_values, axis=1)[None])[0] / width
    gain_first_term = jnp.sum(normed_back * own_values * norm_one[:, None], axis=0)
    input_gradient = share_out(
        bf16(
            hidden_back
            + norm_one[:, None] * scaled
            - own_values * (norm_one**3 * mean)[:, None]
        )
    )
    small_sums = small_gradient(
        jnp.concatenate(
            [
                gain_first_term[None],
                gain_second_term[None],
                router_first_term,
                router_second_term,
            ],
            axis=0,
        ),
        jnp.where(
            jnp.arange(width)[None] % depth_here == side * steps + here, jnp.max(peaks), 0.0
        ),
    )

    query_gradient = (
        project_all[:, :, :inner]
        .reshape(heads, depth_here, experts, HEAD_DIM)
        .transpose(2, 1, 0, 3)
        .reshape(experts, depth_here, local_width)
    )
    key_gradient = (
        project_all[:, :, inner : inner + HEAD_DIM].transpose(1, 0, 2).reshape(depth_here, local_width)
    )
    value_gradient = (
        project_all[:, :, inner + HEAD_DIM :].transpose(1, 0, 2).reshape(depth_here, local_width)
    )
    query_gradient, key_gradient, value_gradient = [
        f32(after(item)) for item in (query_gradient, key_gradient, value_gradient)
    ]
    output_gradient = (
        output_all
        .reshape(heads, depth_here, experts, HEAD_DIM)
        .transpose(2, 0, 3, 1)
        .reshape(experts, local_width, depth_here)
    )
    output_gradient = f32(after(output_gradient))

    head_peaks = jnp.max(
        small_sums[-1, : shards * steps].reshape(shards, steps), axis=0
    )
    factor = jnp.repeat(jnp.sqrt(jnp.minimum(1.0, CLIP / head_peaks)), HEAD_DIM)
    clipped_query = bf16(f32(query_weight) * factor)
    clipped_key = bf16(f32(key_weight) * factor)
    return (
        output,
        input_gradient,
        small_sums[0],
        small_sums[2 : 2 + experts].T,
        query_gradient,
        key_gradient,
        value_gradient,
        output_gradient,
        small_sums[1],
        small_sums[2 + experts : 2 + 2 * experts].T,
        gate_gradient,
        up_gradient,
        down_gradient,
        clipped_query,
        clipped_key,
    )


def on_device(*arrays):
    experts, _, local_width = arrays[6].shape
    steps = lax.axis_size(CTX)
    tokens = arrays[0].shape[0] * steps
    fits = (
        experts == steps
        and local_width == steps * HEAD_DIM
        and lax.axis_size(TP) == 4
        and lax.axis_size(SHARD) == 2
        and tokens % ROWS == 0
    )
    return on_device_fast(*arrays) if fits else on_device_general(*arrays)


def solution(mesh):
    placed = (
        P(BOTH, None),
        P(),
        P(BOTH, None),
        P(BOTH, None),
        P(BOTH),
        P(BOTH, None),
        P(None, BOTH, TP),
        P(BOTH, TP),
        P(BOTH, TP),
        P(None, TP, BOTH),
        P(BOTH),
        P(BOTH, None),
        P(None, BOTH, TP),
        P(None, BOTH, TP),
        P(None, TP, BOTH),
        P(BOTH, None),
    )
    return jax.shard_map(
        on_device,
        mesh=mesh,
        in_specs=placed,
        out_specs=(
            P(BOTH, None),
            P(BOTH, None),
            P(BOTH),
            P(BOTH, None),
            P(None, BOTH, TP),
            P(BOTH, TP),
            P(BOTH, TP),
            P(None, TP, BOTH),
            P(BOTH),
            P(BOTH, None),
            P(None, BOTH, TP),
            P(None, BOTH, TP),
            P(None, TP, BOTH),
            P(None, BOTH, TP),
            P(BOTH, TP),
        ),
        check_vma=False,
    )
```

```python
import jax
import jax.numpy as jnp
from jax import lax
from jax.experimental import pallas as pl
from jax.experimental.pallas import tpu as pltpu
from jax.sharding import PartitionSpec as P

SHARD, CTX, TP = "shard", "ctx", "tp"
BOTH = (SHARD, CTX)
HEAD_DIM = 128
TOP = 2
SEG = 64
PATH = 10
CAP = 176


EPS = 1e-05
ROPE_BASE = 10000.0
CLIP = 2.0
HIGH = lax.Precision.HIGHEST


def normalize(value, gain):
    scale = lax.rsqrt(jnp.mean(value * value, axis=-1, keepdims=True) + EPS)
    return value * scale * gain


def normalize_back(change, value, gain):
    scale = lax.rsqrt(jnp.mean(value * value, axis=-1, keepdims=True) + EPS)
    gain_change = jnp.sum(change * value * scale, axis=0)
    scaled = change * gain
    value_change = scale * scaled - value * scale**3 * jnp.mean(
        scaled * value, axis=-1, keepdims=True
    )
    return (value_change, gain_change)


def gating(normed, router, routes):
    logits = jnp.dot(normed, router, preferred_element_type=jnp.float32)
    chosen = jnp.take_along_axis(logits, routes, axis=1)
    return jax.nn.softmax(chosen, axis=1)


def gating_back(change, gates, routes, experts):
    chosen_change = gates * (change - jnp.sum(gates * change, axis=1, keepdims=True))
    onehot = (routes[:, :, None] == jnp.arange(experts, dtype=jnp.int32)[None, None, :]).astype(
        jnp.float32
    )
    return jnp.sum(chosen_change[:, :, None] * onehot, axis=1)


def slot_tables(routes, experts, capacity):
    number = routes.shape[0] * routes.shape[1]
    flat = routes.reshape(number)
    onehot = (flat[:, None] == jnp.arange(experts, dtype=jnp.int32)[None, :]).astype(jnp.int32)
    before = jnp.cumsum(onehot, axis=0, dtype=jnp.int32) - onehot
    place = jnp.sum(before * onehot, axis=1, dtype=jnp.int32)
    slot_index = flat * capacity + place
    pair_index = (
        jnp.zeros((experts * capacity,), jnp.int32)
        .at[slot_index]
        .set(jnp.arange(number, dtype=jnp.int32))
    )
    filled = jnp.zeros((experts * capacity,), jnp.int32).at[slot_index].set(1)
    return (slot_index, pair_index, filled)


def rope_tables(positions, half):
    frequency = ROPE_BASE ** (-jnp.arange(half, dtype=jnp.float32) / half)
    angle = positions.astype(jnp.float32)[:, None] * frequency[None, :]
    return (jnp.cos(angle), jnp.sin(angle))


def rotate(value, cosine, sine):
    half = value.shape[-1] // 2
    first = value[..., :half]
    second = value[..., half:]
    return jnp.concatenate(
        [first * cosine - second * sine, second * cosine + first * sine], axis=-1
    )


def rotate_back(change, cosine, sine):
    half = change.shape[-1] // 2
    first = change[..., :half]
    second = change[..., half:]
    return jnp.concatenate(
        [first * cosine + second * sine, second * cosine - first * sine], axis=-1
    )


def ancestors(parents, start_units):
    chain = [start_units]
    current = start_units
    for level in range(PATH - 1):
        current = jnp.where(current >= 0, parents[jnp.maximum(current, 0)], -1)
        chain.append(current)
    return jnp.stack(chain, axis=1)


def unit_mask(valid_row):
    token_row = jnp.arange(SEG * TOP) // TOP
    causal = jnp.arange(SEG)[None, :] <= token_row[:, None]
    others = jnp.broadcast_to(valid_row[None, 1:, None], (SEG * TOP, PATH - 1, SEG))
    return jnp.concatenate([causal[:, None, :], others], axis=1).reshape(SEG * TOP, PATH * SEG)


def dispatch(rows, pair_index, filled, choose, experts, capacity):
    picked = rows[pair_index // choose]
    return jnp.where(filled[:, None] > 0, picked, jnp.zeros((), rows.dtype)).reshape(
        experts, capacity, rows.shape[1]
    )


def spread(pairs, pair_index, filled, experts, capacity):
    picked = pairs[pair_index]
    return jnp.where(filled[:, None] > 0, picked, jnp.zeros((), pairs.dtype)).reshape(
        experts, capacity, pairs.shape[1]
    )


def on_device_general(
    inputs,
    parents,
    attention_routes,
    expert_routes,
    attention_gain,
    attention_router,
    query_weight,
    key_weight,
    value_weight,
    output_weight,
    expert_gain,
    expert_router,
    gate_weight,
    up_weight,
    down_weight,
    cotangent,
):
    count = inputs.shape[0]
    width = inputs.shape[1]
    experts = query_weight.shape[0]
    local_width = query_weight.shape[2]
    head_dim = HEAD_DIM
    local_heads = local_width // head_dim
    capacity = CAP
    choose = attention_routes.shape[1]
    segment = SEG
    units_here = count // segment
    group_units = lax.axis_size(CTX) * units_here
    scale = head_dim ** (-0.5)
    gain_one, router_one, query_full, key_full, value_full, output_full, gain_two, router_two = (
        lax.all_gather(attention_gain, BOTH, axis=0, tiled=True),
        lax.all_gather(attention_router, BOTH, axis=0, tiled=True),
        lax.all_gather(query_weight, BOTH, axis=1, tiled=True),
        lax.all_gather(key_weight, BOTH, axis=0, tiled=True),
        lax.all_gather(value_weight, BOTH, axis=0, tiled=True),
        lax.all_gather(output_weight, BOTH, axis=2, tiled=True),
        lax.all_gather(expert_gain, BOTH, axis=0, tiled=True),
        lax.all_gather(expert_router, BOTH, axis=0, tiled=True),
    )
    first_unit = (
        lax.axis_index(SHARD) * lax.axis_size(CTX) + lax.axis_index(CTX)
    ) * units_here
    group_first = lax.axis_index(SHARD) * group_units
    own_units = first_unit + jnp.arange(units_here, dtype=jnp.int32)
    chain = ancestors(parents, own_units)
    valid = chain >= 0
    depth = jnp.sum(valid[:, 1:].astype(jnp.int32), axis=1, dtype=jnp.int32)
    positions = (depth[:, None] * segment + jnp.arange(segment, dtype=jnp.int32)[None, :]).reshape(
        count
    )
    cosine, sine = rope_tables(positions, head_dim // 2)
    local_chain = jnp.clip(chain - group_first, 0, group_units - 1)
    allowed = jax.vmap(unit_mask)(valid)
    residual = inputs.astype(jnp.float32)
    gain_first = gain_one.astype(jnp.float32)
    normed = normalize(residual, gain_first).astype(jnp.bfloat16)
    head_gates = gating(normed, router_one, attention_routes)
    head_slot, head_pair, head_filled = slot_tables(attention_routes, experts, capacity)
    head_rows = dispatch(normed, head_pair, head_filled, choose, experts, capacity)
    query_slots = jnp.einsum(
        "ecd,edf->ecf", head_rows, query_full, preferred_element_type=jnp.float32
    )
    query_pairs = query_slots.reshape(experts * capacity, local_width)[head_slot].reshape(
        count, choose, local_heads, head_dim
    )
    queries = rotate(query_pairs, cosine[:, None, None, :], sine[:, None, None, :]).astype(
        jnp.bfloat16
    )
    key_raw = jnp.dot(normed, key_full, preferred_element_type=jnp.float32).reshape(
        count, local_heads, head_dim
    )
    keys = (
        rotate(key_raw, cosine[:, None, :], sine[:, None, :])
        .astype(jnp.bfloat16)
        .reshape(count, local_width)
    )
    values = jnp.dot(normed, value_full, preferred_element_type=jnp.float32).astype(jnp.bfloat16)
    all_keys, all_values = (
        lax.all_gather(keys, CTX, axis=0, tiled=True),
        lax.all_gather(values, CTX, axis=0, tiled=True),
    )
    path_keys = all_keys.reshape(group_units, segment, local_width)[local_chain].reshape(
        units_here, PATH * segment, local_heads, head_dim
    )
    path_values = all_values.reshape(group_units, segment, local_width)[local_chain].reshape(
        units_here, PATH * segment, local_heads, head_dim
    )
    query_units = queries.reshape(units_here, segment * choose, local_heads, head_dim)
    scores = (
        jnp.einsum("uqhd,ukhd->uhqk", query_units, path_keys, preferred_element_type=jnp.float32)
        * scale
    )
    masked = jnp.where(allowed[:, None], scores, -1e30)
    peak = jnp.max(masked, axis=-1, keepdims=True)
    weights = jnp.where(allowed[:, None], jnp.exp(masked - peak), 0.0)
    total = jnp.sum(weights, axis=-1, keepdims=True)
    log_total = peak + jnp.log(total)
    head_peak = jnp.max(peak[..., 0], axis=(0, 2))
    shares = (weights / total).astype(jnp.bfloat16)
    mixed = (
        jnp.einsum("uhqk,ukhd->uqhd", shares, path_values, preferred_element_type=jnp.float32)
        .astype(jnp.bfloat16)
        .reshape(count * choose, local_width)
    )
    mixed_slots = spread(mixed, head_pair, head_filled, experts, capacity)
    out_slots = jnp.einsum(
        "ecf,efd->ecd", mixed_slots, output_full, preferred_element_type=jnp.float32
    )
    out_pairs = out_slots.reshape(experts * capacity, width)[head_slot].reshape(
        count, choose, width
    )
    attention = lax.psum(jnp.sum(head_gates[:, :, None] * out_pairs, axis=1), TP)
    hidden_state = residual + attention
    peak_all = lax.pmax(head_peak, BOTH)
    gain_second = gain_two.astype(jnp.float32)
    normed_two = normalize(hidden_state, gain_second).astype(jnp.bfloat16)
    expert_gates = gating(normed_two, router_two, expert_routes)
    expert_slot, expert_pair, expert_filled = slot_tables(expert_routes, experts, capacity)
    expert_rows = dispatch(normed_two, expert_pair, expert_filled, choose, experts, capacity)
    gate_full, up_full, down_full = (
        lax.all_gather(gate_weight, BOTH, axis=1, tiled=True),
        lax.all_gather(up_weight, BOTH, axis=1, tiled=True),
        lax.all_gather(down_weight, BOTH, axis=2, tiled=True),
    )
    gate_pre = jnp.einsum(
        "ecd,edf->ecf", expert_rows, gate_full, preferred_element_type=jnp.float32
    )
    up_pre = jnp.einsum("ecd,edf->ecf", expert_rows, up_full, preferred_element_type=jnp.float32)
    activated = (jax.nn.silu(gate_pre) * up_pre).astype(jnp.bfloat16)
    down_slots = jnp.einsum(
        "ecf,efd->ecd", activated, down_full, preferred_element_type=jnp.float32
    )
    down_pairs = down_slots.reshape(experts * capacity, width)[expert_slot].reshape(
        count, choose, width
    )
    feed = lax.psum(
        jnp.sum(expert_gates[:, :, None] * down_pairs, axis=1).astype(jnp.bfloat16), TP
    ).astype(jnp.float32)
    output = (hidden_state + feed).astype(jnp.bfloat16)
    upstream = cotangent.astype(jnp.float32)
    down_back = (
        (expert_gates[:, :, None] * upstream[:, None, :])
        .astype(jnp.bfloat16)
        .reshape(count * choose, width)
    )
    expert_gate_part = jnp.sum(down_pairs * upstream[:, None, :], axis=2)
    down_back_slots = spread(down_back, expert_pair, expert_filled, experts, capacity)
    act_back = jnp.einsum(
        "ecd,efd->ecf", down_back_slots, down_full, preferred_element_type=jnp.float32
    )
    sigmoid = jax.nn.sigmoid(gate_pre)
    gate_back = (act_back * up_pre * sigmoid * (1.0 + gate_pre * (1.0 - sigmoid))).astype(
        jnp.bfloat16
    )
    up_back = (act_back * gate_pre * sigmoid).astype(jnp.bfloat16)
    rows_back = jnp.einsum(
        "ecf,edf->ecd", gate_back, gate_full, preferred_element_type=jnp.float32
    ) + jnp.einsum("ecf,edf->ecd", up_back, up_full, preferred_element_type=jnp.float32)
    normed_two_part = jnp.sum(
        rows_back.reshape(experts * capacity, width)[expert_slot].reshape(count, choose, width),
        axis=1,
    )
    collected = []
    for expert in range(experts):
        gate_term = jnp.einsum(
            "cd,cf->df", expert_rows[expert], gate_back[expert], preferred_element_type=jnp.float32
        )
        up_term = jnp.einsum(
            "cd,cf->df", expert_rows[expert], up_back[expert], preferred_element_type=jnp.float32
        )
        down_term = jnp.einsum(
            "cf,cd->fd",
            activated[expert],
            down_back_slots[expert],
            preferred_element_type=jnp.float32,
        )
        collected.append(
            (
                lax.psum_scatter(
                    gate_term.astype(jnp.bfloat16),
                    BOTH,
                    scatter_dimension=0,
                    tiled=True,
                ).astype(jnp.float32),
                lax.psum_scatter(
                    up_term.astype(jnp.bfloat16), BOTH, scatter_dimension=0, tiled=True
                ).astype(jnp.float32),
                lax.psum_scatter(
                    down_term.astype(jnp.bfloat16),
                    BOTH,
                    scatter_dimension=1,
                    tiled=True,
                ).astype(jnp.float32),
            )
        )
    gate_gradient = jnp.stack([item[0] for item in collected])
    up_gradient = jnp.stack([item[1] for item in collected])
    down_gradient = jnp.stack([item[2] for item in collected])
    normed_two_back, expert_gate_back = lax.psum((normed_two_part, expert_gate_part), TP)
    expert_logit_back = gating_back(expert_gate_back, expert_gates, expert_routes, experts)
    router_two_term = jnp.einsum(
        "td,te->de", normed_two.astype(jnp.float32), expert_logit_back, precision=HIGH
    )
    normed_two_back = normed_two_back + jnp.einsum(
        "te,de->td", expert_logit_back, router_two.astype(jnp.float32), precision=HIGH
    )
    hidden_back, gain_two_term = normalize_back(normed_two_back, hidden_state, gain_second)
    hidden_back = hidden_back + upstream
    head_back = (
        (head_gates[:, :, None] * hidden_back[:, None, :])
        .astype(jnp.bfloat16)
        .reshape(count * choose, width)
    )
    head_gate_part = jnp.sum(out_pairs * hidden_back[:, None, :], axis=2)
    head_back_slots = spread(head_back, head_pair, head_filled, experts, capacity)
    output_term = jnp.einsum(
        "ecf,ecd->efd", mixed_slots, head_back_slots, preferred_element_type=jnp.float32
    )
    mixed_back_slots = jnp.einsum(
        "ecd,efd->ecf", head_back_slots, output_full, preferred_element_type=jnp.float32
    )
    mixed_back = (
        mixed_back_slots.reshape(experts * capacity, local_width)[head_slot]
        .astype(jnp.bfloat16)
        .reshape(units_here, segment * choose, local_heads, head_dim)
    )
    again = (
        jnp.einsum("uqhd,ukhd->uhqk", query_units, path_keys, preferred_element_type=jnp.float32)
        * scale
    )
    chances = jnp.where(allowed[:, None], jnp.exp(again - log_total), 0.0)
    value_path_back = jnp.einsum(
        "uhqk,uqhd->ukhd",
        chances.astype(jnp.bfloat16),
        mixed_back,
        preferred_element_type=jnp.float32,
    )
    share_back = jnp.einsum(
        "uqhd,ukhd->uhqk", mixed_back, path_values, preferred_element_type=jnp.float32
    )
    score_back = (
        chances * (share_back - jnp.sum(chances * share_back, axis=-1, keepdims=True))
    ).astype(jnp.bfloat16)
    query_back_raw = (
        jnp.einsum("uhqk,ukhd->uqhd", score_back, path_keys, preferred_element_type=jnp.float32)
        * scale
    )
    key_path_back = (
        jnp.einsum("uhqk,uqhd->ukhd", score_back, query_units, preferred_element_type=jnp.float32)
        * scale
    )
    owner = (
        (local_chain[:, :, None] == jnp.arange(group_units, dtype=jnp.int32)[None, None, :])
        & valid[:, :, None]
    ).astype(jnp.float32)
    key_group = jnp.einsum(
        "upg,upsc->gsc",
        owner,
        key_path_back.reshape(units_here, PATH, segment, local_width),
        precision=HIGH,
    )
    value_group = jnp.einsum(
        "upg,upsc->gsc",
        owner,
        value_path_back.reshape(units_here, PATH, segment, local_width),
        precision=HIGH,
    )
    key_mine, value_mine = (
        lax.psum_scatter(
            key_group.reshape(group_units * segment, local_width).astype(jnp.bfloat16),
            CTX,
            scatter_dimension=0,
            tiled=True,
        ).astype(jnp.float32),
        lax.psum_scatter(
            value_group.reshape(group_units * segment, local_width).astype(jnp.bfloat16),
            CTX,
            scatter_dimension=0,
            tiled=True,
        ).astype(jnp.float32),
    )
    key_back = (
        rotate_back(
            key_mine.reshape(count, local_heads, head_dim), cosine[:, None, :], sine[:, None, :]
        )
        .astype(jnp.bfloat16)
        .reshape(count, local_width)
    )
    value_back = value_mine.astype(jnp.bfloat16)
    query_back = (
        rotate_back(
            query_back_raw.reshape(count, choose, local_heads, head_dim),
            cosine[:, None, None, :],
            sine[:, None, None, :],
        )
        .astype(jnp.bfloat16)
        .reshape(count * choose, local_width)
    )
    query_back_slots = spread(query_back, head_pair, head_filled, experts, capacity)
    query_term = jnp.einsum(
        "ecd,ecf->edf", head_rows, query_back_slots, preferred_element_type=jnp.float32
    )
    key_term = jnp.einsum("td,tf->df", normed, key_back, preferred_element_type=jnp.float32)
    value_term = jnp.einsum("td,tf->df", normed, value_back, preferred_element_type=jnp.float32)
    query_rows_back = jnp.einsum(
        "ecf,edf->ecd", query_back_slots, query_full, preferred_element_type=jnp.float32
    )
    normed_part = jnp.sum(
        query_rows_back.reshape(experts * capacity, width)[head_slot].reshape(count, choose, width),
        axis=1,
    )
    normed_part = (
        normed_part
        + jnp.einsum("tf,df->td", key_back, key_full, preferred_element_type=jnp.float32)
        + jnp.einsum("tf,df->td", value_back, value_full, preferred_element_type=jnp.float32)
    )
    normed_back, head_gate_back = (
        lax.psum(normed_part.astype(jnp.bfloat16), TP).astype(jnp.float32),
        lax.psum(head_gate_part.astype(jnp.bfloat16), TP).astype(jnp.float32),
    )
    head_logit_back = gating_back(head_gate_back, head_gates, attention_routes, experts)
    router_one_term = jnp.einsum(
        "td,te->de", normed.astype(jnp.float32), head_logit_back, precision=HIGH
    )
    normed_back = normed_back + jnp.einsum(
        "te,de->td", head_logit_back, router_one.astype(jnp.float32), precision=HIGH
    )
    input_back, gain_one_term = normalize_back(normed_back, residual, gain_first)
    input_gradient = (input_back + hidden_back).astype(jnp.bfloat16)
    (
        gain_one_gradient,
        router_one_gradient,
        query_gradient,
        key_gradient,
        value_gradient,
        output_gradient,
        gain_two_gradient,
        router_two_gradient,
    ) = (
        lax.psum_scatter(
            gain_one_term.astype(jnp.bfloat16), BOTH, scatter_dimension=0, tiled=True
        ).astype(jnp.float32),
        lax.psum_scatter(
            router_one_term.astype(jnp.bfloat16), BOTH, scatter_dimension=0, tiled=True
        ).astype(jnp.float32),
        lax.psum_scatter(
            query_term.astype(jnp.bfloat16), BOTH, scatter_dimension=1, tiled=True
        ).astype(jnp.float32),
        lax.psum_scatter(
            key_term.astype(jnp.bfloat16), BOTH, scatter_dimension=0, tiled=True
        ).astype(jnp.float32),
        lax.psum_scatter(
            value_term.astype(jnp.bfloat16), BOTH, scatter_dimension=0, tiled=True
        ).astype(jnp.float32),
        lax.psum_scatter(
            output_term.astype(jnp.bfloat16), BOTH, scatter_dimension=2, tiled=True
        ).astype(jnp.float32),
        lax.psum_scatter(
            gain_two_term.astype(jnp.bfloat16), BOTH, scatter_dimension=0, tiled=True
        ).astype(jnp.float32),
        lax.psum_scatter(
            router_two_term.astype(jnp.bfloat16), BOTH, scatter_dimension=0, tiled=True
        ).astype(jnp.float32),
    )
    factor = jnp.sqrt(jnp.minimum(1.0, CLIP / peak_all))
    columns = jnp.repeat(factor, head_dim)
    clipped_query = (query_weight.astype(jnp.float32) * columns).astype(jnp.bfloat16)
    clipped_key = (key_weight.astype(jnp.float32) * columns).astype(jnp.bfloat16)
    return (
        output,
        input_gradient,
        gain_one_gradient,
        router_one_gradient,
        query_gradient,
        key_gradient,
        value_gradient,
        output_gradient,
        gain_two_gradient,
        router_two_gradient,
        gate_gradient,
        up_gradient,
        down_gradient,
        clipped_query,
        clipped_key,
    )


def along(value, axis, step):
    count = lax.axis_size(axis)
    if step % count == 0:
        return value
    return lax.ppermute(value, axis, [(place, (place + step) % count) for place in range(count)])


def across(value, bits):
    count = lax.axis_size(TP)
    return lax.ppermute(value, TP, [(place, place ^ bits) for place in range(count)])


def f32(value):
    return value.astype(jnp.float32)


def bf16(value):
    return value.astype(jnp.bfloat16)


def dot(left, right, contract):
    return lax.dot_general(
        left, right, ((contract[:1], contract[1:]), ((), ())), preferred_element_type=jnp.float32
    )


def either(bit, zero, one):
    return jnp.where(bit == 0, zero, one)


def tp_bits():
    place = lax.axis_index(TP)
    return place % 2, place // 2


def in_columns(own, other, far, both):
    low, high = tp_bits()
    first, second = either(low, own, other), either(low, other, own)
    third, fourth = either(low, far, both), either(low, both, far)
    return jnp.concatenate(
        [
            either(high, first, third),
            either(high, second, fourth),
            either(high, third, first),
            either(high, fourth, second),
        ],
        axis=1,
    )


def from_ctx(blocks):
    return [along(block, CTX, step) for step, block in enumerate(blocks)]


def gather_pairs(near):
    far = [across(block, 2) for block in near]

    def stacked(items):
        steps, rows = len(items), items[0].shape[0]
        whole = jnp.zeros((steps * rows, items[0].shape[1]), items[0].dtype)
        for step, item in enumerate(items):
            row = ((lax.axis_index(CTX) - step) % steps) * rows
            whole = lax.dynamic_update_slice(whole, item, (row, 0))
        return whole

    return stacked(near), stacked(far)


def gather_columns(near):
    own, far = gather_pairs(near)
    return in_columns(own, across(own, 1), far, across(far, 1))


def gather_dense(own):
    whole = lax.all_gather(own, (TP, CTX), axis=0, tiled=True)
    tps = lax.axis_size(TP)
    whole = whole.reshape(tps, whole.shape[0] // tps, own.shape[1])
    return jnp.concatenate([whole[index] for index in range(tps)], axis=1)


def outward_kernel(left_ref, right_ref, out_ref):
    out_ref[0] = bf16(dot(left_ref[...], right_ref[...], (1, 1)))


def by_quarter(left, right):
    tps = lax.axis_size(TP)
    count, depth = left.shape
    size = right.shape[0] // tps
    return pl.pallas_call(
        outward_kernel,
        grid=(tps,),
        in_specs=[
            pl.BlockSpec((count, depth), lambda q: (0, 0)),
            pl.BlockSpec((size, depth), lambda q: (q, 0)),
        ],
        out_specs=pl.BlockSpec((1, count, size), lambda q: (q, 0, 0)),
        out_shape=jax.ShapeDtypeStruct((tps, count, size), jnp.bfloat16),
        compiler_params=pltpu.CompilerParams(vmem_limit_bytes=32 * 1024 * 1024),
        cost_estimate=pl.CostEstimate(
            flops=2 * count * depth * right.shape[0],
            bytes_accessed=2 * (tps * count * depth + right.size + count * right.shape[0]),
            transcendentals=0,
        ),
    )(left, right)


def scatter_dense(left, right):
    part = by_quarter(left, right)
    part = part.reshape(-1, part.shape[2])
    return f32(lax.psum_scatter(part, (TP, CTX), scatter_dimension=0, tiled=True))


def scatter_columns(part):
    steps = lax.axis_size(CTX)
    low, high = tp_bits()
    size = part.shape[1] // 4
    quarter = [part[:, index * size : (index + 1) * size] for index in range(4)]
    sent = jnp.concatenate(
        [either(low, quarter[1], quarter[0]), either(low, quarter[3], quarter[2])], axis=1
    )
    came = across(sent, 1)
    first = f32(either(low, quarter[0], quarter[1])) + f32(came[:, :size])
    second = f32(either(low, quarter[2], quarter[3])) + f32(came[:, size:])
    kept = bf16(either(high, first, second))
    sent = bf16(either(high, second, first))
    rows = part.shape[0] // steps
    result = [None] * steps
    for step in list(range(1, steps)) + [0]:
        row = ((lax.axis_index(CTX) - step) % steps) * rows
        own, other = [lax.dynamic_slice_in_dim(item, row, rows, axis=0) for item in (kept, sent)]
        done = bf16(f32(own) + f32(across(other, 2)))
        result[step] = along(done, CTX, -step)
    return result


def tp_sum(part):
    return part + across(part, 1) + across(part, 2) + across(part, 3)


def share_out(own):
    return in_columns(own, across(own, 1), across(own, 2), across(own, 3))


def tie(*values):
    return lax.optimization_barrier(values)


def after(value, *others):
    return lax.optimization_barrier((value, *others))[0]


def by_place(blocks):
    order = (lax.axis_index(CTX) - jnp.arange(len(blocks))) % len(blocks)
    return jnp.stack(blocks)[order]


def exchange(parts):
    return lax.all_to_all(parts, CTX, 0, 0)


def swap(value):
    return lax.ppermute(value, SHARD, [(0, 1), (1, 0)])


def joined(near, far):
    first = lax.axis_index(SHARD) == 0
    return jnp.concatenate([jnp.where(first, near, far), jnp.where(first, far, near)], axis=0)


def halves(value):
    half = value.shape[1] // 2
    side = lax.axis_index(SHARD)
    return (
        lax.dynamic_slice_in_dim(value, side * half, half, axis=1),
        lax.dynamic_slice_in_dim(value, (1 - side) * half, half, axis=1),
    )


def far_gradient(rows, change):
    return bf16(dot(halves(rows)[1], change, (0, 0)))


def near_gradient(rows, change, arrived):
    total = bf16(dot(halves(rows)[0], change, (0, 0)) + f32(arrived))
    steps = lax.axis_size(CTX)
    return total.reshape(steps, total.shape[0] // steps, total.shape[1])


def attend_kernel(q_ref, k_ref, v_ref, bias_ref, mixed_ref, norm_ref, peak_ref):
    scale = HEAD_DIM ** (-0.5)
    scores = dot(q_ref[...], k_ref[...], (1, 1)) * scale + f32(bias_ref[...])
    peak = jnp.max(scores, axis=-1, keepdims=True)
    weights = jnp.exp(scores - peak)
    total = jnp.sum(weights, axis=-1, keepdims=True)
    mixed_ref[...] = bf16(dot(bf16(weights / total), v_ref[...], (1, 0)))
    norm_ref[...] = jnp.broadcast_to(peak + jnp.log(total), norm_ref.shape)
    peak_ref[...] = jnp.broadcast_to(jnp.max(peak, axis=0, keepdims=True), peak_ref.shape)


def attend_back_kernel(
    q_ref, k_ref, v_ref, bias_ref, norm_ref, back_ref, dq_ref, dk_ref, dv_ref
):
    scale = HEAD_DIM ** (-0.5)

    @pl.when(pl.program_id(0) == 0)
    def _():
        dk_ref[...] = jnp.zeros_like(dk_ref)
        dv_ref[...] = jnp.zeros_like(dv_ref)

    scores = dot(q_ref[...], k_ref[...], (1, 1)) * scale + f32(bias_ref[...])
    chances = jnp.exp(scores - norm_ref[:, :1])
    dv_ref[...] += dot(bf16(chances), back_ref[...], (0, 0))
    share_back = dot(back_ref[...], v_ref[...], (1, 1))
    score_back = bf16(
        chances * (share_back - jnp.sum(chances * share_back, axis=-1, keepdims=True))
    )
    dq_ref[...] = dot(score_back, k_ref[...], (1, 0)) * scale
    dk_ref[...] += dot(score_back, q_ref[...], (0, 0)) * scale


ROWS = 640


def attend(queries, keys, values, bias):
    rows, size = queries.shape
    count = keys.shape[0]
    turns = count // ROWS
    row = pl.BlockSpec((ROWS, size), lambda i: (i, 0))
    whole = pl.BlockSpec((count, size), lambda i: (0, 0))
    return pl.pallas_call(
        attend_kernel,
        grid=(rows // ROWS,),
        in_specs=[row, whole, whole, pl.BlockSpec((ROWS, count), lambda i: (i % turns, 0))],
        out_specs=[row, row, pl.BlockSpec((8, size), lambda i: (i, 0))],
        out_shape=[
            jax.ShapeDtypeStruct((rows, size), jnp.bfloat16),
            jax.ShapeDtypeStruct((rows, size), jnp.float32),
            jax.ShapeDtypeStruct((rows // ROWS * 8, size), jnp.float32),
        ],
        compiler_params=pltpu.CompilerParams(vmem_limit_bytes=48 * 1024 * 1024),
        cost_estimate=pl.CostEstimate(
            flops=4 * rows * count * size,
            bytes_accessed=4 * rows * size * 2 + 2 * count * count * 2,
            transcendentals=rows * count,
        ),
    )(queries, keys, values, bias)


def attend_back(queries, keys, values, bias, norm, back):
    rows, size = queries.shape
    count = keys.shape[0]
    turns = count // ROWS
    row = pl.BlockSpec((ROWS, size), lambda i: (i, 0))
    whole = pl.BlockSpec((count, size), lambda i: (0, 0))
    return pl.pallas_call(
        attend_back_kernel,
        grid=(rows // ROWS,),
        in_specs=[
            row, whole, whole, pl.BlockSpec((ROWS, count), lambda i: (i % turns, 0)), row, row
        ],
        out_specs=[row, whole, whole],
        out_shape=[
            jax.ShapeDtypeStruct((rows, size), jnp.float32),
            jax.ShapeDtypeStruct((count, size), jnp.float32),
            jax.ShapeDtypeStruct((count, size), jnp.float32),
        ],
        compiler_params=pltpu.CompilerParams(vmem_limit_bytes=48 * 1024 * 1024),
        cost_estimate=pl.CostEstimate(
            flops=10 * rows * count * size,
            bytes_accessed=6 * rows * size * 2 + 2 * count * count * 2,
            transcendentals=rows * count,
        ),
    )(queries, keys, values, bias, norm, back)


def pair_gates(logits, routes):
    chosen = []
    for choice in range(TOP):
        chosen.append(
            sum(
                jnp.where(routes[choice] == expert, logits[expert], 0.0)
                for expert in range(logits.shape[0])
            )
        )
    top = jnp.maximum(chosen[0], chosen[1])
    powers = [jnp.exp(item - top) for item in chosen]
    return [power / (powers[0] + powers[1]) for power in powers]


def pair_gates_back(changes, gates, routes, experts):
    mean = gates[0] * changes[0] + gates[1] * changes[1]
    chosen = [gates[choice] * (changes[choice] - mean) for choice in range(TOP)]
    return jnp.stack(
        [
            sum(jnp.where(routes[choice] == expert, chosen[choice], 0.0) for choice in range(TOP))
            for expert in range(experts)
        ]
    )


def swap_halves(value):
    half = value.shape[-1] // 2
    return jnp.concatenate([value[..., half:], value[..., :half]], axis=-1)


def small_gradient(part, extra):
    steps = lax.axis_size(CTX)
    here, side = lax.axis_index(CTX), lax.axis_index(SHARD)
    whole = jnp.concatenate([share_out(part), extra], axis=0)
    half = whole.shape[1] // 2
    whole = either(side, whole[:, :half], whole[:, half:]) + swap(
        either(side, whole[:, half:], whole[:, :half])
    )
    pieces = whole.reshape(whole.shape[0], steps, half // steps).transpose(1, 0, 2)
    return sum(
        along(
            lax.dynamic_index_in_dim(pieces, (here + step) % steps, 0, keepdims=False), CTX, step
        )
        for step in range(steps)
    )


def on_device_fast(
    inputs,
    parents,
    attention_routes,
    expert_routes,
    attention_gain,
    attention_router,
    query_weight,
    key_weight,
    value_weight,
    output_weight,
    expert_gain,
    expert_router,
    gate_weight,
    up_weight,
    down_weight,
    cotangent,
):
    count, width = inputs.shape
    experts, depth_here, local_width = query_weight.shape
    hidden = gate_weight.shape[2]
    steps, shards, tps = lax.axis_size(CTX), lax.axis_size(SHARD), lax.axis_size(TP)
    here, side, place = lax.axis_index(CTX), lax.axis_index(SHARD), lax.axis_index(TP)
    heads = local_width // HEAD_DIM
    rows, quarter = count // tps, width // tps
    tokens = count * steps
    slots = -(-CAP // 64) * 64

    def own_columns(value):
        return lax.dynamic_slice_in_dim(value, place * quarter, quarter, axis=value.ndim - 1)

    own_inputs = own_columns(inputs)
    def gather_rows(value):
        value = lax.dynamic_slice_in_dim(value, place * rows, rows, axis=0)
        return lax.all_gather(value, (CTX, TP), axis=0, tiled=True)

    all_inputs = gather_rows(inputs)
    small = jnp.concatenate(
        [attention_gain[None], expert_gain[None], attention_router.T, expert_router.T], axis=0
    )
    routes = jnp.concatenate([attention_routes.T, expert_routes.T], axis=0)
    packed = jnp.zeros((small.shape[0] + 2 * TOP, max(count, depth_here)), jnp.bfloat16)
    packed = lax.dynamic_update_slice(packed, small, (0, 0))
    packed = lax.dynamic_update_slice(packed, bf16(routes), (small.shape[0], 0))
    packed_near = [along(packed, CTX, step) for step in range(steps)]
    packed_all = by_place(packed_near)
    routes_all = packed_all[:, small.shape[0] :, :count].transpose(1, 0, 2).astype(jnp.int32)
    head_routes = routes_all[:TOP].reshape(TOP, tokens)
    own_head_routes, own_expert_routes = routes[:TOP], routes[TOP:]
    small_near = packed_all[:, : small.shape[0], :depth_here].transpose(1, 0, 2)
    small_near = small_near.reshape(small.shape[0], steps * depth_here).T
    small_all = joined(small_near, swap(small_near)).T
    gain_first, gain_second = f32(small_all[0]), f32(small_all[1])
    router_first, router_second = small_all[2 : 2 + experts], small_all[2 + experts :]
    own_small = f32(own_columns(small_all))
    own_gain_first, own_gain_second = own_small[0], own_small[1]
    own_router_first, own_router_second = own_small[2 : 2 + experts], own_small[2 + experts :]

    def rows_of(value):
        return value.reshape(-1, value.shape[2])

    def project_parts(query, key, value):
        query = query.reshape(experts, depth_here, heads, HEAD_DIM).transpose(2, 1, 0, 3)
        key, value = [
            item.reshape(depth_here, heads, HEAD_DIM).transpose(1, 0, 2) for item in (key, value)
        ]
        query = query.reshape(heads, depth_here, experts * HEAD_DIM)
        return jnp.concatenate([query, key, value], axis=2)

    def output_parts(weight):
        weight = weight.reshape(experts, heads, HEAD_DIM, depth_here).transpose(1, 3, 0, 2)
        return weight.reshape(heads, depth_here, experts * HEAD_DIM)

    nears = [exchange(project_parts(query_weight, key_weight, value_weight))]
    weight, nears[0] = tie(output_weight, nears[0])
    fars = [swap(nears[0])]
    nears.append(exchange(output_parts(weight)))
    weight, nears[1] = tie(gate_weight, nears[1])
    nears.append(exchange(weight))
    project = joined(rows_of(nears[0]), rows_of(fars[0]))
    own_upstream = own_columns(cotangent)

    target = (here + jnp.arange(steps, dtype=jnp.int32)) % steps
    named = own_expert_routes[None] == target[:, None, None]
    member = named[:, 0] | named[:, 1]
    slot = jnp.cumsum(member.astype(jnp.int32), axis=1) - 1
    onehot = (slot[:, None, :] == jnp.arange(slots, dtype=jnp.int32)[None, :, None]) & member[
        :, None, :
    ]
    onehot_all = onehot.astype(jnp.bfloat16).reshape(steps * slots, count)

    def picked_slots(value):
        picked = bf16(dot(onehot_all, value, (1, 0)))
        return from_ctx([picked[step * slots : (step + 1) * slots] for step in range(steps)])

    def from_slots(value):
        return dot(onehot_all, jnp.concatenate(scatter_columns(value), axis=0), (0, 0))

    chosen = (routes_all[TOP] == here) | (routes_all[TOP + 1] == here)
    chosen_slot = jnp.cumsum(chosen.astype(jnp.int32), axis=1) - 1
    chosen_onehot = (
        chosen_slot[:, None, :] == jnp.arange(slots, dtype=jnp.int32)[None, :, None]
    ) & chosen[:, None, :]

    token = jnp.arange(tokens, dtype=jnp.int32)
    unit = token // SEG
    group_units = tokens // SEG
    group_first = side * group_units
    parents, all_inputs = tie(parents, all_inputs)
    chain = ancestors(parents, group_first + jnp.arange(group_units, dtype=jnp.int32))
    valid = chain >= 0
    depth = jnp.sum(valid[:, 1:].astype(jnp.int32), axis=1, dtype=jnp.int32)
    reached = jnp.any(
        (chain[:, :, None] - group_first == jnp.arange(group_units, dtype=jnp.int32))
        & valid[:, :, None],
        axis=1,
    )
    unit_onehot = (unit[:, None] == jnp.arange(group_units, dtype=jnp.int32)[None, :]).astype(
        jnp.bfloat16
    )
    row_reach = bf16(dot(unit_onehot, reached.astype(jnp.bfloat16), (1, 0)))
    reach = dot(row_reach, unit_onehot, (1, 1))
    allowed = (reach > 0.5) & (
        (unit[:, None] != unit[None, :]) | (token[None, :] <= token[:, None])
    )
    bias = jnp.where(allowed, 0.0, -1e30).astype(jnp.bfloat16)
    token_depth = jnp.sum(
        jnp.where(unit[:, None] == jnp.arange(group_units)[None, :], depth[None, :], 0), axis=1
    )
    cosine, sine = rope_tables(token_depth * SEG + token % SEG, HEAD_DIM // 2)
    cosine = jnp.concatenate([cosine, cosine], axis=1)
    sine = jnp.concatenate([-sine, sine], axis=1)

    normed = bf16(normalize(f32(all_inputs), gain_first))
    head_gates = pair_gates(dot(router_first, normed, (1, 1)), head_routes)
    raw = dot(normed, project, (1, 0))
    nears[1], raw = tie(nears[1], raw)
    fars.append(swap(nears[1]))
    outward = joined(rows_of(nears[1]), rows_of(fars[1]))
    chosen_heads = [
        [head_routes[choice][:, None] == expert for expert in range(experts)]
        for choice in range(TOP)
    ]

    def pick(value, choice):
        return sum(
            jnp.where(
                chosen_heads[choice][expert],
                value[:, expert * HEAD_DIM : (expert + 1) * HEAD_DIM],
                0.0,
            )
            for expert in range(experts)
        )

    def place_pair(pair):
        return jnp.concatenate(
            [
                sum(jnp.where(chosen_heads[choice][expert], pair[choice], 0.0) for choice in range(TOP))
                for expert in range(experts)
            ],
            axis=1,
        )

    def turn(value):
        return value * cosine + swap_halves(value) * sine

    def turn_back(value):
        return value * cosine - swap_halves(value) * sine

    inner = experts * HEAD_DIM
    queries = bf16(jnp.concatenate([turn(pick(raw, choice)) for choice in range(TOP)], axis=0))
    keys = bf16(turn(raw[:, inner : inner + HEAD_DIM]))
    values = bf16(raw[:, inner + HEAD_DIM :])
    mixed, norm, peaks = attend(queries, keys, values, bias)
    mixed_pair = [f32(mixed[:tokens]), f32(mixed[tokens:])]
    gated_mixed = bf16(
        place_pair([head_gates[choice][:, None] * mixed_pair[choice] for choice in range(TOP)])
    )
    weight, nears[2] = tie(up_weight, nears[2])
    fars.append(swap(nears[2]))
    nears.append(exchange(weight))
    attention, nears[3], fars[2] = tie(scatter_dense(gated_mixed, outward), nears[3], fars[2])
    fars.append(swap(nears[3]))
    down_parts = after(down_weight, nears[3]).transpose(0, 2, 1)
    half = depth_here // 2
    down_near = [exchange(down_parts[:, :half])]
    down_far = [swap(down_near[0])]
    hidden_state = f32(own_inputs) + attention
    statistics = tp_sum(
        jnp.concatenate(
            [
                jnp.sum(hidden_state * hidden_state, axis=1)[None],
                jnp.einsum(
                    "td,ed->et", hidden_state * own_gain_second, own_router_second, precision=HIGH
                ),
            ],
            axis=0,
        )
    )
    norm_two = lax.rsqrt(statistics[0] / width + EPS)
    expert_gates = pair_gates(statistics[1:] * norm_two, own_expert_routes)
    own_normed_two = bf16(hidden_state * norm_two[:, None] * own_gain_second)
    gate_of = jnp.where(named[:, 0], expert_gates[0], 0.0) + jnp.where(
        named[:, 1], expert_gates[1], 0.0
    )
    gate_sent = jnp.sum(jnp.where(onehot, gate_of[:, None, :], 0.0), axis=2)
    gate_slot = by_place(from_ctx([gate_sent[step : step + 1] for step in range(steps)]))
    gate_slot = gate_slot.reshape(steps * slots, 1)
    row_blocks = picked_slots(own_normed_two)
    down_near.append(exchange(after(down_parts, *row_blocks)[:, half:]))
    down_far.append(swap(down_near[1]))
    slot_rows, down_near[0] = tie(gather_columns(row_blocks), down_near[0])
    down_near[1], gate_slot = tie(down_near[1], gate_slot)
    all_cotangent = gather_rows(after(cotangent, down_near[0]))
    slot_upstream = bf16(
        jnp.einsum(
            "bst,btd->bsd",
            chosen_onehot.astype(jnp.bfloat16),
            all_cotangent.reshape(steps, count, width),
            preferred_element_type=jnp.float32,
        )
    ).reshape(steps * slots, width)

    def whole(index):
        return joined(rows_of(nears[index]), rows_of(fars[index]))

    gate, up = whole(2), whole(3)
    down = joined(
        rows_of(jnp.concatenate(down_near, axis=1)), rows_of(jnp.concatenate(down_far, axis=1))
    )
    gate_pre = dot(slot_rows, gate, (1, 0))
    up_pre = dot(slot_rows, up, (1, 0))
    act_raw = dot(slot_upstream, down, (1, 0))
    sigmoid = jax.nn.sigmoid(gate_pre)
    activated = gate_pre * sigmoid * up_pre
    gated_act = bf16(activated * gate_slot)
    gate_back_slot = jnp.sum(activated * act_raw, axis=1, keepdims=True)
    act_back = act_raw * gate_slot
    gate_back = bf16(act_back * up_pre * sigmoid * (1.0 + gate_pre * (1.0 - sigmoid)))
    up_back = bf16(act_back * gate_pre * sigmoid)
    pairs = [(slot_upstream, gated_act), (slot_rows, gate_back), (slot_rows, up_back)]
    far_terms = [far_gradient(*pair) for pair in pairs]
    arrived = [swap(term) for term in far_terms]
    rows_back = bf16(
        dot(after(gate_back, *far_terms), gate, (1, 1)) + dot(up_back, up, (1, 1))
    )
    fed = bf16(dot(gated_act, down, (1, 1)))
    gate_sums = tp_sum(after(gate_back_slot, rows_back).reshape(steps, slots))
    gate_sums = jnp.concatenate(
        [
            along(lax.dynamic_slice_in_dim(gate_sums, (here - step) % steps, 1), CTX, -step)
            for step in range(steps)
        ]
    )
    gate_changes = jnp.sum(jnp.where(onehot, gate_sums[:, :, None], 0.0), axis=1)
    normed_two_back, ready = tie(
        from_slots(rows_back), near_gradient(*pairs[0], arrived[0])
    )

    expert_gate_back = [
        sum(
            jnp.where(named[step, choice], gate_changes[step], 0.0) for step in range(steps)
        )
        for choice in range(TOP)
    ]
    expert_logit_back = pair_gates_back(
        expert_gate_back, expert_gates, own_expert_routes, experts
    )
    router_second_term = jnp.einsum(
        "et,td->ed", expert_logit_back, f32(own_normed_two), precision=HIGH
    )
    normed_two_back = normed_two_back + jnp.einsum(
        "et,ed->td", expert_logit_back, own_router_second, precision=HIGH
    )
    scaled = normed_two_back * own_gain_second
    mean = tp_sum(jnp.sum(scaled * hidden_state, axis=1)[None])[0] / width
    gain_second_term = jnp.sum(normed_two_back * hidden_state * norm_two[:, None], axis=0)
    hidden_back = (
        f32(own_upstream)
        + norm_two[:, None] * scaled
        - hidden_state * (norm_two**3 * mean)[:, None]
    )

    down_back = exchange(ready)
    all_back, gate_ready = tie(
        gather_dense(bf16(hidden_back)),
        near_gradient(slot_rows, after(gate_back, hidden_back), arrived[1]),
    )
    raw_back = dot(all_back, outward, (1, 0))
    pair_back = [pick(raw_back, choice) for choice in range(TOP)]
    head_change = jnp.stack(
        [jnp.sum(mixed_pair[choice] * pair_back[choice], axis=1) for choice in range(TOP)]
    )
    head_sums = tp_sum(head_change).reshape(TOP, steps, count).transpose(1, 0, 2)
    head_gate_back = sum(
        along(
            lax.dynamic_index_in_dim(head_sums, (here - step) % steps, 0, keepdims=False),
            CTX,
            -step,
        )
        for step in range(steps)
    )
    mixed_back = bf16(
        jnp.concatenate(
            [head_gates[choice][:, None] * pair_back[choice] for choice in range(TOP)], axis=0
        )
    )
    mixed_back, down_back, head_gate_back = tie(mixed_back, down_back, head_gate_back)
    gate_returned = [exchange(after(gate_ready, down_back)[:, :half])]
    query_change, key_change, value_change = attend_back(
        queries, keys, values, bias, norm, mixed_back
    )
    change = bf16(
        jnp.concatenate(
            [
                place_pair(
                    [turn_back(query_change[:tokens]), turn_back(query_change[tokens:])]
                ),
                turn_back(f32(bf16(key_change))),
                value_change,
            ],
            axis=1,
        )
    )
    change, arrived[2], gate_returned[0] = tie(change, arrived[2], gate_returned[0])
    feed = from_slots(after(fed, change))
    gate_returned.append(exchange(after(gate_ready, gate_returned[0])[:, half:]))
    up_ready = near_gradient(slot_rows, after(up_back, change), arrived[2])
    pairs += [(all_back, gated_mixed), (normed, change)]
    arrived += [swap(far_gradient(*pair)) for pair in pairs[3:]]
    up_returned = exchange(after(up_ready, gate_returned[1]))
    normed_back, feed, output_ready, project_ready, gate_returned[1], up_returned = tie(
        scatter_dense(change, project),
        feed,
        near_gradient(*pairs[3], arrived[3]),
        near_gradient(*pairs[4], arrived[4]),
        gate_returned[1],
        up_returned,
    )
    output = share_out(bf16(hidden_state + feed))
    output_all = exchange(output_ready)
    project_all = exchange(after(project_ready, output_all))
    down_gradient = f32(down_back.transpose(0, 2, 1))
    gate_gradient = f32(jnp.concatenate(gate_returned, axis=1))
    up_gradient = f32(up_returned)
    own_rows = f32(inputs)
    norm_one = lax.rsqrt(jnp.mean(own_rows * own_rows, axis=1) + EPS)
    own_values = f32(own_inputs)
    own_normed = bf16(own_values * norm_one[:, None] * own_gain_first)
    own_head_gates = [
        lax.dynamic_slice_in_dim(gate_item, here * count, count, axis=0)
        for gate_item in head_gates
    ]
    head_logit_back = pair_gates_back(
        [head_gate_back[choice] for choice in range(TOP)],
        own_head_gates,
        own_head_routes,
        experts,
    )
    router_first_term = jnp.einsum(
        "et,td->ed", head_logit_back, f32(own_normed), precision=HIGH
    )
    normed_back = normed_back + jnp.einsum(
        "et,ed->td", head_logit_back, own_router_first, precision=HIGH
    )
    scaled = normed_back * own_gain_first
    mean = tp_sum(jnp.sum(scaled * own_values, axis=1)[None])[0] / width
    gain_first_term = jnp.sum(normed_back * own_values * norm_one[:, None], axis=0)
    input_gradient = share_out(
        bf16(
            hidden_back
            + norm_one[:, None] * scaled
            - own_values * (norm_one**3 * mean)[:, None]
        )
    )
    small_sums = small_gradient(
        jnp.concatenate(
            [
                gain_first_term[None],
                gain_second_term[None],
                router_first_term,
                router_second_term,
            ],
            axis=0,
        ),
        jnp.where(
            jnp.arange(width)[None] % depth_here == side * steps + here, jnp.max(peaks), 0.0
        ),
    )

    query_gradient = (
        project_all[:, :, :inner]
        .reshape(heads, depth_here, experts, HEAD_DIM)
        .transpose(2, 1, 0, 3)
        .reshape(experts, depth_here, local_width)
    )
    key_gradient = (
        project_all[:, :, inner : inner + HEAD_DIM].transpose(1, 0, 2).reshape(depth_here, local_width)
    )
    value_gradient = (
        project_all[:, :, inner + HEAD_DIM :].transpose(1, 0, 2).reshape(depth_here, local_width)
    )
    query_gradient, key_gradient, value_gradient = [
        f32(after(item)) for item in (query_gradient, key_gradient, value_gradient)
    ]
    output_gradient = (
        output_all
        .reshape(heads, depth_here, experts, HEAD_DIM)
        .transpose(2, 0, 3, 1)
        .reshape(experts, local_width, depth_here)
    )
    output_gradient = f32(after(output_gradient))

    head_peaks = jnp.max(
        small_sums[-1, : shards * steps].reshape(shards, steps), axis=0
    )
    factor = jnp.repeat(jnp.sqrt(jnp.minimum(1.0, CLIP / head_peaks)), HEAD_DIM)
    clipped_query = bf16(f32(query_weight) * factor)
    clipped_key = bf16(f32(key_weight) * factor)
    return (
        output,
        input_gradient,
        small_sums[0],
        small_sums[2 : 2 + experts].T,
        query_gradient,
        key_gradient,
        value_gradient,
        output_gradient,
        small_sums[1],
        small_sums[2 + experts : 2 + 2 * experts].T,
        gate_gradient,
        up_gradient,
        down_gradient,
        clipped_query,
        clipped_key,
    )


def on_device(*arrays):
    experts, _, local_width = arrays[6].shape
    steps = lax.axis_size(CTX)
    tokens = arrays[0].shape[0] * steps
    fits = (
        experts == steps
        and local_width == steps * HEAD_DIM
        and lax.axis_size(TP) == 4
        and lax.axis_size(SHARD) == 2
        and tokens % ROWS == 0
    )
    return on_device_fast(*arrays) if fits else on_device_general(*arrays)


def solution(mesh):
    placed = (
        P(BOTH, None),
        P(),
        P(BOTH, None),
        P(BOTH, None),
        P(BOTH),
        P(BOTH, None),
        P(None, BOTH, TP),
        P(BOTH, TP),
        P(BOTH, TP),
        P(None, TP, BOTH),
        P(BOTH),
        P(BOTH, None),
        P(None, BOTH, TP),
        P(None, BOTH, TP),
        P(None, TP, BOTH),
        P(BOTH, None),
    )
    return jax.shard_map(
        on_device,
        mesh=mesh,
        in_specs=placed,
        out_specs=(
            P(BOTH, None),
            P(BOTH, None),
            P(BOTH),
            P(BOTH, None),
            P(None, BOTH, TP),
            P(BOTH, TP),
            P(BOTH, TP),
            P(None, TP, BOTH),
            P(BOTH),
            P(BOTH, None),
            P(None, BOTH, TP),
            P(None, BOTH, TP),
            P(None, TP, BOTH),
            P(None, BOTH, TP),
            P(BOTH, TP),
        ),
        check_vma=False,
    )
```
